32 devices in a mesh: dp: 8 (over z, y), tensor: 4 (over x, core).
Axes of the slice: x: 2, y: 2, z: 4, core: 2. Of those that a mesh axis runs over, the one named last changes fastest.
Arguments:
- tokens: bfloat16 [12608, 768], P(('dp', 'tensor')), may hold values from -6 to 6
- patch_mask: int32 [64, 197], P(('dp', 'tensor')), may hold values 0 or 1
- cotangent: bfloat16 [12608, 768], P(('dp', 'tensor')), may hold values from -6 to 6
- project_qkv: float32 [3, 768, 768], P(None, 'dp', 'tensor'), may hold values from -0.21875 to 0.21875
- first_qkv: float32 [3, 768, 768], P(None, 'dp', 'tensor'), may hold values from -320 to 320
- second_qkv: float32 [3, 768, 768], P(None, 'dp', 'tensor'), may hold values from 3152 to 12608
- project_out: float32 [768, 768], P('tensor', 'dp'), may hold values from -0.625 to 0.625
- first_out: float32 [768, 768], P('tensor', 'dp'), may hold values from -320 to 320
- second_out: float32 [768, 768], P('tensor', 'dp'), may hold values from 3152 to 12608
- expand_weight: float32 [768, 3072], P('dp', 'tensor'), may hold values from -0.21875 to 0.21875
- first_expand: float32 [768, 3072], P('dp', 'tensor'), may hold values from -320 to 320
- second_expand: float32 [768, 3072], P('dp', 'tensor'), may hold values from 3152 to 12608
- reduce_weight: float32 [3072, 768], P('tensor', 'dp'), may hold values from -0.109375 to 0.109375
- first_reduce: float32 [3072, 768], P('tensor', 'dp'), may hold values from -320 to 320
- second_reduce: float32 [3072, 768], P('tensor', 'dp'), may hold values from 3152 to 12608
- vectors: float32 [11, 768], P(None, 'dp'), may hold values from -2 to 2, as said below
- first_vectors: float32 [11, 768], P(None, 'dp'), may hold values from -320 to 320
- second_vectors: float32 [11, 768], P(None, 'dp'), may hold values from 3152 to 12608
- expand_bias: float32 [3072], P('dp'), may hold values from -3 to 3
- first_bias: float32 [3072], P('dp'), may hold values from -320 to 320
- second_bias: float32 [3072], P('dp'), may hold values from 3152 to 12608
Outputs:
- block_out: bfloat16 [12608, 768], P(('dp', 'tensor'))
- tokens_grad: bfloat16 [12608, 768], P(('dp', 'tensor'))
- new_qkv: float32 [3, 768, 768], P(None, 'dp', 'tensor')
- moment_qkv: float32 [3, 768, 768], P(None, 'dp', 'tensor')
- square_qkv: float32 [3, 768, 768], P(None, 'dp', 'tensor')
- new_out: float32 [768, 768], P('tensor', 'dp')
- moment_out: float32 [768, 768], P('tensor', 'dp')
- square_out: float32 [768, 768], P('tensor', 'dp')
- new_expand: float32 [768, 3072], P('dp', 'tensor')
- moment_expand: float32 [768, 3072], P('dp', 'tensor')
- square_expand: float32 [768, 3072], P('dp', 'tensor')
- new_reduce: float32 [3072, 768], P('tensor', 'dp')
- moment_reduce: float32 [3072, 768], P('tensor', 'dp')
- square_reduce: float32 [3072, 768], P('tensor', 'dp')
- new_vectors: float32 [11, 768], P(None, 'dp')
- moment_vectors: float32 [11, 768], P(None, 'dp')
- square_vectors: float32 [11, 768], P(None, 'dp')
- new_bias: float32 [3072], P('dp')
- moment_bias: float32 [3072], P('dp')
- square_bias: float32 [3072], P('dp')
The draws below stay inside these ranges and needn't reach their ends.
Inputs may be any that keep to these rules, and one draw needn't show every extreme that they name: `patch_mask`: 1 marks a patch replaced by the mask token; the class row (position 0 of each image) is never replaced, whatever its entry. `vectors`: rows 0, 2, 4 and 5 (gains and layer scales) are positive, the other rows are biases and the mask token.
All inputs are finite; a program needn't handle non-finite values. No bound on the sum of `patch_mask` on one device may be relied on, other than what follows from the above.
Results may differ from the reference program's by a relative error of at most 0.01.
The reference program's roundings to bfloat16 on the way count: a program that leaves them out, or rounds other values in their place, can miss the bound.
Values may be sent and summed in bfloat16 or wider, within the bound.
No kernel may reach another device: no remote copies, remote signals or barrier semaphores. Data moves between devices by JAX's collectives and lax.ppermute only.
A program may use at most 128 MiB of HBM per device.

```python
import math
import jax
import jax.numpy as jnp
from jax import lax

D = 768
HEADS = 12
HEAD_DIM = 64
FF = 3072
SEQ = 197
IMG_DEV = 8
STEP = 4
IMAGES = 64
TOKENS = 12608
N_DP = 8


def draw_vectors(key, part):
    key = jax.random.fold_in(key, 5)
    key_gain, key_shift = jax.random.split(key)
    row_index = jnp.arange(11)[:, None]
    gain_rows = (row_index == 0) | (row_index == 2) | (row_index == 4) | (row_index == 5)
    gains = jax.random.uniform(key_gain, (11, D), jnp.float32, 0.6, 1.4)
    shifts = jnp.clip(0.5 * jax.random.normal(key_shift, (11, D), jnp.float32), -2.0, 2.0)
    return jnp.where(gain_rows, gains, shifts)


def with_ends(result, rng, least, largest):
    longest = result.shape.index(max(result.shape))
    spots = []
    for shift in (0, 1):
        where = [jax.random.randint(jax.random.fold_in(rng, axis), (), 0, length) for axis, length in enumerate(result.shape)]
        where[longest] = (where[longest] + shift) % result.shape[longest]
        spots.append(tuple(where))
    return result.at[spots[0]].set(least).at[spots[1]].set(largest)


def shard_levels(key, extent, cuts, low, top_value):
    factor_of = 1.0
    for axis_at, shards_of in cuts:
        draws = jax.random.uniform(jax.random.fold_in(jax.random.fold_in(key, 6), axis_at), (shards_of,), jnp.float32, low / len(cuts), top_value / len(cuts))
        factor_of = factor_of * jnp.repeat(jnp.exp(draws), extent[axis_at] // shards_of).reshape((-1,) + (1,) * (len(extent) - 1 - axis_at))
    return factor_of


def scatter_about(rng, extent, scale, most, shards=(), held_as=jnp.bfloat16):
    entries = scale * jax.random.normal(rng, extent, jnp.float32)
    if shards:
        entries = entries * shard_levels(rng, extent, shards, -0.22, 0.18)
    return jnp.clip(entries, -most, most).astype(held_as)


def setup_inputs(seed: int = 0) -> dict:
    streams_of = jax.random.split(jax.random.key(seed), 22)
    tokens = scatter_about(streams_of[0], (TOKENS, D), 1.0, 6.0, ((0, 32),))
    patch_mask = with_ends((jax.random.randint(streams_of[1], (IMAGES, SEQ), 0, 5) < 3).astype(jnp.int32), jax.random.fold_in(streams_of[1], 1), 0, 1)
    cotangent = scatter_about(streams_of[2], (TOKENS, D), 1.0, 6.0, ((0, 32),))
    project_qkv = scatter_about(streams_of[3], (3, D, D), D ** -0.5, 0.21875, ((1, 8), (2, 4)), jnp.float32)
    first_qkv = scatter_about(streams_of[4], (3, D, D), (0.5 * TOKENS ** 0.5), 320.0, ((1, 8), (2, 4)), jnp.float32)
    second_qkv = jnp.clip(jnp.exp(math.log(12608.0) - 1.3862944 * jax.random.uniform(streams_of[5], (3, D, D), jnp.float32) ** shard_levels(streams_of[5], (3, D, D), ((1, 8), (2, 4)), -0.2, 0.2)), 3152.0, 12608.0)
    project_out = scatter_about(streams_of[6], (D, D), (D // 8) ** -0.5, 0.625, ((0, 4), (1, 8)), jnp.float32)
    first_out = scatter_about(streams_of[7], (D, D), (0.5 * TOKENS ** 0.5), 320.0, ((0, 4), (1, 8)), jnp.float32)
    second_out = jnp.clip(jnp.exp(math.log(12608.0) - 1.3862944 * jax.random.uniform(streams_of[8], (D, D), jnp.float32) ** shard_levels(streams_of[8], (D, D), ((0, 4), (1, 8)), -0.2, 0.2)), 3152.0, 12608.0)
    expand_weight = scatter_about(streams_of[9], (D, FF), D ** -0.5, 0.21875, ((0, 8), (1, 4)), jnp.float32)
    first_expand = scatter_about(streams_of[10], (D, FF), (0.5 * TOKENS ** 0.5), 320.0, ((0, 8), (1, 4)), jnp.float32)
    second_expand = jnp.clip(jnp.exp(math.log(12608.0) - 1.3862944 * jax.random.uniform(streams_of[11], (D, FF), jnp.float32) ** shard_levels(streams_of[11], (D, FF), ((0, 8), (1, 4)), -0.2, 0.2)), 3152.0, 12608.0)
    reduce_weight = scatter_about(streams_of[12], (FF, D), FF ** -0.5, 0.109375, ((0, 4), (1, 8)), jnp.float32)
    first_reduce = scatter_about(streams_of[13], (FF, D), (0.5 * TOKENS ** 0.5), 320.0, ((0, 4), (1, 8)), jnp.float32)
    second_reduce = jnp.clip(jnp.exp(math.log(12608.0) - 1.3862944 * jax.random.uniform(streams_of[14], (FF, D), jnp.float32) ** shard_levels(streams_of[14], (FF, D), ((0, 4), (1, 8)), -0.2, 0.2)), 3152.0, 12608.0)
    vectors = draw_vectors(jax.random.fold_in(streams_of[21], 71), 0)
    first_vectors = scatter_about(streams_of[16], (11, D), (0.5 * TOKENS ** 0.5), 320.0, ((1, 8),), jnp.float32)
    second_vectors = jnp.clip(jnp.exp(math.log(12608.0) - 1.3862944 * jax.random.uniform(streams_of[17], (11, D), jnp.float32) ** shard_levels(streams_of[17], (11, D), ((1, 8),), -0.2, 0.2)), 3152.0, 12608.0)
    expand_bias = scatter_about(streams_of[18], (FF,), 0.5, 3.0, ((0, 8),), jnp.float32)
    first_bias = scatter_about(streams_of[19], (FF,), (0.5 * TOKENS ** 0.5), 320.0, ((0, 8),), jnp.float32)
    second_bias = jnp.clip(jnp.exp(math.log(12608.0) - 1.3862944 * jax.random.uniform(streams_of[20], (FF,), jnp.float32) ** shard_levels(streams_of[20], (FF,), ((0, 8),), -0.2, 0.2)), 3152.0, 12608.0)
    return {"tokens": tokens, "patch_mask": patch_mask, "cotangent": cotangent, "project_qkv": project_qkv, "first_qkv": first_qkv, "second_qkv": second_qkv, "project_out": project_out, "first_out": first_out, "second_out": second_out, "expand_weight": expand_weight, "first_expand": first_expand, "second_expand": second_expand, "reduce_weight": reduce_weight, "first_reduce": first_reduce, "second_reduce": second_reduce, "vectors": vectors, "first_vectors": first_vectors, "second_vectors": second_vectors, "expand_bias": expand_bias, "first_bias": first_bias, "second_bias": second_bias}


@jax.custom_vjp
def low(v):
    return lax.optimization_barrier(v.astype(jnp.bfloat16)).astype(jnp.float32)

@jax.custom_vjp
def low_back(v):
    return v

def low_keep(v):
    return (low(v), None)

def low_pass(kept, grad):
    return (grad,)

def back_keep(v):
    return (v, None)

def back_low(kept, grad):
    return (low(grad),)
low.defvjp(low_keep, low_pass)
low_back.defvjp(back_keep, back_low)
BETA_ONE = 0.5
BETA_TWO = 0.5
EPSILON = 1e-08
DECAY = 0.05
RATE_MATRIX = 0.02
RATE_VECTOR = 0.2
NORM_EPS = 1e-06
HIGH = lax.Precision.HIGHEST

def layer_norm(values, gain_row, shift_row):
    row_mean = lax.optimization_barrier(jnp.mean(values, axis=-1, keepdims=True))
    centred = values - row_mean
    row_var = lax.optimization_barrier(jnp.mean(centred * centred, axis=-1, keepdims=True))
    return centred * lax.rsqrt(row_var + NORM_EPS) * gain_row + shift_row

def matmul(left, right):
    return jnp.dot(left, right, precision=HIGH)

def attend(image_block):
    queries, key_rows, value_rows = image_block
    scores = low_back(jnp.einsum('bqhd,bkhd->bhqk', queries, key_rows, precision=HIGH) * HEAD_DIM ** (-0.5))
    soft_weights = low(jax.nn.softmax(scores, axis=-1))
    return jnp.einsum('bhqk,bkhd->bqhd', soft_weights, value_rows, precision=HIGH)

def forward(tokens32, replaced, project_qkv, project_out, expand_weight, reduce_weight, vectors, expand_bias):
    project_qkv = low(project_qkv)
    project_out = low(project_out)
    expand_weight = low(expand_weight)
    reduce_weight = low(reduce_weight)
    vectors = low(vectors)
    expand_bias = low(expand_bias)
    start_rows = tokens32 * (1.0 - replaced) + vectors[6] * replaced
    normed = low(layer_norm(start_rows, vectors[0], vectors[1]))
    queries = low_back(low(matmul(normed, project_qkv[0]) + vectors[9]))
    key_rows = low_back(low(matmul(normed, project_qkv[1])))
    value_rows = low_back(low(matmul(normed, project_qkv[2]) + vectors[10]))
    head_shape = (N_DP, IMG_DEV, SEQ, HEADS, HEAD_DIM)
    attended = lax.map(jax.checkpoint(attend), (queries.reshape(head_shape), key_rows.reshape(head_shape), value_rows.reshape(head_shape)))
    attended = low_back(low(attended.reshape(TOKENS, D)))
    attn_out = low_back(matmul(attended, project_out))
    middle = start_rows + vectors[4] * (attn_out + vectors[7])
    normed_two = low(layer_norm(middle, vectors[2], vectors[3]))
    hidden = low_back(matmul(normed_two, expand_weight) + expand_bias)
    active = low(jax.nn.gelu(hidden, approximate=False))
    branch = low_back(matmul(active, reduce_weight))
    return middle + vectors[5] * (branch + vectors[8])

def adam_update(weight, gradient, first_moment, second, step_rate, decay_rate):
    moment = BETA_ONE * first_moment + (1.0 - BETA_ONE) * gradient
    square = BETA_TWO * second + (1.0 - BETA_TWO) * gradient * gradient
    first_hat = moment / (1.0 - BETA_ONE ** STEP)
    second_hat = square / (1.0 - BETA_TWO ** STEP)
    updated = weight - step_rate * (first_hat / (jnp.sqrt(second_hat) + EPSILON) + decay_rate * weight)
    return (updated, moment, square)

def reference(tokens, patch_mask, cotangent, project_qkv, first_qkv, second_qkv, project_out, first_out, second_out, expand_weight, first_expand, second_expand, reduce_weight, first_reduce, second_reduce, vectors, first_vectors, second_vectors, expand_bias, first_bias, second_bias):
    positions = lax.broadcasted_iota(jnp.int32, patch_mask.shape, 1)
    replaced = jnp.where((patch_mask == 1) & (positions > 0), 1.0, 0.0).astype(jnp.float32).reshape(TOKENS, 1)

    def wrapped(tokens32, qkv_in, out_in, expand_in, reduce_in, vector_in, bias_in):
        return forward(tokens32, replaced, qkv_in, out_in, expand_in, reduce_in, vector_in, bias_in)
    block_f32, pullback = jax.vjp(wrapped, tokens.astype(jnp.float32), project_qkv, project_out, expand_weight, reduce_weight, vectors, expand_bias)
    gradients = pullback(cotangent.astype(jnp.float32))
    new_qkv, moment_qkv, square_qkv = adam_update(project_qkv, gradients[1], first_qkv, second_qkv, RATE_MATRIX, DECAY)
    new_out, moment_out, square_out = adam_update(project_out, gradients[2], first_out, second_out, RATE_MATRIX, DECAY)
    new_expand, moment_expand, square_expand = adam_update(expand_weight, gradients[3], first_expand, second_expand, RATE_MATRIX, DECAY)
    new_reduce, moment_reduce, square_reduce = adam_update(reduce_weight, gradients[4], first_reduce, second_reduce, RATE_MATRIX, DECAY)
    new_vectors, moment_vectors, square_vectors = adam_update(vectors, gradients[5], first_vectors, second_vectors, RATE_VECTOR, 0.0)
    new_bias, moment_bias, square_bias = adam_update(expand_bias, gradients[6], first_bias, second_bias, RATE_VECTOR, 0.0)
    return (block_f32.astype(jnp.bfloat16), gradients[0].astype(jnp.bfloat16), new_qkv, moment_qkv, square_qkv, new_out, moment_out, square_out, new_expand, moment_expand, square_expand, new_reduce, moment_reduce, square_reduce, new_vectors, moment_vectors, square_vectors, new_bias, moment_bias, square_bias)
```

```python
import functools

import jax
import jax.numpy as jnp
import numpy as np
from jax import lax
from jax.experimental import pallas as pl
from jax.experimental.pallas import tpu as pltpu
from jax.sharding import PartitionSpec as P

D = 768
HEAD_DIM = 64
FF = 3072
SEQ = 197
STEP = 4
BETA_ONE = 0.5
BETA_TWO = 0.5
EPSILON = 1e-08
DECAY = 0.05
RATE_MATRIX = 0.02
RATE_VECTOR = 0.2
NORM_EPS = 1e-06

AXES = ("dp", "tensor")
PAD = 208
GROUPS = 4
GROUP_COLS = D // GROUPS
HEADS_IN_GROUP = GROUP_COLS // HEAD_DIM
BLOCKS = 8
BLOCK_ROWS = D // BLOCKS
EXTRA = 8
SCALE = HEAD_DIM**-0.5
F32 = jnp.float32
BF16 = jnp.bfloat16

BIT = {"c": 1, "x": 2, "y": 4, "1": 8, "2": 16}
GATHER = (("12yx", "12xy"), ("x12y", "y12x"), ("2xy1", "2yx1"))
SCATTER = (("12yx", "12xy"), ("x12y", "y12x"), ("2xy1", "2yx1"))


def offset_of(order, place):
    found = 0
    for level in range(4):
        if place >> level & 1:
            found ^= BIT[order[level]]
    return found


def pairs_of(orders, level):
    return [(dev, dev ^ BIT[orders[dev & 1][level]]) for dev in range(32)]


CORE_PAIRS = [(dev, dev ^ 1) for dev in range(32)]


def build_table(gather, scatter):
    table = np.zeros((32, 80), np.int32)
    for dev in range(32):
        core = dev & 1
        for place in range(16):
            table[dev, place] = dev ^ offset_of(gather[core], place)
            table[dev, 16 + place] = dev ^ 1 ^ offset_of(gather[1 - core], place)
            mine = dev ^ offset_of(gather[core], place)
            if mine & 3 == dev & 3:
                table[dev, 32 + (mine >> 2)] = place
            table[dev, 40 + (dev ^ offset_of(scatter[core], place))] = place
            table[dev, 40 + (dev ^ 1 ^ offset_of(scatter[1 - core], place))] = place
        table[dev, 72] = core
    return table


def plain_table():
    table = np.zeros((80,), np.int32)
    for place in range(32):
        table[place] = (place % 8) * 4 + place // 8
    for block in range(8):
        table[32 + block] = block
        for group in range(4):
            table[40 + block * 4 + group] = block * 2 + group // 2
    return table


def dot(left, right):
    return jnp.dot(left, right, preferred_element_type=F32)


def dot_rt(left, right):
    return lax.dot_general(left, right, (((1,), (1,)), ((), ())), preferred_element_type=F32)


def dot_lt(left, right):
    return lax.dot_general(left, right, (((0,), (0,)), ((), ())), preferred_element_type=F32)


def norm_stats(values):
    mean = jnp.mean(values, axis=-1, keepdims=True)
    centred = values - mean
    var = jnp.mean(centred * centred, axis=-1, keepdims=True)
    rstd = lax.rsqrt(var + NORM_EPS)
    return centred * rstd, rstd


def norm_back(grad, gain, unit, rstd):
    grad_unit = grad * gain
    first = jnp.mean(grad_unit, axis=-1, keepdims=True)
    second = jnp.mean(grad_unit * unit, axis=-1, keepdims=True)
    return rstd * (grad_unit - first - unit * second)


def col_sum(values):
    return jnp.sum(values, axis=0, keepdims=True)


def assemble(tab, parts, whole):
    for index, part in enumerate(parts):
        for place in range(8):
            owner = tab[index * 8 + place]
            row = pl.multiple_of((owner >> 2) * BLOCK_ROWS, BLOCK_ROWS)
            whole[owner & 3, pl.ds(row, BLOCK_ROWS), :] = part[place, 0:BLOCK_ROWS, :]


def put_blocks(tab, group, grad, out):
    for block in range(BLOCKS):
        place = tab[40 + block * 4 + group]
        rows = slice(block * BLOCK_ROWS, (block + 1) * BLOCK_ROWS)
        out[place] = grad[rows].astype(BF16)


def mask_rows(tok, rep, vec):
    replaced = rep[...]
    return tok[...].astype(F32) * (1.0 - replaced) + vec[6:7, :] * replaced


def pack_kernel(project_qkv, project_out, vectors, expand_bias, out):
    blank = jnp.zeros((EXTRA, D), F32)
    columns = [project_qkv[0], project_qkv[1], project_qkv[2], project_out[...].T]
    block = jnp.concatenate(columns, axis=1)
    fill = jnp.zeros((EXTRA, 128 - BLOCK_ROWS), F32)
    low = jnp.concatenate([vectors[0:8, :], fill], axis=1)
    high = jnp.concatenate([vectors[8:11, :], jnp.zeros((5, BLOCK_ROWS), F32)], axis=0)
    high = jnp.concatenate([high, fill], axis=1)
    last = jnp.concatenate([expand_bias[...], jnp.zeros((EXTRA - 1, 384), F32)], axis=0)
    extra = jnp.concatenate([low, high, last, blank[:, 640:768]], axis=1)
    out[...] = jnp.concatenate([block, extra], axis=0).astype(BF16)


def attend_kernel(
    imgs, tab, tok, rep, extra, b0, b1, b2, b3,
    vec, bias, w1, normed, qkv, soft, att, attn, mid, normed_two, qb, vb,
):
    low = jnp.zeros((8, D), F32)
    high = jnp.zeros((8, D), F32)
    fill = jnp.zeros((8, D - 128), F32)
    for block in range(BLOCKS):
        piece = extra[tab[32 + block]]
        low += pltpu.roll(jnp.concatenate([piece[:, 0:128], fill], 1), block * BLOCK_ROWS, 1)
        high += pltpu.roll(jnp.concatenate([piece[:, 128:256], fill], 1), block * BLOCK_ROWS, 1)
        half = (block % 2) * 384
        bias[block // 2, 0:1, half : half + 384] = piece[0:1, 256:640]
    vec[0:8, :] = low
    vec[8:16, :] = high
    for group in range(GROUPS):
        cols = slice(group * GROUP_COLS, (group + 1) * GROUP_COLS)
        qb[group, 0:1, :] = vec[9:10, cols]
        vb[group, 0:1, :] = vec[10:11, cols]
    assemble(tab, (b0, b1, b2, b3), w1)
    start = mask_rows(tok, rep, vec)
    unit, _ = norm_stats(start)
    normed[...] = (unit * vec[0:1, :] + vec[1:2, :]).astype(BF16)
    attn[...] = jnp.zeros_like(attn)
    keep = lax.broadcasted_iota(jnp.int32, (PAD, PAD), 1) < SEQ

    def step(group, carry):
        result = dot(normed[...], w1[group, :, 0:576])
        qkv[group, :, 0:192] = (result[:, 0:192] + qb[group, 0:1, :]).astype(BF16)
        qkv[group, :, 192:384] = result[:, 192:384].astype(BF16)
        qkv[group, :, 384:576] = (result[:, 384:576] + vb[group, 0:1, :]).astype(BF16)
        for head in range(HEADS_IN_GROUP):
            c0 = head * HEAD_DIM
            for img in range(imgs):
                rows = slice(img * PAD, (img + 1) * PAD)
                q = qkv[group, rows, c0 : c0 + 64]
                k = qkv[group, rows, 192 + c0 : 256 + c0]
                v = qkv[group, rows, 384 + c0 : 448 + c0]
                scores = jnp.where(keep, dot_rt(q, k) * SCALE, -1e30)
                top = jnp.max(scores, axis=-1, keepdims=True)
                raised = jnp.exp(scores - top)
                weights = raised / jnp.sum(raised, axis=-1, keepdims=True)
                soft[group * (HEADS_IN_GROUP * imgs) + head * imgs + img] = weights
                att[group, rows, c0 : c0 + 64] = dot(weights.astype(BF16), v).astype(BF16)
        attn[...] += dot_rt(att[group], w1[group, :, 576:768])
        return carry

    lax.fori_loop(0, GROUPS, step, 0)
    middle = start + vec[4:5, :] * (attn[...] + vec[7:8, :])
    mid[...] = middle
    unit_two, _ = norm_stats(middle)
    normed_two[...] = (unit_two * vec[2:3, :] + vec[3:4, :]).astype(BF16)


def expand_kernel(
    tab, normed_two, cot, vec, bias, b0, b1, b2, b3,
    w2, active, slope, grad_branch, own, sib,
):
    assemble(tab, (b0, b1, b2, b3), w2)
    grad_branch[...] = (cot[...].astype(F32) * vec[5:6, :]).astype(BF16)
    for part, out in ((1, sib), (0, own)):

        def step(along_x, carry, part=part, out=out):
            group = along_x * 2 + (tab[72] ^ part)
            hidden = dot(normed_two[...], w2[group]) + bias[group, 0:1, :]
            cdf = 0.5 * (1.0 + lax.erf(hidden * 0.7071067811865476))
            pdf = 0.3989422804014327 * jnp.exp(-0.5 * hidden * hidden)
            act = (hidden * cdf).astype(BF16)
            active[group] = act
            slope[group] = cdf + hidden * pdf
            put_blocks(tab, group, dot_lt(grad_branch[...], act), out)
            return carry

        lax.fori_loop(0, 2, step, 0)


def hidden_kernel(
    tab, normed_two, grad_branch, slope, b0, b1, b2, b3,
    w3, grad_hidden, bias_grad, own, sib,
):
    assemble(tab, (b0, b1, b2, b3), w3)
    for part, out in ((1, sib), (0, own)):

        def step(along_x, carry, part=part, out=out):
            group = along_x * 2 + (tab[72] ^ part)
            grad = (dot(grad_branch[...], w3[group]) * slope[group]).astype(BF16)
            grad_hidden[group] = grad
            bias_grad[group, 0:1, :] = col_sum(grad.astype(F32))
            put_blocks(tab, group, dot_lt(normed_two[...], grad), out)
            return carry

        lax.fori_loop(0, 2, step, 0)


def middle_kernel(
    active, grad_hidden, w2, w3, mid, attn, cot, vec,
    block_out, grad_mid, grad_attn, sums, branch, grad_two,
):
    branch[...] = jnp.zeros_like(branch)
    sums[...] = jnp.zeros_like(sums)
    grad_two[...] = jnp.zeros_like(grad_two)

    def step(group, carry):
        branch[...] += dot_rt(active[group], w3[group])
        grad_two[...] += dot_rt(grad_hidden[group], w2[group])
        return carry

    lax.fori_loop(0, GROUPS, step, 0)
    middle = mid[...]
    total = branch[...] + vec[8:9, :]
    block_out[...] = (middle + vec[5:6, :] * total).astype(BF16)
    grad_out = cot[...].astype(F32)
    sums[5:6, :] = col_sum(grad_out * total)
    sums[8:9, :] = col_sum(grad_out * vec[5:6, :])
    unit, rstd = norm_stats(middle)
    grad = grad_two[...]
    sums[2:3, :] = col_sum(grad * unit)
    sums[3:4, :] = col_sum(grad)
    grad_middle = grad_out + norm_back(grad, vec[2:3, :], unit, rstd)
    grad_mid[...] = grad_middle
    sums[4:5, :] = col_sum(grad_middle * (attn[...] + vec[7:8, :]))
    scaled = grad_middle * vec[4:5, :]
    sums[7:8, :] = col_sum(scaled)
    grad_attn[...] = scaled.astype(BF16)


def back_kernel(
    imgs, tab, tok, rep, vec, w1, normed, qkv, soft, att, grad_attn, grad_mid, sums_in, bias_grad,
    tok_grad, own, sib, dw, grad_one, gqkv, qb, vb, packed, sums,
):
    grad_one[...] = jnp.zeros_like(grad_one)

    def step(group, carry):
        grad_att = dot(grad_attn[...], w1[group, :, 576:768]).astype(BF16)
        for head in range(HEADS_IN_GROUP):
            c0 = head * HEAD_DIM
            for img in range(imgs):
                rows = slice(img * PAD, (img + 1) * PAD)
                q = qkv[group, rows, c0 : c0 + 64]
                k = qkv[group, rows, 192 + c0 : 256 + c0]
                v = qkv[group, rows, 384 + c0 : 448 + c0]
                weights = soft[group * (HEADS_IN_GROUP * imgs) + head * imgs + img]
                grad = grad_att[rows, c0 : c0 + 64]
                grad_soft = dot_rt(grad, v)
                grad_v = dot_lt(weights.astype(BF16), grad)
                inner = jnp.sum(weights * grad_soft, axis=-1, keepdims=True)
                grad_scores = (weights * (grad_soft - inner)).astype(BF16)
                grad_q = dot(grad_scores, k) * SCALE
                grad_k = dot_lt(grad_scores, q) * SCALE
                gqkv[rows, c0 : c0 + 64] = grad_q.astype(BF16)
                gqkv[rows, 192 + c0 : 256 + c0] = grad_k.astype(BF16)
                gqkv[rows, 384 + c0 : 448 + c0] = grad_v.astype(BF16)
        all_grads = gqkv[...]
        qb[group, 0:1, :] = col_sum(all_grads[:, 0:192].astype(F32))
        vb[group, 0:1, :] = col_sum(all_grads[:, 384:576].astype(F32))
        dw[group, :, 0:576] = dot_lt(normed[...], all_grads)
        dw[group, :, 576:768] = dot_lt(grad_attn[...], att[group])
        grad_one[...] += dot_rt(all_grads, w1[group, :, 0:576])
        return carry

    lax.fori_loop(0, GROUPS, step, 0)
    replaced = rep[...]
    unit, rstd = norm_stats(mask_rows(tok, rep, vec))
    grad = grad_one[...]
    sums[...] = sums_in[...]
    sums[0:1, :] = col_sum(grad * unit)
    sums[1:2, :] = col_sum(grad)
    grad_start = grad_mid[...] + norm_back(grad, vec[0:1, :], unit, rstd)
    tok_grad[...] = (grad_start * (1.0 - replaced)).astype(BF16)
    sums[6:7, :] = col_sum(grad_start * replaced)
    for group in range(GROUPS):
        cols = slice(group * GROUP_COLS, (group + 1) * GROUP_COLS)
        sums[9:10, cols] = qb[group, 0:1, :]
        sums[10:11, cols] = vb[group, 0:1, :]
    low = sums[0:8, :]
    high = sums[8:16, :]
    for block in range(BLOCKS):
        shift = (D - block * BLOCK_ROWS) % D
        packed[block] = jnp.zeros((EXTRA, D), F32)
        packed[block, :, 0:BLOCK_ROWS] = pltpu.roll(low, shift, 1)[:, 0:BLOCK_ROWS]
        packed[block, :, 128 : 128 + BLOCK_ROWS] = pltpu.roll(high, shift, 1)[:, 0:BLOCK_ROWS]
        half = (block % 2) * 384
        packed[block, 0:1, 256:640] = bias_grad[block // 2, 0:1, half : half + 384]
    for part, out in ((1, sib), (0, own)):
        for along_x in range(2):
            group = along_x * 2 + (tab[72] ^ part)
            for block in range(BLOCKS):
                place = tab[40 + block * 4 + group]
                rows = slice(block * BLOCK_ROWS, (block + 1) * BLOCK_ROWS)
                both = jnp.concatenate([dw[group, rows, :], packed[block]], axis=0)
                out[place] = both.astype(BF16)


VMEM = pl.BlockSpec(memory_space=pltpu.VMEM)
SMEM = pl.BlockSpec(memory_space=pltpu.SMEM)


def shape(dims, dtype=BF16):
    return jax.ShapeDtypeStruct(dims, dtype)


def call(kernel, args, outs, scratch=(), flops=0, moved=0, megabytes=48, table=True):
    return pl.pallas_call(
        kernel,
        out_shape=outs,
        in_specs=[SMEM] * table + [VMEM] * (len(args) - table),
        out_specs=[VMEM] * len(outs),
        scratch_shapes=list(scratch),
        cost_estimate=pl.CostEstimate(flops=flops, bytes_accessed=moved, transcendentals=0),
        compiler_params=pltpu.CompilerParams(vmem_limit_bytes=megabytes << 20),
    )(*args)


def adam_update(weight, gradient, first_moment, second, step_rate, decay_rate):
    moment = BETA_ONE * first_moment + (1.0 - BETA_ONE) * gradient
    square = BETA_TWO * second + (1.0 - BETA_TWO) * gradient * gradient
    first_hat = moment / (1.0 - BETA_ONE**STEP)
    second_hat = square / (1.0 - BETA_TWO**STEP)
    updated = weight - step_rate * (
        first_hat / (jnp.sqrt(second_hat) + EPSILON) + decay_rate * weight
    )
    return (updated, moment, square)


def gather_stream(block, orders):
    held = block[None]
    for level in range(4):
        taken = lax.ppermute(held, AXES, pairs_of(orders, level))
        if level < 3:
            held = jnp.concatenate([held, taken], axis=0)
    return (
        held,
        taken,
        lax.ppermute(held, AXES, CORE_PAIRS),
        lax.ppermute(taken, AXES, CORE_PAIRS),
    )


def scatter_stream(own, sib, orders, even):
    terms = [own, lax.ppermute(sib, AXES, CORE_PAIRS)]

    def total(low, high, last):
        found = terms[0][low:high].astype(F32)
        for index, term in enumerate(terms[1:]):
            found = found + term[low:high].astype(F32)
            if even and not (last and index == len(terms) - 2):
                found = lax.reduce_precision(found, 8, 7)
        return found

    for level in (3, 2, 1, 0):
        size = 1 << level
        sent = total(size, 2 * size, False).astype(BF16)
        terms.append(lax.ppermute(sent, AXES, pairs_of(orders, level)))
    return total(0, 1, True)[0]


def gather_plain(block):
    whole = lax.all_gather(block, AXES, axis=0, tiled=False)
    whole = whole.reshape(-1, GROUPS, *block.shape).transpose(1, 0, 2, 3)
    whole = whole.reshape(GROUPS, BLOCKS, BLOCK_ROWS, D)
    return tuple(whole[group] for group in range(GROUPS))


def scatter_plain(own, sib, n_dp):
    parts = jnp.stack([own, sib]).reshape(2, BLOCKS, 2, BLOCK_ROWS, D)
    whole = parts.transpose(1, 3, 2, 0, 4).reshape(D, GROUPS, D).astype(F32)
    whole = whole.reshape(n_dp, D // n_dp, GROUPS, D).transpose(0, 2, 1, 3)
    whole = whole.reshape(n_dp * GROUPS, D // n_dp, D)
    return lax.psum_scatter(whole, AXES, scatter_dimension=0, tiled=True)[0]


def on_device(
    n_dp,
    tokens,
    patch_mask,
    cotangent,
    project_qkv,
    first_qkv,
    second_qkv,
    project_out,
    first_out,
    second_out,
    expand_weight,
    first_expand,
    second_expand,
    reduce_weight,
    first_reduce,
    second_reduce,
    vectors,
    first_vectors,
    second_vectors,
    expand_bias,
    first_bias,
    second_bias,
):
    direct = n_dp == BLOCKS
    imgs = patch_mask.shape[0]
    rows = imgs * PAD
    wide = vectors.shape[1]
    piece_two = expand_weight.astype(BF16)
    piece_three = reduce_weight.astype(BF16).T
    if direct:
        flat = lax.axis_index("dp") * GROUPS + lax.axis_index("tensor")
        tables = [
            lax.dynamic_index_in_dim(jnp.asarray(build_table(g, s)), flat, 0, keepdims=False)
            for g, s in zip(GATHER, (SCATTER[0], SCATTER[2], SCATTER[1]), strict=True)
        ]
        (piece_one,) = call(
            pack_kernel,
            (project_qkv, project_out, vectors, expand_bias[None]),
            (shape((BLOCK_ROWS + EXTRA, D)),),
            table=False,
        )
        w1_parts = gather_stream(piece_one, GATHER[0])
        w2_parts = gather_stream(piece_two, GATHER[1])
        w3_parts = gather_stream(piece_three, GATHER[2])
        extras = jnp.concatenate(
            [w1_parts[0][:, BLOCK_ROWS:], w1_parts[1][:, BLOCK_ROWS:]], axis=0
        ).astype(F32)
    else:
        tables = [jnp.asarray(plain_table())] * 3
        piece_one = jnp.concatenate(
            [project_qkv[0], project_qkv[1], project_qkv[2], project_out.T], axis=1
        ).astype(BF16)
        w1_parts, w2_parts, w3_parts = (
            gather_plain(piece) for piece in (piece_one, piece_two, piece_three)
        )
        vector_all = lax.all_gather(vectors.astype(BF16), "dp", axis=1, tiled=True).astype(F32)
        bias_all = lax.all_gather(expand_bias.astype(BF16), "dp", axis=0, tiled=True).astype(F32)
        by_block = vector_all.reshape(11, BLOCKS, BLOCK_ROWS).transpose(1, 0, 2)
        extras = jnp.zeros((BLOCKS, EXTRA, D), F32)
        extras = extras.at[:, :, 0:BLOCK_ROWS].set(by_block[:, 0:8])
        extras = extras.at[:, 0:3, 128 : 128 + BLOCK_ROWS].set(by_block[:, 8:11])
        extras = extras.at[:, 0, 256:640].set(bias_all.reshape(BLOCKS, FF // BLOCKS))

    if direct:
        w1_parts, _ = lax.optimization_barrier((w1_parts, (w2_parts[0], w3_parts[0])))

    def padded(values):
        values = values.reshape(imgs, SEQ, -1)
        return jnp.pad(values, ((0, 0), (0, PAD - SEQ), (0, 0))).reshape(rows, -1)

    positions = lax.broadcasted_iota(jnp.int32, patch_mask.shape, 1)
    replaced = jnp.where((patch_mask == 1) & (positions > 0), 1.0, 0.0).astype(F32)
    rep = padded(replaced)
    tok = padded(tokens)
    cot = padded(cotangent)

    matmul = 2 * rows * D * D
    extra_rows = w1_parts[0].shape[1]
    full = (GROUPS, D, D)
    row_f32 = shape((rows, D), F32)
    row_low = shape((rows, D))
    n_soft = GROUPS * HEADS_IN_GROUP * imgs
    vec, bias, w1, normed, qkv, soft, att, attn, mid, normed_two = call(
        functools.partial(attend_kernel, imgs),
        (tables[0], tok, rep, extras, *w1_parts),
        (
            shape((16, D), F32),
            shape((GROUPS, 1, D), F32),
            shape(full),
            row_low,
            shape((GROUPS, rows, 3 * GROUP_COLS)),
            shape((n_soft, PAD, PAD), F32),
            shape((GROUPS, rows, GROUP_COLS)),
            row_f32,
            row_f32,
            row_low,
        ),
        (pltpu.VMEM((GROUPS, 1, GROUP_COLS), F32), pltpu.VMEM((GROUPS, 1, GROUP_COLS), F32)),
        flops=6 * matmul,
        moved=20_000_000,
    )
    half = shape((16, BLOCK_ROWS, D))
    w2, active, slope, grad_branch, reduce_own, reduce_sib = call(
        expand_kernel,
        (tables[1], normed_two, cot, vec, bias, *w2_parts),
        (
            shape(full),
            shape((GROUPS, rows, D)),
            shape((GROUPS, rows, D), F32),
            row_low,
            half,
            half,
        ),
        flops=8 * matmul,
        moved=20_000_000,
    )
    w3, grad_hidden, bias_grad, expand_own, expand_sib = call(
        hidden_kernel,
        (tables[2], normed_two, grad_branch, slope, *w3_parts),
        (
            shape(full),
            shape((GROUPS, rows, D)),
            shape((GROUPS, 1, D), F32),
            half,
            half,
        ),
        flops=8 * matmul,
        moved=20_000_000,
    )
    block_out, grad_mid, grad_attn, sums = call(
        middle_kernel,
        (active, grad_hidden, w2, w3, mid, attn, cot, vec),
        (row_low, row_f32, row_low, shape((16, D), F32)),
        (pltpu.VMEM((rows, D), F32), pltpu.VMEM((rows, D), F32)),
        flops=8 * matmul,
        moved=20_000_000,
        table=False,
    )
    block_rows = BLOCK_ROWS + EXTRA
    tok_grad, first_own, first_sib = call(
        functools.partial(back_kernel, imgs),
        (tables[0], tok, rep, vec, w1, normed, qkv, soft, att, grad_attn, grad_mid, sums, bias_grad),
        (row_low, shape((16, block_rows, D)), shape((16, block_rows, D))),
        (
            pltpu.VMEM(full, F32),
            pltpu.VMEM((rows, D), F32),
            pltpu.VMEM((rows, 3 * GROUP_COLS), BF16),
            pltpu.VMEM((GROUPS, 1, GROUP_COLS), F32),
            pltpu.VMEM((GROUPS, 1, GROUP_COLS), F32),
            pltpu.VMEM((BLOCKS, EXTRA, D), F32),
            pltpu.VMEM((16, D), F32),
        ),
        flops=12 * matmul,
        moved=30_000_000,
    )

    def cut(values):
        return values.reshape(imgs, PAD, D)[:, :SEQ].reshape(imgs * SEQ, D)

    if direct:
        grad_three = scatter_stream(reduce_own, reduce_sib, SCATTER[2], False)
        grad_two = scatter_stream(expand_own, expand_sib, SCATTER[1], False)
        both = scatter_stream(first_own, first_sib, SCATTER[0], True)
        grad_one, mine = both[:BLOCK_ROWS], both[BLOCK_ROWS:]
        other = lax.ppermute(mine, AXES, CORE_PAIRS)
        mine = jnp.where(lax.axis_index("tensor") % 2 == 0, mine, other)
        vector_grad = jnp.concatenate([mine[:, 0:wide], mine[0:3, 128 : 128 + wide]], axis=0)
        grad_bias = mine[0, 256:640]
    else:
        grad_three = scatter_plain(reduce_own, reduce_sib, n_dp)
        grad_two = scatter_plain(expand_own, expand_sib, n_dp)
        grad_one = scatter_plain(
            first_own[:, :BLOCK_ROWS], first_sib[:, :BLOCK_ROWS], n_dp
        )
        packed = first_own[0::2, BLOCK_ROWS:].astype(F32)
        low = packed[:, :, 0:BLOCK_ROWS].transpose(1, 0, 2).reshape(8, D)
        high = packed[:, 0:3, 128 : 128 + BLOCK_ROWS].transpose(1, 0, 2).reshape(3, D)
        vector_sum, bias_sum = lax.psum(
            (jnp.concatenate([low, high], axis=0), packed[:, 0, 256:640].reshape(-1)), AXES
        )
        spot = lax.axis_index("dp")
        vector_grad = lax.dynamic_slice_in_dim(vector_sum, spot * wide, wide, 1)
        units = expand_bias.shape[0]
        grad_bias = lax.dynamic_slice_in_dim(bias_sum, spot * units, units, 0)
    grad_qkv = jnp.stack([grad_one[:, i * GROUP_COLS : (i + 1) * GROUP_COLS] for i in range(3)])
    grad_out = grad_one[:, 3 * GROUP_COLS :].T
    return (
        cut(block_out),
        cut(tok_grad),
        *adam_update(project_qkv, grad_qkv, first_qkv, second_qkv, RATE_MATRIX, DECAY),
        *adam_update(project_out, grad_out, first_out, second_out, RATE_MATRIX, DECAY),
        *adam_update(expand_weight, grad_two, first_expand, second_expand, RATE_MATRIX, DECAY),
        *adam_update(reduce_weight, grad_three.T, first_reduce, second_reduce, RATE_MATRIX, DECAY),
        *adam_update(vectors, vector_grad, first_vectors, second_vectors, RATE_VECTOR, 0.0),
        *adam_update(expand_bias, grad_bias, first_bias, second_bias, RATE_VECTOR, 0.0),
    )


def solution(mesh):
    rows = P(AXES, None)
    states = (
        *(P(None, "dp", "tensor"),) * 3,
        *(P("tensor", "dp"),) * 3,
        *(P("dp", "tensor"),) * 3,
        *(P("tensor", "dp"),) * 3,
        *(P(None, "dp"),) * 3,
        *(P("dp"),) * 3,
    )
    return jax.shard_map(
        functools.partial(on_device, mesh.shape["dp"]),
        mesh=mesh,
        in_specs=(rows, rows, rows, *states),
        out_specs=(rows, rows, *states),
        check_vma=False,
    )
```

```python
import functools

import jax
import jax.numpy as jnp
import numpy as np
from jax import lax
from jax.experimental import pallas as pl
from jax.experimental.pallas import tpu as pltpu
from jax.sharding import PartitionSpec as P

D = 768
HEAD_DIM = 64
FF = 3072
SEQ = 197
STEP = 4
BETA_ONE = 0.5
BETA_TWO = 0.5
EPSILON = 1e-08
DECAY = 0.05
RATE_MATRIX = 0.02
RATE_VECTOR = 0.2
NORM_EPS = 1e-06

AXES = ("dp", "tensor")
PAD = 208
GROUPS = 4
GROUP_COLS = D // GROUPS
HEADS_IN_GROUP = GROUP_COLS // HEAD_DIM
BLOCKS = 8
BLOCK_ROWS = D // BLOCKS
EXTRA = 8
SCALE = HEAD_DIM**-0.5
SHORT = 1
LONG = 10**11
F32 = jnp.float32
BF16 = jnp.bfloat16

BIT = {"c": 1, "x": 2, "y": 4, "1": 8, "2": 16}
GATHER = (("12yx", "21xy"), ("xy21", "2y1x"), ("1x2y", "y21x"))
SCATTER = (("2y1x", "12xy"), ("21xy", "2xy1"), ("2y1x", "12xy"))
STEPS = "S0S1S2D0S0D1S1D2S2D1S1D0S0F0D2S2D0S0D1S1D2S2F1D0"


def offset_of(order, place):
    found = 0
    for level in range(4):
        if place >> level & 1:
            found ^= BIT[order[level]]
    return found


def pairs_of(orders, level):
    return [(dev, dev ^ BIT[orders[dev & 1][level]]) for dev in range(32)]


CORE_PAIRS = [(dev, dev ^ 1) for dev in range(32)]


def build_table(gather, scatter):
    table = np.zeros((32, 80), np.int32)
    for dev in range(32):
        core = dev & 1
        for place in range(16):
            table[dev, place] = dev ^ offset_of(gather[core], place)
            table[dev, 16 + place] = dev ^ 1 ^ offset_of(gather[1 - core], place)
            mine = dev ^ offset_of(gather[core], place)
            if mine & 3 == dev & 3:
                table[dev, 32 + (mine >> 2)] = place
            table[dev, 40 + (dev ^ offset_of(scatter[core], place))] = place
            table[dev, 40 + (dev ^ 1 ^ offset_of(scatter[1 - core], place))] = place
        table[dev, 72] = core
    return table


def plain_table():
    table = np.zeros((80,), np.int32)
    for place in range(32):
        table[place] = (place % 8) * 4 + place // 8
    for block in range(8):
        table[32 + block] = block
        for group in range(4):
            table[40 + block * 4 + group] = block * 2 + group // 2
    return table


def dot(left, right):
    return jnp.dot(left, right, preferred_element_type=F32)


def dot_rt(left, right):
    return lax.dot_general(left, right, (((1,), (1,)), ((), ())), preferred_element_type=F32)


def dot_lt(left, right):
    return lax.dot_general(left, right, (((0,), (0,)), ((), ())), preferred_element_type=F32)


def norm_stats(values):
    mean = jnp.mean(values, axis=-1, keepdims=True)
    centred = values - mean
    var = jnp.mean(centred * centred, axis=-1, keepdims=True)
    rstd = lax.rsqrt(var + NORM_EPS)
    return centred * rstd, rstd


def norm_back(grad, gain, unit, rstd):
    grad_unit = grad * gain
    first = jnp.mean(grad_unit, axis=-1, keepdims=True)
    second = jnp.mean(grad_unit * unit, axis=-1, keepdims=True)
    return rstd * (grad_unit - first - unit * second)


def col_sum(values):
    return jnp.sum(values, axis=0, keepdims=True)


def assemble(tab, parts, whole):
    for index, part in enumerate(parts):
        for place in range(8):
            owner = tab[index * 8 + place]
            row = pl.multiple_of((owner >> 2) * BLOCK_ROWS, BLOCK_ROWS)
            whole[owner & 3, pl.ds(row, BLOCK_ROWS), :] = part[place, 0:BLOCK_ROWS, :]


def put_blocks(tab, group, grad, out):
    for block in range(BLOCKS):
        place = tab[40 + block * 4 + group]
        rows = slice(block * BLOCK_ROWS, (block + 1) * BLOCK_ROWS)
        out[place] = grad[rows].astype(BF16)


def mask_rows(tok, rep, vec):
    replaced = rep[...]
    return tok[...].astype(F32) * (1.0 - replaced) + vec[6:7, :] * replaced


def pad_kernel(values, out):
    wide = values[...].astype(F32)
    gap = jnp.zeros((PAD - SEQ, D), F32)
    rows = []
    for start in range(0, wide.shape[0], SEQ):
        rows += [wide[start : start + SEQ], gap]
    out[...] = jnp.concatenate(rows, axis=0).astype(BF16)


def cut_kernel(values, out):
    wide = values[...].astype(F32)
    rows = [wide[start : start + SEQ] for start in range(0, wide.shape[0], PAD)]
    out[...] = jnp.concatenate(rows, axis=0).astype(BF16)


def fence_kernel(values, out):
    out[...] = values[...] + 1.0


def pack_kernel(project_qkv, project_out, vectors, expand_bias, out):
    columns = [project_qkv[0], project_qkv[1], project_qkv[2], project_out[...].T]
    block = jnp.concatenate(columns, axis=1)
    fill = jnp.zeros((EXTRA, 128 - BLOCK_ROWS), F32)
    low = jnp.concatenate([vectors[0:8, :], fill], axis=1)
    high = jnp.concatenate([vectors[8:11, :], jnp.zeros((5, BLOCK_ROWS), F32)], axis=0)
    high = jnp.concatenate([high, fill], axis=1)
    last = jnp.concatenate([expand_bias[...], jnp.zeros((EXTRA - 1, 384), F32)], axis=0)
    extra = jnp.concatenate([low, high, last, jnp.zeros((EXTRA, 128), F32)], axis=1)
    out[...] = jnp.concatenate([block, extra], axis=0).astype(BF16)


def attend_kernel(
    imgs, tab, tok, rep, b0, b1, b2, b3,
    vec, bias, w1, normed, qkv, soft, att, attn, mid, normed_two, qb, vb,
):
    low = jnp.zeros((8, D), F32)
    high = jnp.zeros((8, D), F32)
    fill = jnp.zeros((8, D - 128), F32)
    for block in range(BLOCKS):
        place = tab[32 + block]
        near = b0[place & 7].astype(F32)[BLOCK_ROWS:]
        far = b1[place & 7].astype(F32)[BLOCK_ROWS:]
        piece = jnp.where(place < 8, near, far)
        low += pltpu.roll(jnp.concatenate([piece[:, 0:128], fill], 1), block * BLOCK_ROWS, 1)
        high += pltpu.roll(jnp.concatenate([piece[:, 128:256], fill], 1), block * BLOCK_ROWS, 1)
        half = (block % 2) * 384
        bias[block // 2, 0:1, half : half + 384] = piece[0:1, 256:640]
    vec[0:8, :] = low
    vec[8:16, :] = high
    for group in range(GROUPS):
        cols = slice(group * GROUP_COLS, (group + 1) * GROUP_COLS)
        qb[group, 0:1, :] = vec[9:10, cols]
        vb[group, 0:1, :] = vec[10:11, cols]
    assemble(tab, (b0, b1, b2, b3), w1)
    start = mask_rows(tok, rep, vec)
    unit, _ = norm_stats(start)
    normed[...] = (unit * vec[0:1, :] + vec[1:2, :]).astype(BF16)
    attn[...] = jnp.zeros_like(attn)
    keep = lax.broadcasted_iota(jnp.int32, (PAD, PAD), 1) < SEQ

    def step(group, carry):
        result = dot(normed[...], w1[group, :, 0:576])
        qkv[group, :, 0:192] = (result[:, 0:192] + qb[group, 0:1, :]).astype(BF16)
        qkv[group, :, 192:384] = result[:, 192:384].astype(BF16)
        qkv[group, :, 384:576] = (result[:, 384:576] + vb[group, 0:1, :]).astype(BF16)
        for head in range(HEADS_IN_GROUP):
            c0 = head * HEAD_DIM
            for img in range(imgs):
                rows = slice(img * PAD, (img + 1) * PAD)
                q = qkv[group, rows, c0 : c0 + 64]
                k = qkv[group, rows, 192 + c0 : 256 + c0]
                v = qkv[group, rows, 384 + c0 : 448 + c0]
                scores = jnp.where(keep, dot_rt(q, k) * SCALE, -1e30)
                top = jnp.max(scores, axis=-1, keepdims=True)
                raised = jnp.exp(scores - top)
                weights = raised / jnp.sum(raised, axis=-1, keepdims=True)
                soft[group * (HEADS_IN_GROUP * imgs) + head * imgs + img] = weights
                att[group, rows, c0 : c0 + 64] = dot(weights.astype(BF16), v).astype(BF16)
        attn[...] += dot_rt(att[group], w1[group, :, 576:768])
        return carry

    lax.fori_loop(0, GROUPS, step, 0)
    middle = start + vec[4:5, :] * (attn[...] + vec[7:8, :])
    mid[...] = middle
    unit_two, _ = norm_stats(middle)
    normed_two[...] = (unit_two * vec[2:3, :] + vec[3:4, :]).astype(BF16)


def expand_groups(tab, part, normed_two, grad_branch, bias, w2, active, slope, out):
    def step(along_x, carry):
        group = along_x * 2 + (tab[72] ^ part)
        hidden = dot(normed_two[...], w2[group]) + bias[group, 0:1, :]
        cdf = 0.5 * (1.0 + lax.erf(hidden * 0.7071067811865476))
        pdf = 0.3989422804014327 * jnp.exp(-0.5 * hidden * hidden)
        act = (hidden * cdf).astype(BF16)
        active[along_x] = act
        slope[along_x] = cdf + hidden * pdf
        put_blocks(tab, group, dot_lt(grad_branch[...], act), out)
        return carry

    lax.fori_loop(0, 2, step, 0)


def expand_sib_kernel(
    tab, normed_two, cot, vec, bias, b0, b1, b2, b3, w2, active, slope, grad_branch, out
):
    assemble(tab, (b0, b1, b2, b3), w2)
    grad_branch[...] = (cot[...].astype(F32) * vec[5:6, :]).astype(BF16)
    expand_groups(tab, 1, normed_two, grad_branch, bias, w2, active, slope, out)


def expand_own_kernel(tab, normed_two, grad_branch, bias, w2, active, slope, out):
    expand_groups(tab, 0, normed_two, grad_branch, bias, w2, active, slope, out)


def hidden_groups(tab, part, normed_two, grad_branch, slope, w3, grad_hidden, bias_grad, out):
    def step(along_x, carry):
        group = along_x * 2 + (tab[72] ^ part)
        grad = (dot(grad_branch[...], w3[group]) * slope[along_x]).astype(BF16)
        grad_hidden[along_x] = grad
        bias_grad[along_x, 0:1, :] = col_sum(grad.astype(F32))
        put_blocks(tab, group, dot_lt(normed_two[...], grad), out)
        return carry

    lax.fori_loop(0, 2, step, 0)


def hidden_sib_kernel(
    tab, normed_two, grad_branch, slope, b0, b1, b2, b3, w3, grad_hidden, bias_grad, out
):
    assemble(tab, (b0, b1, b2, b3), w3)
    hidden_groups(tab, 1, normed_two, grad_branch, slope, w3, grad_hidden, bias_grad, out)


def hidden_own_kernel(tab, normed_two, grad_branch, slope, w3, grad_hidden, bias_grad, out):
    hidden_groups(tab, 0, normed_two, grad_branch, slope, w3, grad_hidden, bias_grad, out)


def middle_kernel(
    tab, act_sib, act_own, hid_sib, hid_own, w2, w3, mid, attn, cot, vec,
    block_out, grad_mid, grad_attn, sums, branch, grad_two,
):
    branch[...] = jnp.zeros_like(branch)
    grad_two[...] = jnp.zeros_like(grad_two)
    sums[...] = jnp.zeros_like(sums)
    for part, active, grad_hidden in ((1, act_sib, hid_sib), (0, act_own, hid_own)):

        def step(along_x, carry, part=part, active=active, grad_hidden=grad_hidden):
            group = along_x * 2 + (tab[72] ^ part)
            branch[...] += dot_rt(active[along_x], w3[group])
            grad_two[...] += dot_rt(grad_hidden[along_x], w2[group])
            return carry

        lax.fori_loop(0, 2, step, 0)
    middle = mid[...]
    total = branch[...] + vec[8:9, :]
    block_out[...] = (middle + vec[5:6, :] * total).astype(BF16)
    grad_out = cot[...].astype(F32)
    sums[5:6, :] = col_sum(grad_out * total)
    sums[8:9, :] = col_sum(grad_out * vec[5:6, :])
    unit, rstd = norm_stats(middle)
    grad = grad_two[...]
    sums[2:3, :] = col_sum(grad * unit)
    sums[3:4, :] = col_sum(grad)
    grad_middle = grad_out + norm_back(grad, vec[2:3, :], unit, rstd)
    grad_mid[...] = grad_middle
    sums[4:5, :] = col_sum(grad_middle * (attn[...] + vec[7:8, :]))
    scaled = grad_middle * vec[4:5, :]
    sums[7:8, :] = col_sum(scaled)
    grad_attn[...] = scaled.astype(BF16)


def back_groups(
    imgs, tab, part, w1, normed, qkv, soft, att, grad_attn, out, grad_one, gqkv, bias_sums
):
    def step(along_x, carry):
        group = along_x * 2 + (tab[72] ^ part)
        grad_att = dot(grad_attn[...], w1[group, :, 576:768]).astype(BF16)
        for head in range(HEADS_IN_GROUP):
            c0 = head * HEAD_DIM
            for img in range(imgs):
                rows = slice(img * PAD, (img + 1) * PAD)
                q = qkv[group, rows, c0 : c0 + 64]
                k = qkv[group, rows, 192 + c0 : 256 + c0]
                v = qkv[group, rows, 384 + c0 : 448 + c0]
                weights = soft[group * (HEADS_IN_GROUP * imgs) + head * imgs + img]
                grad = grad_att[rows, c0 : c0 + 64]
                grad_soft = dot_rt(grad, v)
                grad_v = dot_lt(weights.astype(BF16), grad)
                inner = jnp.sum(weights * grad_soft, axis=-1, keepdims=True)
                grad_scores = (weights * (grad_soft - inner)).astype(BF16)
                grad_q = dot(grad_scores, k) * SCALE
                grad_k = dot_lt(grad_scores, q) * SCALE
                gqkv[rows, c0 : c0 + 64] = grad_q.astype(BF16)
                gqkv[rows, 192 + c0 : 256 + c0] = grad_k.astype(BF16)
                gqkv[rows, 384 + c0 : 448 + c0] = grad_v.astype(BF16)
        all_grads = gqkv[...]
        bias_sums[along_x, 0:1, :] = col_sum(all_grads[:, 0:192].astype(F32))
        bias_sums[along_x, 1:2, :] = col_sum(all_grads[:, 384:576].astype(F32))
        grad_one[...] += dot_rt(all_grads, w1[group, :, 0:576])
        both = jnp.concatenate(
            [dot_lt(normed[...], all_grads), dot_lt(grad_attn[...], att[group])], axis=1
        )
        put_blocks(tab, group, both, out)
        return carry

    lax.fori_loop(0, 2, step, 0)


def back_sib_kernel(
    imgs, tab, w1, normed, qkv, soft, att, grad_attn, out, grad_one, bias_sums, gqkv
):
    grad_one[...] = jnp.zeros_like(grad_one)
    back_groups(
        imgs, tab, 1, w1, normed, qkv, soft, att, grad_attn, out, grad_one, gqkv, bias_sums
    )


def back_own_kernel(
    imgs, tab, w1, normed, qkv, soft, att, grad_attn, grad_one_in, out, grad_one, bias_sums, gqkv
):
    grad_one[...] = grad_one_in[...]
    back_groups(
        imgs, tab, 0, w1, normed, qkv, soft, att, grad_attn, out, grad_one, gqkv, bias_sums
    )


def start_kernel(
    tab, tok, rep, vec, grad_one, bias_sib, bias_own, grad_mid, sums_in, units_sib, units_own,
    tok_grad, sums,
):
    replaced = rep[...]
    unit, rstd = norm_stats(mask_rows(tok, rep, vec))
    grad = grad_one[...]
    sums[0:16, :] = sums_in[...]
    sums[16:24, :] = jnp.zeros((8, D), F32)
    sums[0:1, :] = col_sum(grad * unit)
    sums[1:2, :] = col_sum(grad)
    grad_start = grad_mid[...] + norm_back(grad, vec[0:1, :], unit, rstd)
    tok_grad[...] = (grad_start * (1.0 - replaced)).astype(BF16)
    sums[6:7, :] = col_sum(grad_start * replaced)
    for group in range(GROUPS):
        cols = slice(group * GROUP_COLS, (group + 1) * GROUP_COLS)
        own = tab[72] == group % 2
        along_x = group // 2
        both = jnp.where(own, bias_own[along_x], bias_sib[along_x])
        sums[9:10, cols] = both[0:1]
        sums[10:11, cols] = both[1:2]
        sums[16 + group : 17 + group, :] = jnp.where(own, units_own[along_x], units_sib[along_x])


def adam_update(weight, gradient, first_moment, second, step_rate, decay_rate):
    moment = BETA_ONE * first_moment + (1.0 - BETA_ONE) * gradient
    square = BETA_TWO * second + (1.0 - BETA_TWO) * gradient * gradient
    first_hat = moment / (1.0 - BETA_ONE**STEP)
    second_hat = square / (1.0 - BETA_TWO**STEP)
    updated = weight - step_rate * (
        first_hat / (jnp.sqrt(second_hat) + EPSILON) + decay_rate * weight
    )
    return (updated, moment, square)


def finish_kernel(
    partial, last, qkv, first_qkv, second_qkv, out, first_out, second_out, *results
):
    grad = partial[...] + last[...].astype(F32)
    for index in range(3):
        cols = slice(index * GROUP_COLS, (index + 1) * GROUP_COLS)
        found = adam_update(
            qkv[index], grad[:, cols], first_qkv[index], second_qkv[index], RATE_MATRIX, DECAY
        )
        for result, values in zip(results[:3], found, strict=True):
            result[index] = values
    found = adam_update(
        out[...], grad[:, 576:768].T, first_out[...], second_out[...], RATE_MATRIX, DECAY
    )
    for result, values in zip(results[3:], found, strict=True):
        result[...] = values


VMEM = pl.BlockSpec(memory_space=pltpu.VMEM)
SMEM = pl.BlockSpec(memory_space=pltpu.SMEM)


def shape(dims, dtype=BF16):
    return jax.ShapeDtypeStruct(dims, dtype)


def call(kernel, args, outs, scratch=(), flops=SHORT, megabytes=10, table=True):
    return pl.pallas_call(
        kernel,
        out_shape=outs,
        in_specs=[SMEM] * table + [VMEM] * (len(args) - table),
        out_specs=[VMEM] * len(outs),
        scratch_shapes=list(scratch),
        cost_estimate=pl.CostEstimate(flops=flops, bytes_accessed=1, transcendentals=0),
        compiler_params=pltpu.CompilerParams(vmem_limit_bytes=megabytes << 20),
    )(*args)


def after(value, *earlier):
    return lax.optimization_barrier((value, earlier))[0]


def add_across(values, *masks):
    for mask in masks:
        pairs = [(dev, dev ^ mask) for dev in range(32)]
        values = values + lax.ppermute(values, AXES, pairs)
    return values


class Gather:
    def __init__(self, block, orders):
        self.held = block[None]
        self.orders = orders
        self.level = 0
        self.taken = None

    def start(self, *earlier):
        if earlier:
            self.held = after(self.held, *earlier)
        self.taken = lax.ppermute(self.held, AXES, pairs_of(self.orders, self.level))
        self.level += 1
        if self.level == 4:
            self.held_sib = lax.ppermute(self.held, AXES, CORE_PAIRS)

    def take(self):
        if self.level < 4:
            self.held = jnp.concatenate([self.held, self.taken], axis=0)
        return self.taken

    def finish(self, *earlier):
        while self.level < 4:
            self.taken = after(self.taken, *earlier)
            self.take()
            self.start()

    def parts(self, *earlier):
        if earlier:
            self.taken = after(self.taken, *earlier)
        self.taken_sib = lax.ppermute(self.taken, AXES, CORE_PAIRS)
        return self.held, self.taken, self.held_sib, self.taken_sib


class Scatter:
    def __init__(self, orders):
        self.orders = orders
        self.level = 4
        self.terms = []

    def swap(self, sib):
        self.terms.append(lax.ppermute(sib, AXES, CORE_PAIRS))

    def add(self, own):
        self.terms.insert(0, own)

    def total(self, low, high):
        return sum(term[low:high].astype(F32) for term in self.terms)

    def step(self, *earlier):
        self.level -= 1
        size = 1 << self.level
        if earlier:
            self.terms[-1] = after(self.terms[-1], *earlier)
        sent = self.total(size, 2 * size).astype(BF16)
        self.terms.append(lax.ppermute(sent, AXES, pairs_of(self.orders, self.level)))
        return sent

    def result(self):
        return self.total(0, 1)[0]


def gather_plain(block):
    whole = lax.all_gather(block, AXES, axis=0, tiled=False)
    whole = whole.reshape(-1, GROUPS, *block.shape).transpose(1, 0, 2, 3)
    whole = whole.reshape(GROUPS, BLOCKS, BLOCK_ROWS, D)
    return tuple(whole[group] for group in range(GROUPS))


def scatter_plain(own, sib, n_dp):
    parts = jnp.stack([own, sib]).reshape(2, BLOCKS, 2, BLOCK_ROWS, D)
    whole = parts.transpose(1, 3, 2, 0, 4).reshape(D, GROUPS, D).astype(F32)
    whole = whole.reshape(n_dp, D // n_dp, GROUPS, D).transpose(0, 2, 1, 3)
    whole = whole.reshape(n_dp * GROUPS, D // n_dp, D)
    return lax.psum_scatter(whole, AXES, scatter_dimension=0, tiled=True)[0]


def on_device(
    n_dp,
    tokens,
    patch_mask,
    cotangent,
    project_qkv,
    first_qkv,
    second_qkv,
    project_out,
    first_out,
    second_out,
    expand_weight,
    first_expand,
    second_expand,
    reduce_weight,
    first_reduce,
    second_reduce,
    vectors,
    first_vectors,
    second_vectors,
    expand_bias,
    first_bias,
    second_bias,
):
    direct = n_dp == BLOCKS
    imgs = patch_mask.shape[0]
    rows = imgs * PAD
    wide = vectors.shape[1]
    units = expand_bias.shape[0]

    def padded(values):
        values = values.reshape(imgs, SEQ, -1)
        return jnp.pad(values, ((0, 0), (0, PAD - SEQ), (0, 0))).reshape(rows, -1)

    positions = lax.broadcasted_iota(jnp.int32, patch_mask.shape, 1)
    replaced = jnp.where((patch_mask == 1) & (positions > 0), 1.0, 0.0).astype(F32)
    rep = padded(replaced)

    def cut(values):
        out = shape((imgs * SEQ, D))
        return call(cut_kernel, (values,), (out,), table=False)[0]

    def pad_rows(values):
        return call(pad_kernel, (values,), (shape((rows, D)),), flops=LONG, table=False)[0]

    piece_two = expand_weight.astype(BF16)
    piece_three = reduce_weight.astype(BF16).T
    if direct:
        flat = lax.axis_index("dp") * GROUPS + lax.axis_index("tensor")
        chosen = zip(GATHER, (SCATTER[0], SCATTER[2], SCATTER[1]), strict=True)
        every = np.concatenate([build_table(g, s) for g, s in chosen], axis=1)
        table = lax.dynamic_index_in_dim(jnp.asarray(every), flat, 0, keepdims=False)
        tables = [table[0:80], table[80:160], table[160:240]]
        (piece_one,) = call(
            pack_kernel,
            (project_qkv, project_out, vectors, expand_bias[None]),
            (shape((BLOCK_ROWS + EXTRA, D)),),
            table=False,
        )
        streams = [
            Gather(piece, orders)
            for piece, orders in zip((piece_one, piece_two, piece_three), GATHER, strict=True)
        ]
        seen = {}
        mark = jnp.zeros((8, 128), F32)
        for kind, index in zip(STEPS[0::2], STEPS[1::2], strict=True):
            stream = streams[int(index)]
            held = [stream.held for stream in streams]
            if kind == "X":
                mark = after(mark, *held, *seen.values())
                (mark,) = call(fence_kernel, (mark,), (shape((8, 128), F32),), flops=LONG, table=False)
                seen["mark"] = mark
            elif kind == "F":
                if index == "0":
                    tok = pad_rows(after(tokens, *held))
                    seen["tok"] = (tok, rep, *tables)
                else:
                    cot = pad_rows(after(cotangent, *held))
                    seen["cot"] = cot
            elif kind == "S":
                stream.start(*seen.values())
            else:
                seen[index] = stream.take()
        w1_parts = streams[0].parts(*[seen[name] for name in seen if name not in "12"])
    else:
        tables = [jnp.asarray(plain_table())] * 3
        tok, cot = pad_rows(tokens), pad_rows(cotangent)
        piece_one = jnp.concatenate(
            [project_qkv[0], project_qkv[1], project_qkv[2], project_out.T], axis=1
        ).astype(BF16)
        w1_parts, w2_parts, w3_parts = (
            gather_plain(piece) for piece in (piece_one, piece_two, piece_three)
        )
        vector_all = lax.all_gather(vectors.astype(BF16), "dp", axis=1, tiled=True)
        bias_all = lax.all_gather(expand_bias.astype(BF16), "dp", axis=0, tiled=True)
        by_block = vector_all.reshape(11, BLOCKS, BLOCK_ROWS).transpose(1, 0, 2)
        extras = jnp.zeros((BLOCKS, EXTRA, D), BF16)
        extras = extras.at[:, :, 0:BLOCK_ROWS].set(by_block[:, 0:8])
        extras = extras.at[:, 0:3, 128 : 128 + BLOCK_ROWS].set(by_block[:, 8:11])
        extras = extras.at[:, 0, 256:640].set(bias_all.reshape(BLOCKS, FF // BLOCKS))
        w1_parts = tuple(jnp.concatenate([part, extras], axis=1) for part in w1_parts)

    full = (GROUPS, D, D)
    row_f32 = shape((rows, D), F32)
    row_low = shape((rows, D))
    half = shape((16, BLOCK_ROWS, D))
    two_low = shape((2, rows, D))
    two_f32 = shape((2, rows, D), F32)
    two_bias = shape((2, 1, D), F32)
    group_bias = pltpu.VMEM((GROUPS, 1, GROUP_COLS), F32)
    n_soft = GROUPS * HEADS_IN_GROUP * imgs
    vec, bias, w1, normed, qkv, soft, att, attn, mid, normed_two = call(
        functools.partial(attend_kernel, imgs),
        (tables[0], tok, rep, *w1_parts),
        (
            shape((16, D), F32),
            shape((GROUPS, 1, D), F32),
            shape(full),
            row_low,
            shape((GROUPS, rows, 3 * GROUP_COLS)),
            shape((n_soft, PAD, PAD), F32),
            shape((GROUPS, rows, GROUP_COLS)),
            row_f32,
            row_f32,
            row_low,
        ),
        (group_bias, group_bias),
        flops=SHORT,
    )
    if direct:
        streams[1].finish(normed_two)
        streams[2].finish(normed_two)
        w2_parts = streams[1].parts(normed_two)
    three, two, one = (Scatter(SCATTER[index]) for index in (2, 1, 0))
    w2, act_sib, slope_sib, grad_branch, reduce_sib = call(
        expand_sib_kernel,
        (tables[1], normed_two, cot, vec, bias, *w2_parts),
        (shape(full), two_low, two_f32, row_low, half),
        flops=SHORT,
    )
    if direct:
        three.swap(reduce_sib)
    act_own, slope_own, reduce_own = call(
        expand_own_kernel,
        (tables[1], normed_two, grad_branch, bias, w2),
        (two_low, two_f32, half),
        flops=LONG,
    )
    if direct:
        w3_parts = streams[2].parts(reduce_own)
        three.add(reduce_own)
        w3_parts = after(w3_parts, three.step())
    w3, hid_sib, units_sib, expand_sib = call(
        hidden_sib_kernel,
        (tables[2], normed_two, grad_branch, slope_sib, *w3_parts),
        (shape(full), two_low, two_bias, half),
        flops=SHORT,
    )
    if direct:
        two.swap(expand_sib)
    hid_own, units_own, expand_own = call(
        hidden_own_kernel,
        (tables[2], normed_two, grad_branch, slope_own, w3),
        (two_low, two_bias, half),
        flops=LONG,
    )
    if direct:
        two.add(expand_own)
        mid = after(mid, two.step())
    block_out, grad_mid, grad_attn, sums = call(
        middle_kernel,
        (tables[0], act_sib, act_own, hid_sib, hid_own, w2, w3, mid, attn, cot, vec),
        (row_low, row_f32, row_low, shape((16, D), F32)),
        (pltpu.VMEM((rows, D), F32), pltpu.VMEM((rows, D), F32)),
        flops=SHORT,
    )
    if direct:
        grad_attn = after(grad_attn, three.step(sums))
    shared = (w1, normed, qkv, soft, att, grad_attn)
    held = pltpu.VMEM((rows, 3 * GROUP_COLS), BF16)
    bias_sums = (2, 2, GROUP_COLS)
    first_sib, grad_one, bias_sib = call(
        functools.partial(back_sib_kernel, imgs),
        (tables[0], *shared),
        (half, row_f32, shape(bias_sums, F32)),
        (held,),
        flops=SHORT,
    )
    if direct:
        one.swap(first_sib)
        grad_one = after(grad_one, three.step(grad_one), two.step(grad_one))
    first_own, grad_one, bias_own = call(
        functools.partial(back_own_kernel, imgs),
        (tables[0], *shared, grad_one),
        (half, row_f32, shape(bias_sums, F32)),
        (held,),
        flops=LONG,
    )
    if direct:
        first_own, grad_one = after((first_own, grad_one), three.terms[-1], two.terms[-1])
        one.add(first_own)
        sent = one.step()
        grad_one = after(grad_one, three.step(sent), two.step(sent))
    tok_grad, sums = call(
        start_kernel,
        (
            tables[0], tok, rep, vec, grad_one, bias_sib, bias_own, grad_mid, sums,
            units_sib, units_own,
        ),
        (row_low, shape((24, D), F32)),
    )

    if direct:
        sums = add_across(sums, 1, 8, 16)
        block_rows, token_rows = cut(block_out), cut(tok_grad)
        sent = one.step(sums, block_rows, token_rows)
        grad_three = after(three.result(), sent)
        states_three = adam_update(
            reduce_weight, grad_three.T, first_reduce, second_reduce, RATE_MATRIX, DECAY
        )
        sums = add_across(after(sums, sent), 4)
        sent_two = two.step(sent)
        sent = one.step(states_three[0], sent_two, sums)
        sums = add_across(after(sums, sent), 2)
        sent = one.step(sums)
        grad_two = after(two.result(), sent)
        partial = sum(term[0].astype(F32) for term in one.terms[:-1])
        finished = call(
            finish_kernel,
            (
                partial, one.terms[-1][0], project_qkv, first_qkv, second_qkv,
                project_out, first_out, second_out,
            ),
            (shape(project_qkv.shape, F32),) * 3 + (shape(project_out.shape, F32),) * 3,
            table=False,
        )
    else:
        block_rows, token_rows = cut(block_out), cut(tok_grad)
        grad_three = scatter_plain(reduce_own, reduce_sib, n_dp)
        grad_two = scatter_plain(expand_own, expand_sib, n_dp)
        grad_one = scatter_plain(first_own, first_sib, n_dp)
        sums = lax.psum(sums, AXES)
        grad_qkv = jnp.stack([grad_one[:, i * GROUP_COLS : (i + 1) * GROUP_COLS] for i in range(3)])
        grad_out = grad_one[:, 3 * GROUP_COLS :].T
        states_three = adam_update(
            reduce_weight, grad_three.T, first_reduce, second_reduce, RATE_MATRIX, DECAY
        )
        finished = (
            *adam_update(project_qkv, grad_qkv, first_qkv, second_qkv, RATE_MATRIX, DECAY),
            *adam_update(project_out, grad_out, first_out, second_out, RATE_MATRIX, DECAY),
        )
    spot = lax.axis_index("dp")
    vector_grad = lax.dynamic_slice_in_dim(sums[0:11], spot * wide, wide, 1)
    grad_bias = lax.dynamic_slice_in_dim(sums[16:20].reshape(-1), spot * units, units, 0)
    return (
        block_rows,
        token_rows,
        *finished,
        *adam_update(expand_weight, grad_two, first_expand, second_expand, RATE_MATRIX, DECAY),
        *states_three,
        *adam_update(vectors, vector_grad, first_vectors, second_vectors, RATE_VECTOR, 0.0),
        *adam_update(expand_bias, grad_bias, first_bias, second_bias, RATE_VECTOR, 0.0),
    )


def solution(mesh):
    rows = P(AXES, None)
    states = (
        *(P(None, "dp", "tensor"),) * 3,
        *(P("tensor", "dp"),) * 3,
        *(P("dp", "tensor"),) * 3,
        *(P("tensor", "dp"),) * 3,
        *(P(None, "dp"),) * 3,
        *(P("dp"),) * 3,
    )
    return jax.shard_map(
        functools.partial(on_device, mesh.shape["dp"]),
        mesh=mesh,
        in_specs=(rows, rows, rows, *states),
        out_specs=(rows, rows, *states),
        check_vma=False,
    )
```

```python
import functools

import jax
import jax.numpy as jnp
import numpy as np
from jax import lax
from jax.experimental import pallas as pl
from jax.experimental.pallas import tpu as pltpu
from jax.sharding import PartitionSpec as P

D = 768
HEAD_DIM = 64
FF = 3072
SEQ = 197
STEP = 4
BETA_ONE = 0.5
BETA_TWO = 0.5
EPSILON = 1e-08
DECAY = 0.05
RATE_MATRIX = 0.02
RATE_VECTOR = 0.2
NORM_EPS = 1e-06

AXES = ("dp", "tensor")
PAD = 208
GROUPS = 4
GROUP_COLS = D // GROUPS
HEADS_IN_GROUP = GROUP_COLS // HEAD_DIM
BLOCKS = 8
BLOCK_ROWS = D // BLOCKS
EXTRA = 8
SCALE = HEAD_DIM**-0.5
SHORT = 1
LONG = 10**11
F32 = jnp.float32
BF16 = jnp.bfloat16

BIT = {"c": 1, "x": 2, "y": 4, "1": 8, "2": 16}
GATHER = (("12yx", "21xy"), ("xy21", "2y1x"), ("1x2y", "y21x"))
SCATTER = (("21yx", "12xy"), ("2x1y", "x21y"), ("y2x1", "y21x"))
STEPS = "S0S1S2D0S0D1S1D2S2D0S0F0D1S1D0S0D2S2D1S1F1D0"


def offset_of(order, place):
    found = 0
    for level in range(4):
        if place >> level & 1:
            found ^= BIT[order[level]]
    return found


def pairs_of(orders, level):
    return [(dev, dev ^ BIT[orders[dev & 1][level]]) for dev in range(32)]


CORE_PAIRS = [(dev, dev ^ 1) for dev in range(32)]


def build_table(gather, scatter):
    table = np.zeros((32, 80), np.int32)
    for dev in range(32):
        core = dev & 1
        for place in range(16):
            table[dev, place] = dev ^ offset_of(gather[core], place)
            table[dev, 16 + place] = dev ^ 1 ^ offset_of(gather[1 - core], place)
            mine = dev ^ offset_of(gather[core], place)
            if mine & 3 == dev & 3:
                table[dev, 32 + (mine >> 2)] = place
            table[dev, 40 + (dev ^ offset_of(scatter[core], place))] = place
            table[dev, 40 + (dev ^ 1 ^ offset_of(scatter[1 - core], place))] = place
        table[dev, 72] = core
    return table


def plain_table():
    table = np.zeros((80,), np.int32)
    for place in range(32):
        part, along_x, block = place // 16, place // 8 % 2, place % 8
        table[place] = block * 4 + along_x * 2 + part
    for block in range(8):
        table[32 + block] = block
        for group in range(4):
            table[40 + block * 4 + group] = block * 2 + group // 2
    return table


def dot(left, right):
    return jnp.dot(left, right, preferred_element_type=F32)


def dot_rt(left, right):
    return lax.dot_general(left, right, (((1,), (1,)), ((), ())), preferred_element_type=F32)


def dot_lt(left, right):
    return lax.dot_general(left, right, (((0,), (0,)), ((), ())), preferred_element_type=F32)


def norm_stats(values):
    mean = jnp.mean(values, axis=-1, keepdims=True)
    centred = values - mean
    var = jnp.mean(centred * centred, axis=-1, keepdims=True)
    rstd = lax.rsqrt(var + NORM_EPS)
    return centred * rstd, rstd


def norm_back(grad, gain, unit, rstd):
    grad_unit = grad * gain
    first = jnp.mean(grad_unit, axis=-1, keepdims=True)
    second = jnp.mean(grad_unit * unit, axis=-1, keepdims=True)
    return rstd * (grad_unit - first - unit * second)


def col_sum(values):
    return jnp.sum(values, axis=0, keepdims=True)


def assemble(tab, first, parts, whole):
    for index, part in enumerate(parts):
        for place in range(4):
            owner = tab[first + index * 4 + place]
            row = pl.multiple_of((owner >> 2) * BLOCK_ROWS, BLOCK_ROWS)
            whole[(owner >> 1) & 1, pl.ds(row, BLOCK_ROWS), :] = part[place, 0:BLOCK_ROWS, :]


def put_blocks(tab, group, grad, out):
    for block in range(BLOCKS):
        place = tab[40 + block * 4 + group]
        rows = slice(block * BLOCK_ROWS, (block + 1) * BLOCK_ROWS)
        out[place] = grad[rows].astype(BF16)


def mask_rows(tok, rep, vec):
    replaced = rep[...]
    return tok[...].astype(F32) * (1.0 - replaced) + vec[6:7, :] * replaced


def pad_kernel(values, out):
    wide = values[...].astype(F32)
    gap = jnp.zeros((PAD - SEQ, D), F32)
    rows = []
    for start in range(0, wide.shape[0], SEQ):
        rows += [wide[start : start + SEQ], gap]
    out[...] = jnp.concatenate(rows, axis=0).astype(BF16)


def cut_rows(wide):
    rows = [wide[start : start + SEQ] for start in range(0, wide.shape[0], PAD)]
    return jnp.concatenate(rows, axis=0).astype(BF16)


def fence_kernel(values, out):
    out[...] = values[...] + 1.0


def pack_kernel(project_qkv, project_out, vectors, expand_bias, out):
    columns = [project_qkv[0], project_qkv[1], project_qkv[2], project_out[...].T]
    block = jnp.concatenate(columns, axis=1)
    fill = jnp.zeros((EXTRA, 128 - BLOCK_ROWS), F32)
    low = jnp.concatenate([vectors[0:8, :], fill], axis=1)
    high = jnp.concatenate([vectors[8:11, :], jnp.zeros((5, BLOCK_ROWS), F32)], axis=0)
    high = jnp.concatenate([high, fill], axis=1)
    last = jnp.concatenate([expand_bias[...], jnp.zeros((EXTRA - 1, 384), F32)], axis=0)
    extra = jnp.concatenate([low, high, last, jnp.zeros((EXTRA, 128), F32)], axis=1)
    out[...] = jnp.concatenate([block, extra], axis=0).astype(BF16)


def attend_groups(imgs, tab, part, normed, qb, vb, w1, qkv, soft, att, attn):
    keep = lax.broadcasted_iota(jnp.int32, (PAD, PAD), 1) < SEQ

    def step(along_x, carry):
        group = along_x * 2 + (tab[72] ^ part)
        result = dot(normed[...], w1[along_x, :, 0:576])
        qkv[along_x, :, 0:192] = (result[:, 0:192] + qb[group, 0:1, :]).astype(BF16)
        qkv[along_x, :, 192:384] = result[:, 192:384].astype(BF16)
        qkv[along_x, :, 384:576] = (result[:, 384:576] + vb[group, 0:1, :]).astype(BF16)
        for head in range(HEADS_IN_GROUP):
            c0 = head * HEAD_DIM
            for img in range(imgs):
                rows = slice(img * PAD, (img + 1) * PAD)
                q = qkv[along_x, rows, c0 : c0 + 64]
                k = qkv[along_x, rows, 192 + c0 : 256 + c0]
                v = qkv[along_x, rows, 384 + c0 : 448 + c0]
                scores = jnp.where(keep, dot_rt(q, k) * SCALE, -1e30)
                top = jnp.max(scores, axis=-1, keepdims=True)
                raised = jnp.exp(scores - top)
                weights = raised / jnp.sum(raised, axis=-1, keepdims=True)
                soft[along_x * (HEADS_IN_GROUP * imgs) + head * imgs + img] = weights
                att[along_x, rows, c0 : c0 + 64] = dot(weights.astype(BF16), v).astype(BF16)
        attn[...] += dot_rt(att[along_x], w1[along_x, :, 576:768])
        return carry

    lax.fori_loop(0, 2, step, 0)


def attend_own_kernel(
    imgs, tab, tok, rep, b0, b1, b2, b3,
    vec, bias, start_rows, normed, qb, vb, w1, qkv, soft, att, attn,
):
    low = jnp.zeros((8, D), F32)
    high = jnp.zeros((8, D), F32)
    fill = jnp.zeros((8, D - 128), F32)
    for block in range(BLOCKS):
        place = tab[32 + block]
        piece = jnp.zeros((EXTRA, D), F32)
        for index, part in enumerate((b0, b1, b2, b3)):
            rows = part[place & 3].astype(F32)[BLOCK_ROWS:]
            piece = jnp.where(place >> 2 == index, rows, piece)
        low += pltpu.roll(jnp.concatenate([piece[:, 0:128], fill], 1), block * BLOCK_ROWS, 1)
        high += pltpu.roll(jnp.concatenate([piece[:, 128:256], fill], 1), block * BLOCK_ROWS, 1)
        half = (block % 2) * 384
        bias[block // 2, 0:1, half : half + 384] = piece[0:1, 256:640]
    vec[0:8, :] = low
    vec[8:16, :] = high
    for group in range(GROUPS):
        cols = slice(group * GROUP_COLS, (group + 1) * GROUP_COLS)
        qb[group, 0:1, :] = vec[9:10, cols]
        vb[group, 0:1, :] = vec[10:11, cols]
    assemble(tab, 0, (b0, b1, b2, b3), w1)
    start = mask_rows(tok, rep, vec)
    start_rows[...] = start
    unit, _ = norm_stats(start)
    normed[...] = (unit * vec[0:1, :] + vec[1:2, :]).astype(BF16)
    attn[...] = jnp.zeros_like(attn)
    attend_groups(imgs, tab, 0, normed, qb, vb, w1, qkv, soft, att, attn)


def attend_sib_kernel(
    imgs, tab, vec, start_rows, normed, qb, vb, attn_in, b0, b1, b2, b3,
    w1, qkv, soft, att, attn, mid, normed_two,
):
    assemble(tab, 16, (b0, b1, b2, b3), w1)
    attn[...] = attn_in[...]
    attend_groups(imgs, tab, 1, normed, qb, vb, w1, qkv, soft, att, attn)
    middle = start_rows[...] + vec[4:5, :] * (attn[...] + vec[7:8, :])
    mid[...] = middle
    unit_two, _ = norm_stats(middle)
    normed_two[...] = (unit_two * vec[2:3, :] + vec[3:4, :]).astype(BF16)


def expand_groups(tab, part, normed_two, grad_branch, bias, w2, active, slope, out):
    def step(along_x, carry):
        group = along_x * 2 + (tab[72] ^ part)
        hidden = dot(normed_two[...], w2[along_x]) + bias[group, 0:1, :]
        cdf = 0.5 * (1.0 + lax.erf(hidden * 0.7071067811865476))
        pdf = 0.3989422804014327 * jnp.exp(-0.5 * hidden * hidden)
        act = (hidden * cdf).astype(BF16)
        active[along_x] = act
        slope[along_x] = cdf + hidden * pdf
        put_blocks(tab, group, dot_lt(grad_branch[...], act), out)
        return carry

    lax.fori_loop(0, 2, step, 0)


def expand_own_kernel(
    tab, normed_two, cot, vec, bias, b0, b1, b2, b3, w2, active, slope, grad_branch, out
):
    assemble(tab, 0, (b0, b1, b2, b3), w2)
    grad_branch[...] = (cot[...].astype(F32) * vec[5:6, :]).astype(BF16)
    expand_groups(tab, 0, normed_two, grad_branch, bias, w2, active, slope, out)


def expand_sib_kernel(
    tab, normed_two, grad_branch, bias, b0, b1, b2, b3, w2, active, slope, out
):
    assemble(tab, 16, (b0, b1, b2, b3), w2)
    expand_groups(tab, 1, normed_two, grad_branch, bias, w2, active, slope, out)


def hidden_groups(tab, part, normed_two, grad_branch, slope, w3, grad_hidden, bias_grad, out):
    def step(along_x, carry):
        group = along_x * 2 + (tab[72] ^ part)
        grad = (dot(grad_branch[...], w3[along_x]) * slope[along_x]).astype(BF16)
        grad_hidden[along_x] = grad
        bias_grad[along_x, 0:1, :] = col_sum(grad.astype(F32))
        put_blocks(tab, group, dot_lt(normed_two[...], grad), out)
        return carry

    lax.fori_loop(0, 2, step, 0)


def hidden_kernel(
    part, tab, normed_two, grad_branch, slope, b0, b1, b2, b3, w3, grad_hidden, bias_grad, out
):
    assemble(tab, 16 * part, (b0, b1, b2, b3), w3)
    hidden_groups(tab, part, normed_two, grad_branch, slope, w3, grad_hidden, bias_grad, out)


def middle_kernel(
    act_sib, act_own, hid_sib, hid_own, w2_sib, w2_own, w3_sib, w3_own, mid, attn, cot, vec,
    block_out, grad_mid, grad_attn, sums, branch, grad_two,
):
    sums[...] = jnp.zeros_like(sums)
    found = jnp.zeros(branch.shape, F32)
    for active, w3 in ((act_sib, w3_sib), (act_own, w3_own)):
        for along_x in range(2):
            found += dot_rt(active[along_x], w3[along_x])
    branch[...] = found
    found = jnp.zeros(branch.shape, F32)
    for grad_hidden, w2 in ((hid_sib, w2_sib), (hid_own, w2_own)):
        for along_x in range(2):
            found += dot_rt(grad_hidden[along_x], w2[along_x])
    grad_two[...] = found
    middle = mid[...]
    total = branch[...] + vec[8:9, :]
    block_out[...] = cut_rows(middle + vec[5:6, :] * total)
    grad_out = cot[...].astype(F32)
    sums[5:6, :] = col_sum(grad_out * total)
    sums[8:9, :] = col_sum(grad_out * vec[5:6, :])
    unit, rstd = norm_stats(middle)
    grad = grad_two[...]
    sums[2:3, :] = col_sum(grad * unit)
    sums[3:4, :] = col_sum(grad)
    grad_middle = grad_out + norm_back(grad, vec[2:3, :], unit, rstd)
    grad_mid[...] = grad_middle
    sums[4:5, :] = col_sum(grad_middle * (attn[...] + vec[7:8, :]))
    scaled = grad_middle * vec[4:5, :]
    sums[7:8, :] = col_sum(scaled)
    grad_attn[...] = scaled.astype(BF16)


def back_groups(
    imgs, tab, part, w1, normed, qkv, soft, att, grad_attn, out, grad_one, gqkv, bias_sums
):
    def step(along_x, carry):
        group = along_x * 2 + (tab[72] ^ part)
        grad_att = dot(grad_attn[...], w1[along_x, :, 576:768]).astype(BF16)
        for head in range(HEADS_IN_GROUP):
            c0 = head * HEAD_DIM
            for img in range(imgs):
                rows = slice(img * PAD, (img + 1) * PAD)
                q = qkv[along_x, rows, c0 : c0 + 64]
                k = qkv[along_x, rows, 192 + c0 : 256 + c0]
                v = qkv[along_x, rows, 384 + c0 : 448 + c0]
                weights = soft[along_x * (HEADS_IN_GROUP * imgs) + head * imgs + img]
                grad = grad_att[rows, c0 : c0 + 64]
                grad_soft = dot_rt(grad, v)
                grad_v = dot_lt(weights.astype(BF16), grad)
                inner = jnp.sum(weights * grad_soft, axis=-1, keepdims=True)
                grad_scores = (weights * (grad_soft - inner)).astype(BF16)
                grad_q = dot(grad_scores, k) * SCALE
                grad_k = dot_lt(grad_scores, q) * SCALE
                gqkv[rows, c0 : c0 + 64] = grad_q.astype(BF16)
                gqkv[rows, 192 + c0 : 256 + c0] = grad_k.astype(BF16)
                gqkv[rows, 384 + c0 : 448 + c0] = grad_v.astype(BF16)
        all_grads = gqkv[...]
        bias_sums[along_x, 0:1, :] = col_sum(all_grads[:, 0:192].astype(F32))
        bias_sums[along_x, 1:2, :] = col_sum(all_grads[:, 384:576].astype(F32))
        grad_one[...] += dot_rt(all_grads, w1[along_x, :, 0:576])
        both = jnp.concatenate(
            [dot_lt(normed[...], all_grads), dot_lt(grad_attn[...], att[along_x])], axis=1
        )
        put_blocks(tab, group, both, out)
        return carry

    lax.fori_loop(0, 2, step, 0)


def back_sib_kernel(
    imgs, tab, w1, normed, qkv, soft, att, grad_attn, out, grad_one, bias_sums, gqkv
):
    grad_one[...] = jnp.zeros_like(grad_one)
    back_groups(
        imgs, tab, 1, w1, normed, qkv, soft, att, grad_attn, out, grad_one, gqkv, bias_sums
    )


def back_own_kernel(
    imgs, tab, w1, normed, qkv, soft, att, grad_attn, grad_one_in, out, grad_one, bias_sums, gqkv
):
    grad_one[...] = grad_one_in[...]
    back_groups(
        imgs, tab, 0, w1, normed, qkv, soft, att, grad_attn, out, grad_one, gqkv, bias_sums
    )


def start_kernel(
    tab, tok, rep, vec, grad_one, bias_sib, bias_own, grad_mid, sums_in, units_sib, units_own,
    tok_grad, sums,
):
    replaced = rep[...]
    unit, rstd = norm_stats(mask_rows(tok, rep, vec))
    grad = grad_one[...]
    sums[0:16, :] = sums_in[...]
    sums[16:24, :] = jnp.zeros((8, D), F32)
    sums[0:1, :] = col_sum(grad * unit)
    sums[1:2, :] = col_sum(grad)
    grad_start = grad_mid[...] + norm_back(grad, vec[0:1, :], unit, rstd)
    tok_grad[...] = cut_rows(grad_start * (1.0 - replaced))
    sums[6:7, :] = col_sum(grad_start * replaced)
    for group in range(GROUPS):
        cols = slice(group * GROUP_COLS, (group + 1) * GROUP_COLS)
        own = tab[72] == group % 2
        along_x = group // 2
        both = jnp.where(own, bias_own[along_x], bias_sib[along_x])
        sums[9:10, cols] = both[0:1]
        sums[10:11, cols] = both[1:2]
        sums[16 + group : 17 + group, :] = jnp.where(own, units_own[along_x], units_sib[along_x])


def adam_update(weight, gradient, first_moment, second, step_rate, decay_rate):
    moment = BETA_ONE * first_moment + (1.0 - BETA_ONE) * gradient
    square = BETA_TWO * second + (1.0 - BETA_TWO) * gradient * gradient
    first_hat = moment / (1.0 - BETA_ONE**STEP)
    second_hat = square / (1.0 - BETA_TWO**STEP)
    updated = weight - step_rate * (
        first_hat / (jnp.sqrt(second_hat) + EPSILON) + decay_rate * weight
    )
    return (updated, moment, square)


def finish_kernel(
    partial, last, qkv, first_qkv, second_qkv, out, first_out, second_out, *results
):
    grad = partial[...] + last[...].astype(F32)
    for index in range(3):
        cols = slice(index * GROUP_COLS, (index + 1) * GROUP_COLS)
        found = adam_update(
            qkv[index], grad[:, cols], first_qkv[index], second_qkv[index], RATE_MATRIX, DECAY
        )
        for result, values in zip(results[:3], found, strict=True):
            result[index] = values
    found = adam_update(
        out[...], grad[:, 576:768].T, first_out[...], second_out[...], RATE_MATRIX, DECAY
    )
    for result, values in zip(results[3:], found, strict=True):
        result[...] = values


VMEM = pl.BlockSpec(memory_space=pltpu.VMEM)
SMEM = pl.BlockSpec(memory_space=pltpu.SMEM)


def shape(dims, dtype=BF16):
    return jax.ShapeDtypeStruct(dims, dtype)


def call(kernel, args, outs, scratch=(), flops=SHORT, megabytes=10, table=True):
    return pl.pallas_call(
        kernel,
        out_shape=outs,
        in_specs=[SMEM] * table + [VMEM] * (len(args) - table),
        out_specs=[VMEM] * len(outs),
        scratch_shapes=list(scratch),
        cost_estimate=pl.CostEstimate(flops=flops, bytes_accessed=1, transcendentals=0),
        compiler_params=pltpu.CompilerParams(vmem_limit_bytes=megabytes << 20),
    )(*args)


def after(value, *earlier):
    return lax.optimization_barrier((value, earlier))[0]


def fence(*earlier):
    mark = after(jnp.zeros((8, 128), F32), *earlier)
    return call(fence_kernel, (mark,), (shape((8, 128), F32),), flops=LONG, table=False)[0]


def add_across(values, *masks):
    for mask in masks:
        pairs = [(dev, dev ^ mask) for dev in range(32)]
        values = values + lax.ppermute(values, AXES, pairs)
    return values


def send_all(values, one, two):
    return [
        lax.ppermute(values, AXES, [(dev, dev ^ mask) for dev in range(32)])
        for mask in (one, two, one ^ two)
    ]


def take_all(values, parts):
    return (values + parts[0]) + (parts[1] + parts[2])


class Gather:
    def __init__(self, block, orders):
        self.held = block[None]
        self.orders = orders
        self.level = 0

    def send(self, values, level):
        return lax.ppermute(values, AXES, pairs_of(self.orders, level))

    def start(self, *earlier):
        if earlier:
            self.held = after(self.held, *earlier)
        if self.level < 3:
            self.taken = self.send(self.held, self.level)
            if self.level == 2:
                self.far = self.send(self.held, 3)
        else:
            self.last = self.send(self.held, 3)
        self.level += 1

    def take(self):
        if self.level < 3:
            self.held = jnp.concatenate([self.held, self.taken], axis=0)
            return self.taken
        if self.level == 3:
            self.near = self.held
            self.held = self.taken
            return self.taken, self.far
        return self.last

    def finish(self, *earlier):
        while self.level < 4:
            self.taken = after(self.taken, *earlier)
            self.take()
            self.start()

    def own(self):
        return self.near, self.taken, self.far, self.last

    def sib(self, *earlier):
        own = self.near, self.taken, self.far, after(self.last, *earlier)
        return tuple(lax.ppermute(values, AXES, CORE_PAIRS) for values in own)


class Scatter:
    def __init__(self, orders):
        self.orders = orders
        self.level = 4
        self.terms = []

    def swap(self, sib):
        self.terms.append(lax.ppermute(sib, AXES, CORE_PAIRS))

    def add(self, own):
        self.terms.insert(0, own)

    def total(self, low, high):
        return sum(term[low:high].astype(F32) for term in self.terms)

    def step(self, *earlier):
        self.level -= 1
        size = 1 << self.level
        if earlier:
            self.terms[-1] = after(self.terms[-1], *earlier)
        sent = self.total(size, 2 * size).astype(BF16)
        self.terms.append(lax.ppermute(sent, AXES, pairs_of(self.orders, self.level)))
        return sent

    def hold(self, *earlier):
        self.terms[-1] = after(self.terms[-1], *earlier)

    def result(self):
        return self.total(0, 1)[0]


def gather_plain(block):
    whole = lax.all_gather(block, AXES, axis=0, tiled=False)
    whole = whole.reshape(-1, GROUPS, *block.shape).transpose(1, 0, 2, 3)
    whole = whole.reshape(2, 2, BLOCKS, BLOCK_ROWS, D).transpose(1, 0, 2, 3, 4)
    whole = whole.reshape(2, 4, 4, BLOCK_ROWS, D)
    return tuple(tuple(part[index] for index in range(4)) for part in whole)


def scatter_plain(own, sib, n_dp):
    parts = jnp.stack([own, sib]).reshape(2, BLOCKS, 2, BLOCK_ROWS, D)
    whole = parts.transpose(1, 3, 2, 0, 4).reshape(D, GROUPS, D).astype(F32)
    whole = whole.reshape(n_dp, D // n_dp, GROUPS, D).transpose(0, 2, 1, 3)
    whole = whole.reshape(n_dp * GROUPS, D // n_dp, D)
    return lax.psum_scatter(whole, AXES, scatter_dimension=0, tiled=True)[0]


def on_device(
    n_dp,
    tokens,
    patch_mask,
    cotangent,
    project_qkv,
    first_qkv,
    second_qkv,
    project_out,
    first_out,
    second_out,
    expand_weight,
    first_expand,
    second_expand,
    reduce_weight,
    first_reduce,
    second_reduce,
    vectors,
    first_vectors,
    second_vectors,
    expand_bias,
    first_bias,
    second_bias,
):
    direct = n_dp == BLOCKS
    imgs = patch_mask.shape[0]
    rows = imgs * PAD
    wide = vectors.shape[1]
    units = expand_bias.shape[0]

    def padded(values):
        values = values.reshape(imgs, SEQ, -1)
        return jnp.pad(values, ((0, 0), (0, PAD - SEQ), (0, 0))).reshape(rows, -1)

    positions = lax.broadcasted_iota(jnp.int32, patch_mask.shape, 1)
    replaced = jnp.where((patch_mask == 1) & (positions > 0), 1.0, 0.0).astype(F32)
    rep = padded(replaced)

    def pad_rows(values):
        return call(pad_kernel, (values,), (shape((rows, D)),), flops=LONG, table=False)[0]

    piece_two = expand_weight.astype(BF16)
    piece_three = reduce_weight.astype(BF16).T
    if direct:
        flat = lax.axis_index("dp") * GROUPS + lax.axis_index("tensor")
        chosen = zip(GATHER, (SCATTER[0], SCATTER[2], SCATTER[1]), strict=True)
        every = np.concatenate([build_table(g, s) for g, s in chosen], axis=1)
        table = lax.dynamic_index_in_dim(jnp.asarray(every), flat, 0, keepdims=False)
        tables = [table[0:80], table[80:160], table[160:240]]
        (piece_one,) = call(
            pack_kernel,
            (project_qkv, project_out, vectors, expand_bias[None]),
            (shape((BLOCK_ROWS + EXTRA, D)),),
            table=False,
        )
        streams = [
            Gather(piece, orders)
            for piece, orders in zip((piece_one, piece_two, piece_three), GATHER, strict=True)
        ]
        seen = {}
        for kind, index in zip(STEPS[0::2], STEPS[1::2], strict=True):
            stream = streams[int(index)]
            held = [stream.held for stream in streams]
            if kind == "X":
                seen["mark"] = fence(*held, *seen.values())
            elif kind == "F":
                if index == "0":
                    tok = pad_rows(after(tokens, *held))
                    seen["tok"] = (tok, rep, *tables)
                else:
                    cot = pad_rows(after(cotangent, *held))
                    seen["cot"] = cot
            elif kind == "S":
                stream.start(*seen.values())
            else:
                seen[index] = stream.take()
        marks = [seen[name] for name in seen if name not in "12"]
        w1_own, w1_sib = streams[0].own(), streams[0].sib(*marks)
    else:
        tables = [jnp.asarray(plain_table())] * 3
        tok, cot = pad_rows(tokens), pad_rows(cotangent)
        piece_one = jnp.concatenate(
            [project_qkv[0], project_qkv[1], project_qkv[2], project_out.T], axis=1
        ).astype(BF16)
        w1_parts, (w2_own, w2_sib), (w3_own, w3_sib) = (
            gather_plain(piece) for piece in (piece_one, piece_two, piece_three)
        )
        vector_all = lax.all_gather(vectors.astype(BF16), "dp", axis=1, tiled=True)
        bias_all = lax.all_gather(expand_bias.astype(BF16), "dp", axis=0, tiled=True)
        by_block = vector_all.reshape(11, BLOCKS, BLOCK_ROWS).transpose(1, 0, 2)
        extras = jnp.zeros((BLOCKS, EXTRA, D), BF16)
        extras = extras.at[:, :, 0:BLOCK_ROWS].set(by_block[:, 0:8])
        extras = extras.at[:, 0:3, 128 : 128 + BLOCK_ROWS].set(by_block[:, 8:11])
        extras = extras.at[:, 0, 256:640].set(bias_all.reshape(BLOCKS, FF // BLOCKS))
        w1_own, w1_sib = (
            tuple(
                jnp.concatenate([part, extras[4 * (at % 2) : 4 * (at % 2) + 4]], axis=1)
                for at, part in enumerate(parts)
            )
            for parts in w1_parts
        )

    full = (GROUPS, D, D)
    row_f32 = shape((rows, D), F32)
    row_low = shape((rows, D))
    half = shape((16, BLOCK_ROWS, D))
    two_low = shape((2, rows, D))
    two_f32 = shape((2, rows, D), F32)
    two_bias = shape((2, 1, D), F32)
    group_bias = shape((GROUPS, 1, GROUP_COLS), F32)
    weights = shape((2, D, D))
    heads = (
        shape((2, rows, 3 * GROUP_COLS)),
        shape((2 * HEADS_IN_GROUP * imgs, PAD, PAD), F32),
        shape((2, rows, GROUP_COLS)),
        row_f32,
    )
    vec, bias, start_rows, normed, qb, vb, w1_own, *heads_own, attn = call(
        functools.partial(attend_own_kernel, imgs),
        (tables[0], tok, rep, *w1_own),
        (
            shape((16, D), F32), shape((GROUPS, 1, D), F32), row_f32, row_low,
            group_bias, group_bias, weights, *heads,
        ),
        flops=SHORT,
    )
    w1_sib, *heads_sib, attn, mid, normed_two = call(
        functools.partial(attend_sib_kernel, imgs),
        (tables[0], vec, start_rows, normed, qb, vb, attn, *w1_sib),
        (weights, *heads, row_f32, row_low),
        flops=SHORT,
    )
    if direct:
        streams[1].finish(normed)
        w2_own, w2_sib = streams[1].own(), streams[1].sib(normed_two)
    three, two, one = (Scatter(SCATTER[index]) for index in (2, 1, 0))
    w2_own, act_own, slope_own, grad_branch, reduce_own = call(
        expand_own_kernel,
        (tables[1], normed_two, cot, vec, bias, *w2_own),
        (weights, two_low, two_f32, row_low, half),
        flops=LONG,
    )
    if direct:
        streams[2].finish(grad_branch)
    w2_sib, act_sib, slope_sib, reduce_sib = call(
        expand_sib_kernel,
        (tables[1], normed_two, grad_branch, bias, *w2_sib),
        (weights, two_low, two_f32, half),
        flops=SHORT,
    )
    if direct:
        three.swap(reduce_sib)
        w3_own, w3_sib = streams[2].own(), streams[2].sib(reduce_sib)
    w3_sib, hid_sib, units_sib, expand_sib = call(
        functools.partial(hidden_kernel, 1),
        (tables[2], normed_two, grad_branch, slope_sib, *w3_sib),
        (weights, two_low, two_bias, half),
        flops=LONG,
    )
    if direct:
        two.swap(expand_sib)
        three.add(reduce_own)
        slope_own = after(slope_own, three.step(expand_sib))
    w3_own, hid_own, units_own, expand_own = call(
        functools.partial(hidden_kernel, 0),
        (tables[2], normed_two, grad_branch, slope_own, *w3_own),
        (weights, two_low, two_bias, half),
        flops=LONG,
    )
    if direct:
        two.add(expand_own)
        mid = after(mid, two.step())
    block_out, grad_mid, grad_attn, sums = call(
        middle_kernel,
        (
            act_sib, act_own, hid_sib, hid_own, w2_sib, w2_own, w3_sib, w3_own,
            mid, attn, cot, vec,
        ),
        (shape(tokens.shape), row_f32, row_low, shape((16, D), F32)),
        (pltpu.VMEM((rows, D), F32), pltpu.VMEM((rows, D), F32)),
        flops=SHORT,
        table=False,
    )
    held = pltpu.VMEM((rows, 3 * GROUP_COLS), BF16)
    bias_sums = (2, 2, GROUP_COLS)
    first_sib, grad_one, bias_sib = call(
        functools.partial(back_sib_kernel, imgs),
        (tables[0], w1_sib, normed, *heads_sib, grad_attn),
        (half, row_f32, shape(bias_sums, F32)),
        (held,),
        flops=SHORT,
    )
    if direct:
        one.swap(first_sib)
        grad_one = after(grad_one, three.step(grad_one))
    first_own, grad_one, bias_own = call(
        functools.partial(back_own_kernel, imgs),
        (tables[0], w1_own, normed, *heads_own, grad_attn, grad_one),
        (half, row_f32, shape(bias_sums, F32)),
        (held,),
        flops=LONG,
    )
    if direct:
        first_own, grad_one = after((first_own, grad_one), three.terms[-1])
        one.add(first_own)
        sent = one.step()
        sent_three, sent_two = three.step(sent), two.step(sent)
        grad_one = after(grad_one, sent)
    tok_grad, sums = call(
        start_kernel,
        (
            tables[0], tok, rep, vec, grad_one, bias_sib, bias_own, grad_mid, sums,
            units_sib, units_own,
        ),
        (shape(tokens.shape), shape((24, D), F32)),
    )

    if direct:
        sums = add_across(sums, 1)
        one.hold(fence(sums, sent_three, sent_two))
        parts = send_all(sums, 8, 16)
        sent = one.step()
        mark = sent
        sums = take_all(sums, after(parts, mark))
        three.step(mark)
        two.step(mark)
        sent = one.step()
        mark = sent
        parts = send_all(after(sums, mark), 2, 4)
        three.hold(mark)
        two.step(mark)
        sent = one.step()
        sums = take_all(sums, after(parts, sent))
        grad_three = three.result()
        states_three = adam_update(
            reduce_weight, grad_three.T, first_reduce, second_reduce, RATE_MATRIX, DECAY
        )
        two.hold(sent)
        grad_two = two.result()
        partial = sum(term[0].astype(F32) for term in one.terms[:-1])
        finished = call(
            finish_kernel,
            (
                partial, one.terms[-1][0], project_qkv, first_qkv, second_qkv,
                project_out, first_out, second_out,
            ),
            (shape(project_qkv.shape, F32),) * 3 + (shape(project_out.shape, F32),) * 3,
            table=False,
        )
    else:
        grad_three = scatter_plain(reduce_own, reduce_sib, n_dp)
        grad_two = scatter_plain(expand_own, expand_sib, n_dp)
        grad_one = scatter_plain(first_own, first_sib, n_dp)
        sums = lax.psum(sums, AXES)
        grad_qkv = jnp.stack([grad_one[:, i * GROUP_COLS : (i + 1) * GROUP_COLS] for i in range(3)])
        grad_out = grad_one[:, 3 * GROUP_COLS :].T
        states_three = adam_update(
            reduce_weight, grad_three.T, first_reduce, second_reduce, RATE_MATRIX, DECAY
        )
        finished = (
            *adam_update(project_qkv, grad_qkv, first_qkv, second_qkv, RATE_MATRIX, DECAY),
            *adam_update(project_out, grad_out, first_out, second_out, RATE_MATRIX, DECAY),
        )
    spot = lax.axis_index("dp")
    vector_grad = lax.dynamic_slice_in_dim(sums[0:11], spot * wide, wide, 1)
    grad_bias = lax.dynamic_slice_in_dim(sums[16:20].reshape(-1), spot * units, units, 0)
    return (
        block_out,
        tok_grad,
        *finished,
        *adam_update(expand_weight, grad_two, first_expand, second_expand, RATE_MATRIX, DECAY),
        *states_three,
        *adam_update(vectors, vector_grad, first_vectors, second_vectors, RATE_VECTOR, 0.0),
        *adam_update(expand_bias, grad_bias, first_bias, second_bias, RATE_VECTOR, 0.0),
    )


def solution(mesh):
    rows = P(AXES, None)
    states = (
        *(P(None, "dp", "tensor"),) * 3,
        *(P("tensor", "dp"),) * 3,
        *(P("dp", "tensor"),) * 3,
        *(P("tensor", "dp"),) * 3,
        *(P(None, "dp"),) * 3,
        *(P("dp"),) * 3,
    )
    return jax.shard_map(
        functools.partial(on_device, mesh.shape["dp"]),
        mesh=mesh,
        in_specs=(rows, rows, rows, *states),
        out_specs=(rows, rows, *states),
        check_vma=False,
    )
```

```python
import functools

import jax
import jax.numpy as jnp
import numpy as np
from jax import lax
from jax.experimental import pallas as pl
from jax.experimental.pallas import tpu as pltpu
from jax.sharding import PartitionSpec as P

D = 768
HEAD_DIM = 64
FF = 3072
SEQ = 197
STEP = 4
BETA_ONE = 0.5
BETA_TWO = 0.5
EPSILON = 1e-08
DECAY = 0.05
RATE_MATRIX = 0.02
RATE_VECTOR = 0.2
NORM_EPS = 1e-06

AXES = ("dp", "tensor")
PAD = 208
GROUPS = 4
GROUP_COLS = D // GROUPS
HEADS_IN_GROUP = GROUP_COLS // HEAD_DIM
BLOCKS = 8
BLOCK_ROWS = D // BLOCKS
EXTRA = 8
SCALE = HEAD_DIM**-0.5
SHORT = 1
LONG = 10**11
F32 = jnp.float32
BF16 = jnp.bfloat16

BIT = {"c": 1, "x": 2, "y": 4, "1": 8, "2": 16}
GATHER = (("21xy", "12yx"), ("2y1x", "yx21"), ("y21x", "1x2y"))
SCATTER = (("21yx", "12xy"), ("2x1y", "x21y"), ("y2x1", "y21x"))
STEPS = "S0S1S2D0S0D1S1D0S0D2S2F0D1S1D0S0D2S2D1S1F1D0"


def offset_of(order, place):
    found = 0
    for level in range(4):
        if place >> level & 1:
            found ^= BIT[order[level]]
    return found


def pairs_of(orders, level):
    return [(dev, dev ^ BIT[orders[dev & 1][level]]) for dev in range(32)]


CORE_PAIRS = [(dev, dev ^ 1) for dev in range(32)]


def build_table(gather, scatter):
    table = np.zeros((32, 80), np.int32)
    for dev in range(32):
        core = dev & 1
        for place in range(16):
            table[dev, place] = dev ^ offset_of(gather[core], place)
            table[dev, 16 + place] = dev ^ 1 ^ offset_of(gather[1 - core], place)
            mine = dev ^ offset_of(gather[core], place)
            if mine & 3 == dev & 3:
                table[dev, 32 + (mine >> 2)] = place
            table[dev, 40 + (dev ^ offset_of(scatter[core], place))] = place
            table[dev, 40 + (dev ^ 1 ^ offset_of(scatter[1 - core], place))] = place
        table[dev, 72] = core
    return table


def plain_table():
    table = np.zeros((80,), np.int32)
    for place in range(32):
        part, along_x, block = place // 16, place // 8 % 2, place % 8
        table[place] = block * 4 + along_x * 2 + part
    for block in range(8):
        table[32 + block] = block
        for group in range(4):
            table[40 + block * 4 + group] = block * 2 + group // 2
    return table


def dot(left, right):
    return jnp.dot(left, right, preferred_element_type=F32)


def dot_rt(left, right):
    return lax.dot_general(left, right, (((1,), (1,)), ((), ())), preferred_element_type=F32)


def dot_lt(left, right):
    return lax.dot_general(left, right, (((0,), (0,)), ((), ())), preferred_element_type=F32)


def norm_stats(values):
    mean = jnp.mean(values, axis=-1, keepdims=True)
    centred = values - mean
    var = jnp.mean(centred * centred, axis=-1, keepdims=True)
    rstd = lax.rsqrt(var + NORM_EPS)
    return centred * rstd, rstd


def norm_back(grad, gain, unit, rstd):
    grad_unit = grad * gain
    first = jnp.mean(grad_unit, axis=-1, keepdims=True)
    second = jnp.mean(grad_unit * unit, axis=-1, keepdims=True)
    return rstd * (grad_unit - first - unit * second)


def col_sum(values):
    return jnp.sum(values, axis=0, keepdims=True)


def assemble(tab, first, parts, whole):
    for index, part in enumerate(parts):
        for place in range(4):
            owner = tab[first + index * 4 + place]
            row = pl.multiple_of((owner >> 2) * BLOCK_ROWS, BLOCK_ROWS)
            whole[(owner >> 1) & 1, pl.ds(row, BLOCK_ROWS), :] = part[place, 0:BLOCK_ROWS, :]


def put_blocks(tab, group, grad, out):
    for block in range(BLOCKS):
        place = tab[40 + block * 4 + group]
        rows = slice(block * BLOCK_ROWS, (block + 1) * BLOCK_ROWS)
        out[place] = grad[rows].astype(BF16)


def mask_rows(tok, rep, vec):
    replaced = rep[...]
    return tok[...].astype(F32) * (1.0 - replaced) + vec[6:7, :] * replaced


def pad_kernel(values, out):
    wide = values[...].astype(F32)
    gap = jnp.zeros((PAD - SEQ, D), F32)
    rows = []
    for start in range(0, wide.shape[0], SEQ):
        rows += [wide[start : start + SEQ], gap]
    out[...] = jnp.concatenate(rows, axis=0).astype(BF16)


def cut_rows(wide):
    rows = [wide[start : start + SEQ] for start in range(0, wide.shape[0], PAD)]
    return jnp.concatenate(rows, axis=0).astype(BF16)


def fence_kernel(values, out):
    out[...] = values[...] + 1.0


def pack_kernel(project_qkv, project_out, vectors, expand_bias, out):
    columns = [project_qkv[0], project_qkv[1], project_qkv[2], project_out[...].T]
    block = jnp.concatenate(columns, axis=1)
    fill = jnp.zeros((EXTRA, 128 - BLOCK_ROWS), F32)
    low = jnp.concatenate([vectors[0:8, :], fill], axis=1)
    high = jnp.concatenate([vectors[8:11, :], jnp.zeros((5, BLOCK_ROWS), F32)], axis=0)
    high = jnp.concatenate([high, fill], axis=1)
    last = jnp.concatenate([expand_bias[...], jnp.zeros((EXTRA - 1, 384), F32)], axis=0)
    extra = jnp.concatenate([low, high, last, jnp.zeros((EXTRA, 128), F32)], axis=1)
    out[...] = jnp.concatenate([block, extra], axis=0).astype(BF16)


def attend_groups(imgs, tab, part, normed, qb, vb, w1, qkv, soft, att, attn):
    keep = lax.broadcasted_iota(jnp.int32, (PAD, PAD), 1) < SEQ

    def step(along_x, carry):
        group = along_x * 2 + (tab[72] ^ part)
        result = dot(normed[...], w1[along_x, :, 0:576])
        qkv[along_x, :, 0:192] = (result[:, 0:192] + qb[group, 0:1, :]).astype(BF16)
        qkv[along_x, :, 192:384] = result[:, 192:384].astype(BF16)
        qkv[along_x, :, 384:576] = (result[:, 384:576] + vb[group, 0:1, :]).astype(BF16)
        for head in range(HEADS_IN_GROUP):
            c0 = head * HEAD_DIM
            for img in range(imgs):
                rows = slice(img * PAD, (img + 1) * PAD)
                q = qkv[along_x, rows, c0 : c0 + 64]
                k = qkv[along_x, rows, 192 + c0 : 256 + c0]
                v = qkv[along_x, rows, 384 + c0 : 448 + c0]
                scores = jnp.where(keep, dot_rt(q, k) * SCALE, -1e30)
                top = jnp.max(scores, axis=-1, keepdims=True)
                raised = jnp.exp(scores - top)
                weights = raised / jnp.sum(raised, axis=-1, keepdims=True)
                soft[along_x * (HEADS_IN_GROUP * imgs) + head * imgs + img] = weights
                att[along_x, rows, c0 : c0 + 64] = dot(weights.astype(BF16), v).astype(BF16)
        attn[...] += dot_rt(att[along_x], w1[along_x, :, 576:768])
        return carry

    lax.fori_loop(0, 2, step, 0)


def attend_own_kernel(
    imgs, tab, tok, rep, b0, b1, b2, b3,
    vec, bias, start_rows, normed, qb, vb, w1, qkv, soft, att, attn,
):
    low = jnp.zeros((8, D), F32)
    high = jnp.zeros((8, D), F32)
    fill = jnp.zeros((8, D - 128), F32)
    for block in range(BLOCKS):
        place = tab[32 + block]
        piece = jnp.zeros((EXTRA, D), F32)
        for index, part in enumerate((b0, b1, b2, b3)):
            rows = part[place & 3].astype(F32)[BLOCK_ROWS:]
            piece = jnp.where(place >> 2 == index, rows, piece)
        low += pltpu.roll(jnp.concatenate([piece[:, 0:128], fill], 1), block * BLOCK_ROWS, 1)
        high += pltpu.roll(jnp.concatenate([piece[:, 128:256], fill], 1), block * BLOCK_ROWS, 1)
        half = (block % 2) * 384
        bias[block // 2, 0:1, half : half + 384] = piece[0:1, 256:640]
    vec[0:8, :] = low
    vec[8:16, :] = high
    for group in range(GROUPS):
        cols = slice(group * GROUP_COLS, (group + 1) * GROUP_COLS)
        qb[group, 0:1, :] = vec[9:10, cols]
        vb[group, 0:1, :] = vec[10:11, cols]
    assemble(tab, 0, (b0, b1, b2, b3), w1)
    start = mask_rows(tok, rep, vec)
    start_rows[...] = start
    unit, _ = norm_stats(start)
    normed[...] = (unit * vec[0:1, :] + vec[1:2, :]).astype(BF16)
    attn[...] = jnp.zeros_like(attn)
    attend_groups(imgs, tab, 0, normed, qb, vb, w1, qkv, soft, att, attn)


def attend_sib_kernel(
    imgs, tab, vec, start_rows, normed, qb, vb, attn_in, b0, b1, b2, b3,
    w1, qkv, soft, att, attn, mid, normed_two,
):
    assemble(tab, 16, (b0, b1, b2, b3), w1)
    attn[...] = attn_in[...]
    attend_groups(imgs, tab, 1, normed, qb, vb, w1, qkv, soft, att, attn)
    middle = start_rows[...] + vec[4:5, :] * (attn[...] + vec[7:8, :])
    mid[...] = middle
    unit_two, _ = norm_stats(middle)
    normed_two[...] = (unit_two * vec[2:3, :] + vec[3:4, :]).astype(BF16)


def expand_groups(tab, part, normed_two, grad_branch, bias, w2, active, slope, out):
    def step(along_x, carry):
        group = along_x * 2 + (tab[72] ^ part)
        hidden = dot(normed_two[...], w2[along_x]) + bias[group, 0:1, :]
        cdf = 0.5 * (1.0 + lax.erf(hidden * 0.7071067811865476))
        pdf = 0.3989422804014327 * jnp.exp(-0.5 * hidden * hidden)
        act = (hidden * cdf).astype(BF16)
        active[along_x] = act
        slope[along_x] = cdf + hidden * pdf
        put_blocks(tab, group, dot_lt(grad_branch[...], act), out)
        return carry

    lax.fori_loop(0, 2, step, 0)


def expand_own_kernel(
    tab, normed_two, cot, vec, bias, b0, b1, b2, b3, w2, active, slope, grad_branch, out
):
    assemble(tab, 0, (b0, b1, b2, b3), w2)
    grad_branch[...] = (cot[...].astype(F32) * vec[5:6, :]).astype(BF16)
    expand_groups(tab, 0, normed_two, grad_branch, bias, w2, active, slope, out)


def expand_sib_kernel(
    tab, normed_two, grad_branch, bias, b0, b1, b2, b3, w2, active, slope, out
):
    assemble(tab, 16, (b0, b1, b2, b3), w2)
    expand_groups(tab, 1, normed_two, grad_branch, bias, w2, active, slope, out)


def hidden_groups(tab, part, normed_two, grad_branch, slope, w3, grad_hidden, bias_grad, out):
    def step(along_x, carry):
        group = along_x * 2 + (tab[72] ^ part)
        grad = (dot(grad_branch[...], w3[along_x]) * slope[along_x]).astype(BF16)
        grad_hidden[along_x] = grad
        bias_grad[along_x, 0:1, :] = col_sum(grad.astype(F32))
        put_blocks(tab, group, dot_lt(normed_two[...], grad), out)
        return carry

    lax.fori_loop(0, 2, step, 0)


def hidden_kernel(
    part, tab, normed_two, grad_branch, slope, b0, b1, b2, b3, w3, grad_hidden, bias_grad, out
):
    assemble(tab, 16 * part, (b0, b1, b2, b3), w3)
    hidden_groups(tab, part, normed_two, grad_branch, slope, w3, grad_hidden, bias_grad, out)


def middle_kernel(
    act_sib, act_own, hid_sib, hid_own, w2_sib, w2_own, w3_sib, w3_own, mid, attn, cot, vec,
    block_out, grad_mid, grad_attn, sums, branch, grad_two,
):
    sums[...] = jnp.zeros_like(sums)
    found = jnp.zeros(branch.shape, F32)
    for active, w3 in ((act_sib, w3_sib), (act_own, w3_own)):
        for along_x in range(2):
            found += dot_rt(active[along_x], w3[along_x])
    branch[...] = found
    found = jnp.zeros(branch.shape, F32)
    for grad_hidden, w2 in ((hid_sib, w2_sib), (hid_own, w2_own)):
        for along_x in range(2):
            found += dot_rt(grad_hidden[along_x], w2[along_x])
    grad_two[...] = found
    middle = mid[...]
    total = branch[...] + vec[8:9, :]
    block_out[...] = cut_rows(middle + vec[5:6, :] * total)
    grad_out = cot[...].astype(F32)
    sums[5:6, :] = col_sum(grad_out * total)
    sums[8:9, :] = col_sum(grad_out * vec[5:6, :])
    unit, rstd = norm_stats(middle)
    grad = grad_two[...]
    sums[2:3, :] = col_sum(grad * unit)
    sums[3:4, :] = col_sum(grad)
    grad_middle = grad_out + norm_back(grad, vec[2:3, :], unit, rstd)
    grad_mid[...] = grad_middle
    sums[4:5, :] = col_sum(grad_middle * (attn[...] + vec[7:8, :]))
    scaled = grad_middle * vec[4:5, :]
    sums[7:8, :] = col_sum(scaled)
    grad_attn[...] = scaled.astype(BF16)


def back_groups(
    imgs, tab, part, w1, normed, qkv, soft, att, grad_attn, out, grad_one, gqkv, bias_sums
):
    def step(along_x, carry):
        group = along_x * 2 + (tab[72] ^ part)
        grad_att = dot(grad_attn[...], w1[along_x, :, 576:768]).astype(BF16)
        for head in range(HEADS_IN_GROUP):
            c0 = head * HEAD_DIM
            for img in range(imgs):
                rows = slice(img * PAD, (img + 1) * PAD)
                q = qkv[along_x, rows, c0 : c0 + 64]
                k = qkv[along_x, rows, 192 + c0 : 256 + c0]
                v = qkv[along_x, rows, 384 + c0 : 448 + c0]
                weights = soft[along_x * (HEADS_IN_GROUP * imgs) + head * imgs + img]
                grad = grad_att[rows, c0 : c0 + 64]
                grad_soft = dot_rt(grad, v)
                grad_v = dot_lt(weights.astype(BF16), grad)
                inner = jnp.sum(weights * grad_soft, axis=-1, keepdims=True)
                grad_scores = (weights * (grad_soft - inner)).astype(BF16)
                grad_q = dot(grad_scores, k) * SCALE
                grad_k = dot_lt(grad_scores, q) * SCALE
                gqkv[rows, c0 : c0 + 64] = grad_q.astype(BF16)
                gqkv[rows, 192 + c0 : 256 + c0] = grad_k.astype(BF16)
                gqkv[rows, 384 + c0 : 448 + c0] = grad_v.astype(BF16)
        all_grads = gqkv[...]
        bias_sums[along_x, 0:1, :] = col_sum(all_grads[:, 0:192].astype(F32))
        bias_sums[along_x, 1:2, :] = col_sum(all_grads[:, 384:576].astype(F32))
        grad_one[...] += dot_rt(all_grads, w1[along_x, :, 0:576])
        both = jnp.concatenate(
            [dot_lt(normed[...], all_grads), dot_lt(grad_attn[...], att[along_x])], axis=1
        )
        put_blocks(tab, group, both, out)
        return carry

    lax.fori_loop(0, 2, step, 0)


def back_sib_kernel(
    imgs, tab, w1, normed, qkv, soft, att, grad_attn, out, grad_one, bias_sums, gqkv
):
    grad_one[...] = jnp.zeros_like(grad_one)
    back_groups(
        imgs, tab, 1, w1, normed, qkv, soft, att, grad_attn, out, grad_one, gqkv, bias_sums
    )


def back_own_kernel(
    imgs, tab, w1, normed, qkv, soft, att, grad_attn, grad_one_in, out, grad_one, bias_sums, gqkv
):
    grad_one[...] = grad_one_in[...]
    back_groups(
        imgs, tab, 0, w1, normed, qkv, soft, att, grad_attn, out, grad_one, gqkv, bias_sums
    )


def start_kernel(
    tab, tok, rep, vec, grad_one, bias_sib, bias_own, grad_mid, sums_in, units_sib, units_own,
    tok_grad, sums,
):
    replaced = rep[...]
    unit, rstd = norm_stats(mask_rows(tok, rep, vec))
    grad = grad_one[...]
    sums[0:16, :] = sums_in[...]
    sums[16:24, :] = jnp.zeros((8, D), F32)
    sums[0:1, :] = col_sum(grad * unit)
    sums[1:2, :] = col_sum(grad)
    grad_start = grad_mid[...] + norm_back(grad, vec[0:1, :], unit, rstd)
    tok_grad[...] = cut_rows(grad_start * (1.0 - replaced))
    sums[6:7, :] = col_sum(grad_start * replaced)
    for group in range(GROUPS):
        cols = slice(group * GROUP_COLS, (group + 1) * GROUP_COLS)
        own = tab[72] == group % 2
        along_x = group // 2
        both = jnp.where(own, bias_own[along_x], bias_sib[along_x])
        sums[9:10, cols] = both[0:1]
        sums[10:11, cols] = both[1:2]
        sums[16 + group : 17 + group, :] = jnp.where(own, units_own[along_x], units_sib[along_x])


def adam_update(weight, gradient, first_moment, second, step_rate, decay_rate):
    moment = BETA_ONE * first_moment + (1.0 - BETA_ONE) * gradient
    square = BETA_TWO * second + (1.0 - BETA_TWO) * gradient * gradient
    first_hat = moment / (1.0 - BETA_ONE**STEP)
    second_hat = square / (1.0 - BETA_TWO**STEP)
    updated = weight - step_rate * (
        first_hat / (jnp.sqrt(second_hat) + EPSILON) + decay_rate * weight
    )
    return (updated, moment, square)


def finish_kernel(
    partial, last, qkv, first_qkv, second_qkv, out, first_out, second_out, *results
):
    grad = partial[...] + last[...].astype(F32)
    for index in range(3):
        cols = slice(index * GROUP_COLS, (index + 1) * GROUP_COLS)
        found = adam_update(
            qkv[index], grad[:, cols], first_qkv[index], second_qkv[index], RATE_MATRIX, DECAY
        )
        for result, values in zip(results[:3], found, strict=True):
            result[index] = values
    found = adam_update(
        out[...], grad[:, 576:768].T, first_out[...], second_out[...], RATE_MATRIX, DECAY
    )
    for result, values in zip(results[3:], found, strict=True):
        result[...] = values


VMEM = pl.BlockSpec(memory_space=pltpu.VMEM)
SMEM = pl.BlockSpec(memory_space=pltpu.SMEM)


def shape(dims, dtype=BF16):
    return jax.ShapeDtypeStruct(dims, dtype)


def call(kernel, args, outs, scratch=(), flops=SHORT, megabytes=10, table=True):
    return pl.pallas_call(
        kernel,
        out_shape=outs,
        in_specs=[SMEM] * table + [VMEM] * (len(args) - table),
        out_specs=[VMEM] * len(outs),
        scratch_shapes=list(scratch),
        cost_estimate=pl.CostEstimate(flops=flops, bytes_accessed=1, transcendentals=0),
        compiler_params=pltpu.CompilerParams(vmem_limit_bytes=megabytes << 20),
    )(*args)


def after(value, *earlier):
    return lax.optimization_barrier((value, earlier))[0]


def fence(*earlier):
    mark = after(jnp.zeros((8, 128), F32), *earlier)
    return call(fence_kernel, (mark,), (shape((8, 128), F32),), flops=LONG, table=False)[0]


def send_across(values, mask):
    return lax.ppermute(values, AXES, [(dev, dev ^ mask) for dev in range(32)])


def add_across(values, mask):
    return values + send_across(values, mask)


class Gather:
    def __init__(self, block, orders):
        self.held = block[None]
        self.orders = orders
        self.level = 0

    def send(self, values, level):
        return lax.ppermute(values, AXES, pairs_of(self.orders, level))

    def start(self, *earlier):
        if earlier:
            self.held = after(self.held, *earlier)
        if self.level < 3:
            self.taken = self.send(self.held, self.level)
            if self.level == 2:
                self.far = self.send(self.held, 3)
        else:
            self.last = self.send(self.held, 3)
        self.level += 1

    def take(self):
        if self.level < 3:
            self.held = jnp.concatenate([self.held, self.taken], axis=0)
            return self.taken
        if self.level == 3:
            self.near = self.held
            self.held = self.taken
            return self.taken, self.far
        return self.last

    def finish(self, *earlier):
        while self.level < 4:
            self.taken = after(self.taken, *earlier)
            self.take()
            self.start()

    def own(self):
        return self.near, self.taken, self.far, self.last

    def sib(self, *earlier):
        own = self.near, self.taken, self.far, after(self.last, *earlier)
        return tuple(lax.ppermute(values, AXES, CORE_PAIRS) for values in own)


class Scatter:
    def __init__(self, orders):
        self.orders = orders
        self.level = 4
        self.terms = []

    def swap(self, sib):
        self.terms.append(lax.ppermute(sib, AXES, CORE_PAIRS))

    def add(self, own):
        self.terms.insert(0, own)

    def total(self, low, high):
        return sum(term[low:high].astype(F32) for term in self.terms)

    def step(self, *earlier):
        self.level -= 1
        size = 1 << self.level
        if earlier:
            self.terms[-1] = after(self.terms[-1], *earlier)
        sent = self.total(size, 2 * size).astype(BF16)
        self.terms.append(lax.ppermute(sent, AXES, pairs_of(self.orders, self.level)))
        return sent

    def hold(self, *earlier):
        self.terms[-1] = after(self.terms[-1], *earlier)

    def result(self):
        return self.total(0, 1)[0]


def gather_plain(block):
    whole = lax.all_gather(block, AXES, axis=0, tiled=False)
    whole = whole.reshape(-1, GROUPS, *block.shape).transpose(1, 0, 2, 3)
    whole = whole.reshape(2, 2, BLOCKS, BLOCK_ROWS, D).transpose(1, 0, 2, 3, 4)
    whole = whole.reshape(2, 4, 4, BLOCK_ROWS, D)
    return tuple(tuple(part[index] for index in range(4)) for part in whole)


def scatter_plain(own, sib, n_dp):
    parts = jnp.stack([own, sib]).reshape(2, BLOCKS, 2, BLOCK_ROWS, D)
    whole = parts.transpose(1, 3, 2, 0, 4).reshape(D, GROUPS, D).astype(F32)
    whole = whole.reshape(n_dp, D // n_dp, GROUPS, D).transpose(0, 2, 1, 3)
    whole = whole.reshape(n_dp * GROUPS, D // n_dp, D)
    return lax.psum_scatter(whole, AXES, scatter_dimension=0, tiled=True)[0]


def on_device(
    n_dp,
    tokens,
    patch_mask,
    cotangent,
    project_qkv,
    first_qkv,
    second_qkv,
    project_out,
    first_out,
    second_out,
    expand_weight,
    first_expand,
    second_expand,
    reduce_weight,
    first_reduce,
    second_reduce,
    vectors,
    first_vectors,
    second_vectors,
    expand_bias,
    first_bias,
    second_bias,
):
    direct = n_dp == BLOCKS
    imgs = patch_mask.shape[0]
    rows = imgs * PAD
    wide = vectors.shape[1]
    units = expand_bias.shape[0]

    def padded(values):
        values = values.reshape(imgs, SEQ, -1)
        return jnp.pad(values, ((0, 0), (0, PAD - SEQ), (0, 0))).reshape(rows, -1)

    positions = lax.broadcasted_iota(jnp.int32, patch_mask.shape, 1)
    replaced = jnp.where((patch_mask == 1) & (positions > 0), 1.0, 0.0).astype(F32)
    rep = padded(replaced)

    def pad_rows(values):
        return call(pad_kernel, (values,), (shape((rows, D)),), flops=LONG, table=False)[0]

    piece_two = expand_weight.astype(BF16)
    piece_three = reduce_weight.astype(BF16).T
    if direct:
        flat = lax.axis_index("dp") * GROUPS + lax.axis_index("tensor")
        chosen = zip(GATHER, (SCATTER[0], SCATTER[2], SCATTER[1]), strict=True)
        every = np.concatenate([build_table(g, s) for g, s in chosen], axis=1)
        table = lax.dynamic_index_in_dim(jnp.asarray(every), flat, 0, keepdims=False)
        tables = [table[0:80], table[80:160], table[160:240]]
        (piece_one,) = call(
            pack_kernel,
            (project_qkv, project_out, vectors, expand_bias[None]),
            (shape((BLOCK_ROWS + EXTRA, D)),),
            table=False,
        )
        streams = [
            Gather(piece, orders)
            for piece, orders in zip((piece_one, piece_two, piece_three), GATHER, strict=True)
        ]
        seen = {}
        for kind, index in zip(STEPS[0::2], STEPS[1::2], strict=True):
            stream = streams[int(index)]
            held = [stream.held for stream in streams]
            if kind == "X":
                seen["mark"] = fence(*held, *seen.values())
            elif kind == "F":
                if index == "0":
                    tok = pad_rows(after(tokens, *held[:2]))
                    seen["tok"] = (tok, rep, *tables)
                else:
                    cot = pad_rows(after(cotangent, held[1]))
                    seen["cot"] = cot
            elif kind == "S":
                stream.start(*seen.values())
            else:
                seen[index] = stream.take()
        marks = [seen[name] for name in seen if name not in "12"]
        w1_own, w1_sib = streams[0].own(), streams[0].sib(*marks)
    else:
        tables = [jnp.asarray(plain_table())] * 3
        tok, cot = pad_rows(tokens), pad_rows(cotangent)
        piece_one = jnp.concatenate(
            [project_qkv[0], project_qkv[1], project_qkv[2], project_out.T], axis=1
        ).astype(BF16)
        w1_parts, (w2_own, w2_sib), (w3_own, w3_sib) = (
            gather_plain(piece) for piece in (piece_one, piece_two, piece_three)
        )
        vector_all = lax.all_gather(vectors.astype(BF16), "dp", axis=1, tiled=True)
        bias_all = lax.all_gather(expand_bias.astype(BF16), "dp", axis=0, tiled=True)
        by_block = vector_all.reshape(11, BLOCKS, BLOCK_ROWS).transpose(1, 0, 2)
        extras = jnp.zeros((BLOCKS, EXTRA, D), BF16)
        extras = extras.at[:, :, 0:BLOCK_ROWS].set(by_block[:, 0:8])
        extras = extras.at[:, 0:3, 128 : 128 + BLOCK_ROWS].set(by_block[:, 8:11])
        extras = extras.at[:, 0, 256:640].set(bias_all.reshape(BLOCKS, FF // BLOCKS))
        w1_own, w1_sib = (
            tuple(
                jnp.concatenate([part, extras[4 * (at % 2) : 4 * (at % 2) + 4]], axis=1)
                for at, part in enumerate(parts)
            )
            for parts in w1_parts
        )

    full = (GROUPS, D, D)
    row_f32 = shape((rows, D), F32)
    row_low = shape((rows, D))
    half = shape((16, BLOCK_ROWS, D))
    two_low = shape((2, rows, D))
    two_f32 = shape((2, rows, D), F32)
    two_bias = shape((2, 1, D), F32)
    group_bias = shape((GROUPS, 1, GROUP_COLS), F32)
    weights = shape((2, D, D))
    heads = (
        shape((2, rows, 3 * GROUP_COLS)),
        shape((2 * HEADS_IN_GROUP * imgs, PAD, PAD), F32),
        shape((2, rows, GROUP_COLS)),
        row_f32,
    )
    vec, bias, start_rows, normed, qb, vb, w1_own, *heads_own, attn = call(
        functools.partial(attend_own_kernel, imgs),
        (tables[0], tok, rep, *w1_own),
        (
            shape((16, D), F32), shape((GROUPS, 1, D), F32), row_f32, row_low,
            group_bias, group_bias, weights, *heads,
        ),
        flops=SHORT,
    )
    w1_sib, *heads_sib, attn, mid, normed_two = call(
        functools.partial(attend_sib_kernel, imgs),
        (tables[0], vec, start_rows, normed, qb, vb, attn, *w1_sib),
        (weights, *heads, row_f32, row_low),
        flops=SHORT,
    )
    if direct:
        streams[1].finish(normed)
        w2_own, w2_sib = streams[1].own(), streams[1].sib(normed_two)
    three, two, one = (Scatter(SCATTER[index]) for index in (2, 1, 0))
    w2_own, act_own, slope_own, grad_branch, reduce_own = call(
        expand_own_kernel,
        (tables[1], normed_two, cot, vec, bias, *w2_own),
        (weights, two_low, two_f32, row_low, half),
        flops=LONG,
    )
    if direct:
        streams[2].finish(grad_branch)
    w2_sib, act_sib, slope_sib, reduce_sib = call(
        expand_sib_kernel,
        (tables[1], normed_two, grad_branch, bias, *w2_sib),
        (weights, two_low, two_f32, half),
        flops=SHORT,
    )
    if direct:
        three.swap(reduce_sib)
        w3_own, w3_sib = streams[2].own(), streams[2].sib(reduce_sib)
    w3_sib, hid_sib, units_sib, expand_sib = call(
        functools.partial(hidden_kernel, 1),
        (tables[2], normed_two, grad_branch, slope_sib, *w3_sib),
        (weights, two_low, two_bias, half),
        flops=LONG,
    )
    if direct:
        two.swap(expand_sib)
        three.add(reduce_own)
        slope_own = after(slope_own, three.step(expand_sib))
    w3_own, hid_own, units_own, expand_own = call(
        functools.partial(hidden_kernel, 0),
        (tables[2], normed_two, grad_branch, slope_own, *w3_own),
        (weights, two_low, two_bias, half),
        flops=LONG,
    )
    if direct:
        two.add(expand_own)
        mid = after(mid, two.step())
    block_out, grad_mid, grad_attn, sums = call(
        middle_kernel,
        (
            act_sib, act_own, hid_sib, hid_own, w2_sib, w2_own, w3_sib, w3_own,
            mid, attn, cot, vec,
        ),
        (shape(tokens.shape), row_f32, row_low, shape((16, D), F32)),
        (pltpu.VMEM((rows, D), F32), pltpu.VMEM((rows, D), F32)),
        flops=SHORT,
        table=False,
    )
    held = pltpu.VMEM((rows, 3 * GROUP_COLS), BF16)
    bias_sums = (2, 2, GROUP_COLS)
    first_sib, grad_one, bias_sib = call(
        functools.partial(back_sib_kernel, imgs),
        (tables[0], w1_sib, normed, *heads_sib, grad_attn),
        (half, row_f32, shape(bias_sums, F32)),
        (held,),
        flops=SHORT,
    )
    if direct:
        one.swap(first_sib)
        grad_one = after(grad_one, three.step(grad_one))
    first_own, grad_one, bias_own = call(
        functools.partial(back_own_kernel, imgs),
        (tables[0], w1_own, normed, *heads_own, grad_attn, grad_one),
        (half, row_f32, shape(bias_sums, F32)),
        (held,),
        flops=LONG,
    )
    if direct:
        first_own, grad_one = after((first_own, grad_one), three.terms[-1])
        one.add(first_own)
        sent = one.step()
        sent_three, sent_two = three.step(sent), two.step(sent)
        grad_one = after(grad_one, sent)
    tok_grad, sums = call(
        start_kernel,
        (
            tables[0], tok, rep, vec, grad_one, bias_sib, bias_own, grad_mid, sums,
            units_sib, units_own,
        ),
        (shape(tokens.shape), shape((24, D), F32)),
    )

    if direct:
        sums = add_across(sums, 1)
        one.hold(fence(sums, sent_three, sent_two))
        part = send_across(sums, 2)
        sent = one.step()
        sums = sums + after(part, sent)
        part = send_across(sums, 16)
        three.step(sent)
        two.step(sent)
        sent = one.step()
        sums = sums + after(part, sent)
        part = send_across(sums, 8)
        two.step(sent)
        sent = one.step()
        sums = add_across(sums + after(part, sent), 4)
        grad_three = three.result()
        states_three = adam_update(
            reduce_weight, grad_three.T, first_reduce, second_reduce, RATE_MATRIX, DECAY
        )
        two.hold(sent)
        grad_two = two.result()
        partial = sum(term[0].astype(F32) for term in one.terms[:-1])
        finished = call(
            finish_kernel,
            (
                partial, one.terms[-1][0], project_qkv, first_qkv, second_qkv,
                project_out, first_out, second_out,
            ),
            (shape(project_qkv.shape, F32),) * 3 + (shape(project_out.shape, F32),) * 3,
            table=False,
        )
    else:
        grad_three = scatter_plain(reduce_own, reduce_sib, n_dp)
        grad_two = scatter_plain(expand_own, expand_sib, n_dp)
        grad_one = scatter_plain(first_own, first_sib, n_dp)
        sums = lax.psum(sums, AXES)
        grad_qkv = jnp.stack([grad_one[:, i * GROUP_COLS : (i + 1) * GROUP_COLS] for i in range(3)])
        grad_out = grad_one[:, 3 * GROUP_COLS :].T
        states_three = adam_update(
            reduce_weight, grad_three.T, first_reduce, second_reduce, RATE_MATRIX, DECAY
        )
        finished = (
            *adam_update(project_qkv, grad_qkv, first_qkv, second_qkv, RATE_MATRIX, DECAY),
            *adam_update(project_out, grad_out, first_out, second_out, RATE_MATRIX, DECAY),
        )
    spot = lax.axis_index("dp")
    vector_grad = lax.dynamic_slice_in_dim(sums[0:11], spot * wide, wide, 1)
    grad_bias = lax.dynamic_slice_in_dim(sums[16:20].reshape(-1), spot * units, units, 0)
    return (
        block_out,
        tok_grad,
        *finished,
        *adam_update(expand_weight, grad_two, first_expand, second_expand, RATE_MATRIX, DECAY),
        *states_three,
        *adam_update(vectors, vector_grad, first_vectors, second_vectors, RATE_VECTOR, 0.0),
        *adam_update(expand_bias, grad_bias, first_bias, second_bias, RATE_VECTOR, 0.0),
    )


def solution(mesh):
    rows = P(AXES, None)
    states = (
        *(P(None, "dp", "tensor"),) * 3,
        *(P("tensor", "dp"),) * 3,
        *(P("dp", "tensor"),) * 3,
        *(P("tensor", "dp"),) * 3,
        *(P(None, "dp"),) * 3,
        *(P("dp"),) * 3,
    )
    return jax.shard_map(
        functools.partial(on_device, mesh.shape["dp"]),
        mesh=mesh,
        in_specs=(rows, rows, rows, *states),
        out_specs=(rows, rows, *states),
        check_vma=False,
    )
```

```python
import functools

import jax
import jax.numpy as jnp
import numpy as np
from jax import lax
from jax.experimental import pallas as pl
from jax.experimental.pallas import tpu as pltpu
from jax.sharding import PartitionSpec as P

D = 768
HEAD_DIM = 64
FF = 3072
SEQ = 197
STEP = 4
BETA_ONE = 0.5
BETA_TWO = 0.5
EPSILON = 1e-08
DECAY = 0.05
RATE_MATRIX = 0.02
RATE_VECTOR = 0.2
NORM_EPS = 1e-06

AXES = ("dp", "tensor")
PAD = 208
GROUPS = 4
GROUP_COLS = D // GROUPS
HEADS_IN_GROUP = GROUP_COLS // HEAD_DIM
BLOCKS = 8
BLOCK_ROWS = D // BLOCKS
EXTRA = 8
SCALE = HEAD_DIM**-0.5
SHORT = 1
LONG = 10**11
F32 = jnp.float32
BF16 = jnp.bfloat16

BIT = {"c": 1, "x": 2, "y": 4, "1": 8, "2": 16}
GATHER = (("21xy", "12yx"), ("2y1x", "yx21"), ("y21x", "1x2y"))
SCATTER = (("21yx", "12xy"), ("2x1y", "x21y"), ("y2x1", "y21x"))
STEPS = "S0S1S2D0S0D1S1D0S0D2S2F0D1S1D0S0D2S2D1S1F1D0"


def offset_of(order, place):
    found = 0
    for level in range(4):
        if place >> level & 1:
            found ^= BIT[order[level]]
    return found


def pairs_of(orders, level):
    return [(dev, dev ^ BIT[orders[dev & 1][level]]) for dev in range(32)]


CORE_PAIRS = [(dev, dev ^ 1) for dev in range(32)]


def build_table(gather, scatter):
    table = np.zeros((32, 80), np.int32)
    for dev in range(32):
        core = dev & 1
        for place in range(16):
            table[dev, place] = dev ^ offset_of(gather[core], place)
            table[dev, 16 + place] = dev ^ 1 ^ offset_of(gather[1 - core], place)
            mine = dev ^ offset_of(gather[core], place)
            if mine & 3 == dev & 3:
                table[dev, 32 + (mine >> 2)] = place
            table[dev, 40 + (dev ^ offset_of(scatter[core], place))] = place
            table[dev, 40 + (dev ^ 1 ^ offset_of(scatter[1 - core], place))] = place
        table[dev, 72] = core
    return table


def plain_table():
    table = np.zeros((80,), np.int32)
    for place in range(32):
        part, along_x, block = place // 16, place // 8 % 2, place % 8
        table[place] = block * 4 + along_x * 2 + part
    for block in range(8):
        table[32 + block] = block
        for group in range(4):
            table[40 + block * 4 + group] = block * 2 + group // 2
    return table


def dot(left, right):
    return jnp.dot(left, right, preferred_element_type=F32)


def dot_rt(left, right):
    return lax.dot_general(left, right, (((1,), (1,)), ((), ())), preferred_element_type=F32)


def dot_lt(left, right):
    return lax.dot_general(left, right, (((0,), (0,)), ((), ())), preferred_element_type=F32)


def norm_stats(values):
    mean = jnp.mean(values, axis=-1, keepdims=True)
    centred = values - mean
    var = jnp.mean(centred * centred, axis=-1, keepdims=True)
    rstd = lax.rsqrt(var + NORM_EPS)
    return centred * rstd, rstd


def norm_back(grad, gain, unit, rstd):
    grad_unit = grad * gain
    first = jnp.mean(grad_unit, axis=-1, keepdims=True)
    second = jnp.mean(grad_unit * unit, axis=-1, keepdims=True)
    return rstd * (grad_unit - first - unit * second)


def col_sum(values):
    return jnp.sum(values, axis=0, keepdims=True)


def assemble(tab, first, parts, whole):
    for index, part in enumerate(parts):
        for place in range(4):
            owner = tab[first + index * 4 + place]
            row = pl.multiple_of((owner >> 2) * BLOCK_ROWS, BLOCK_ROWS)
            whole[(owner >> 1) & 1, pl.ds(row, BLOCK_ROWS), :] = part[place, 0:BLOCK_ROWS, :]


def put_blocks(tab, group, grad, out):
    for block in range(BLOCKS):
        place = tab[40 + block * 4 + group]
        rows = slice(block * BLOCK_ROWS, (block + 1) * BLOCK_ROWS)
        out[place] = grad[rows].astype(BF16)


def mask_rows(tok, rep, vec):
    replaced = rep[...]
    return tok[...].astype(F32) * (1.0 - replaced) + vec[6:7, :] * replaced


def pad_kernel(values, out):
    wide = values[...].astype(F32)
    gap = jnp.zeros((PAD - SEQ, D), F32)
    rows = []
    for start in range(0, wide.shape[0], SEQ):
        rows += [wide[start : start + SEQ], gap]
    out[...] = jnp.concatenate(rows, axis=0).astype(BF16)


def cut_rows(wide):
    rows = [wide[start : start + SEQ] for start in range(0, wide.shape[0], PAD)]
    return jnp.concatenate(rows, axis=0).astype(BF16)


def fence_kernel(values, out):
    out[...] = values[...] + 1.0


def pack_kernel(project_qkv, project_out, vectors, expand_bias, out):
    columns = [project_qkv[0], project_qkv[1], project_qkv[2], project_out[...].T]
    block = jnp.concatenate(columns, axis=1)
    fill = jnp.zeros((EXTRA, 128 - BLOCK_ROWS), F32)
    low = jnp.concatenate([vectors[0:8, :], fill], axis=1)
    high = jnp.concatenate([vectors[8:11, :], jnp.zeros((5, BLOCK_ROWS), F32)], axis=0)
    high = jnp.concatenate([high, fill], axis=1)
    last = jnp.concatenate([expand_bias[...].reshape(1, 384), jnp.zeros((EXTRA - 1, 384), F32)], axis=0)
    extra = jnp.concatenate([low, high, last, jnp.zeros((EXTRA, 128), F32)], axis=1)
    out[...] = jnp.concatenate([block, extra], axis=0).astype(BF16)


def attend_groups(imgs, tab, part, normed, qb, vb, w1, qkv, soft, att, attn):
    keep = lax.broadcasted_iota(jnp.int32, (PAD, PAD), 1) < SEQ

    def step(along_x, carry):
        group = along_x * 2 + (tab[72] ^ part)
        result = dot(normed[...], w1[along_x, :, 0:576])
        qkv[along_x, :, 0:192] = (result[:, 0:192] + qb[group, 0:1, :]).astype(BF16)
        qkv[along_x, :, 192:384] = result[:, 192:384].astype(BF16)
        qkv[along_x, :, 384:576] = (result[:, 384:576] + vb[group, 0:1, :]).astype(BF16)
        for head in range(HEADS_IN_GROUP):
            c0 = head * HEAD_DIM
            for img in range(imgs):
                rows = slice(img * PAD, (img + 1) * PAD)
                q = qkv[along_x, rows, c0 : c0 + 64]
                k = qkv[along_x, rows, 192 + c0 : 256 + c0]
                v = qkv[along_x, rows, 384 + c0 : 448 + c0]
                scores = jnp.where(keep, dot_rt(q, k) * SCALE, -1e30)
                top = jnp.max(scores, axis=-1, keepdims=True)
                raised = jnp.exp(scores - top)
                weights = raised / jnp.sum(raised, axis=-1, keepdims=True)
                soft[along_x * (HEADS_IN_GROUP * imgs) + head * imgs + img] = weights
                att[along_x, rows, c0 : c0 + 64] = dot(weights.astype(BF16), v).astype(BF16)
        attn[...] += dot_rt(att[along_x], w1[along_x, :, 576:768])
        return carry

    lax.fori_loop(0, 2, step, 0)


def attend_own_kernel(
    imgs, tab, tok, rep, b0, b1, b2, b3,
    vec, bias, start_rows, normed, qb, vb, w1, qkv, soft, att, attn,
):
    low = jnp.zeros((8, D), F32)
    high = jnp.zeros((8, D), F32)
    fill = jnp.zeros((8, D - 128), F32)
    for block in range(BLOCKS):
        place = tab[32 + block]
        piece = jnp.zeros((EXTRA, D), F32)
        for index, part in enumerate((b0, b1, b2, b3)):
            rows = part[place & 3].astype(F32)[BLOCK_ROWS:]
            piece = jnp.where(place >> 2 == index, rows, piece)
        low += pltpu.roll(jnp.concatenate([piece[:, 0:128], fill], 1), block * BLOCK_ROWS, 1)
        high += pltpu.roll(jnp.concatenate([piece[:, 128:256], fill], 1), block * BLOCK_ROWS, 1)
        half = (block % 2) * 384
        bias[block // 2, 0:1, half : half + 384] = piece[0:1, 256:640]
    vec[0:8, :] = low
    vec[8:16, :] = high
    for group in range(GROUPS):
        cols = slice(group * GROUP_COLS, (group + 1) * GROUP_COLS)
        qb[group, 0:1, :] = vec[9:10, cols]
        vb[group, 0:1, :] = vec[10:11, cols]
    assemble(tab, 0, (b0, b1, b2, b3), w1)
    start = mask_rows(tok, rep, vec)
    start_rows[...] = start
    unit, _ = norm_stats(start)
    normed[...] = (unit * vec[0:1, :] + vec[1:2, :]).astype(BF16)
    attn[...] = jnp.zeros_like(attn)
    attend_groups(imgs, tab, 0, normed, qb, vb, w1, qkv, soft, att, attn)


def attend_sib_kernel(
    imgs, tab, vec, start_rows, normed, qb, vb, attn_in, b0, b1, b2, b3,
    w1, qkv, soft, att, attn, mid, normed_two,
):
    assemble(tab, 16, (b0, b1, b2, b3), w1)
    attn[...] = attn_in[...]
    attend_groups(imgs, tab, 1, normed, qb, vb, w1, qkv, soft, att, attn)
    middle = start_rows[...] + vec[4:5, :] * (attn[...] + vec[7:8, :])
    mid[...] = middle
    unit_two, _ = norm_stats(middle)
    normed_two[...] = (unit_two * vec[2:3, :] + vec[3:4, :]).astype(BF16)


def expand_groups(tab, part, normed_two, grad_branch, bias, w2, active, slope, out):
    def step(along_x, carry):
        group = along_x * 2 + (tab[72] ^ part)
        hidden = dot(normed_two[...], w2[along_x]) + bias[group, 0:1, :]
        cdf = 0.5 * (1.0 + lax.erf(hidden * 0.7071067811865476))
        pdf = 0.3989422804014327 * jnp.exp(-0.5 * hidden * hidden)
        act = (hidden * cdf).astype(BF16)
        active[along_x] = act
        slope[along_x] = cdf + hidden * pdf
        put_blocks(tab, group, dot_lt(grad_branch[...], act), out)
        return carry

    lax.fori_loop(0, 2, step, 0)


def expand_own_kernel(
    tab, normed_two, cot, vec, bias, b0, b1, b2, b3, w2, active, slope, grad_branch, out
):
    assemble(tab, 0, (b0, b1, b2, b3), w2)
    grad_branch[...] = (cot[...].astype(F32) * vec[5:6, :]).astype(BF16)
    expand_groups(tab, 0, normed_two, grad_branch, bias, w2, active, slope, out)


def expand_sib_kernel(
    tab, normed_two, grad_branch, bias, b0, b1, b2, b3, w2, active, slope, out
):
    assemble(tab, 16, (b0, b1, b2, b3), w2)
    expand_groups(tab, 1, normed_two, grad_branch, bias, w2, active, slope, out)


def hidden_groups(tab, part, normed_two, grad_branch, slope, w3, grad_hidden, bias_grad, out):
    def step(along_x, carry):
        group = along_x * 2 + (tab[72] ^ part)
        grad = (dot(grad_branch[...], w3[along_x]) * slope[along_x]).astype(BF16)
        grad_hidden[along_x] = grad
        bias_grad[along_x, 0:1, :] = col_sum(grad.astype(F32))
        put_blocks(tab, group, dot_lt(normed_two[...], grad), out)
        return carry

    lax.fori_loop(0, 2, step, 0)


def hidden_kernel(
    part, tab, normed_two, grad_branch, slope, b0, b1, b2, b3, w3, grad_hidden, bias_grad, out
):
    assemble(tab, 16 * part, (b0, b1, b2, b3), w3)
    hidden_groups(tab, part, normed_two, grad_branch, slope, w3, grad_hidden, bias_grad, out)


def middle_kernel(
    act_sib, act_own, hid_sib, hid_own, w2_sib, w2_own, w3_sib, w3_own, mid, attn, cot, vec,
    block_out, grad_mid, grad_attn, sums, branch, grad_two,
):
    sums[...] = jnp.zeros_like(sums)
    found = jnp.zeros(branch.shape, F32)
    for active, w3 in ((act_sib, w3_sib), (act_own, w3_own)):
        for along_x in range(2):
            found += dot_rt(active[along_x], w3[along_x])
    branch[...] = found
    found = jnp.zeros(branch.shape, F32)
    for grad_hidden, w2 in ((hid_sib, w2_sib), (hid_own, w2_own)):
        for along_x in range(2):
            found += dot_rt(grad_hidden[along_x], w2[along_x])
    grad_two[...] = found
    middle = mid[...]
    total = branch[...] + vec[8:9, :]
    block_out[...] = cut_rows(middle + vec[5:6, :] * total)
    grad_out = cot[...].astype(F32)
    sums[5:6, :] = col_sum(grad_out * total)
    sums[8:9, :] = col_sum(grad_out * vec[5:6, :])
    unit, rstd = norm_stats(middle)
    grad = grad_two[...]
    sums[2:3, :] = col_sum(grad * unit)
    sums[3:4, :] = col_sum(grad)
    grad_middle = grad_out + norm_back(grad, vec[2:3, :], unit, rstd)
    grad_mid[...] = grad_middle
    sums[4:5, :] = col_sum(grad_middle * (attn[...] + vec[7:8, :]))
    scaled = grad_middle * vec[4:5, :]
    sums[7:8, :] = col_sum(scaled)
    grad_attn[...] = scaled.astype(BF16)


def back_groups(
    imgs, tab, part, w1, normed, qkv, soft, att, grad_attn, out, grad_one, gqkv, bias_sums
):
    def step(along_x, carry):
        group = along_x * 2 + (tab[72] ^ part)
        grad_att = dot(grad_attn[...], w1[along_x, :, 576:768]).astype(BF16)
        for head in range(HEADS_IN_GROUP):
            c0 = head * HEAD_DIM
            for img in range(imgs):
                rows = slice(img * PAD, (img + 1) * PAD)
                q = qkv[along_x, rows, c0 : c0 + 64]
                k = qkv[along_x, rows, 192 + c0 : 256 + c0]
                v = qkv[along_x, rows, 384 + c0 : 448 + c0]
                weights = soft[along_x * (HEADS_IN_GROUP * imgs) + head * imgs + img]
                grad = grad_att[rows, c0 : c0 + 64]
                grad_soft = dot_rt(grad, v)
                grad_v = dot_lt(weights.astype(BF16), grad)
                inner = jnp.sum(weights * grad_soft, axis=-1, keepdims=True)
                grad_scores = (weights * (grad_soft - inner)).astype(BF16)
                grad_q = dot(grad_scores, k) * SCALE
                grad_k = dot_lt(grad_scores, q) * SCALE
                gqkv[rows, c0 : c0 + 64] = grad_q.astype(BF16)
                gqkv[rows, 192 + c0 : 256 + c0] = grad_k.astype(BF16)
                gqkv[rows, 384 + c0 : 448 + c0] = grad_v.astype(BF16)
        all_grads = gqkv[...]
        bias_sums[along_x, 0:1, :] = col_sum(all_grads[:, 0:192].astype(F32))
        bias_sums[along_x, 1:2, :] = col_sum(all_grads[:, 384:576].astype(F32))
        grad_one[...] += dot_rt(all_grads, w1[along_x, :, 0:576])
        both = jnp.concatenate(
            [dot_lt(normed[...], all_grads), dot_lt(grad_attn[...], att[along_x])], axis=1
        )
        put_blocks(tab, group, both, out)
        return carry

    lax.fori_loop(0, 2, step, 0)


def back_sib_kernel(
    imgs, tab, w1, normed, qkv, soft, att, grad_attn, out, grad_one, bias_sums, gqkv
):
    grad_one[...] = jnp.zeros_like(grad_one)
    back_groups(
        imgs, tab, 1, w1, normed, qkv, soft, att, grad_attn, out, grad_one, gqkv, bias_sums
    )


def back_own_kernel(
    imgs, tab, w1, normed, qkv, soft, att, grad_attn, grad_one_in, out, grad_one, bias_sums, gqkv
):
    grad_one[...] = grad_one_in[...]
    back_groups(
        imgs, tab, 0, w1, normed, qkv, soft, att, grad_attn, out, grad_one, gqkv, bias_sums
    )


def start_kernel(
    tab, tok, rep, vec, grad_one, bias_sib, bias_own, grad_mid, sums_in, units_sib, units_own,
    tok_grad, sums,
):
    replaced = rep[...]
    unit, rstd = norm_stats(mask_rows(tok, rep, vec))
    grad = grad_one[...]
    sums[0:16, :] = sums_in[...]
    sums[16:24, :] = jnp.zeros((8, D), F32)
    sums[0:1, :] = col_sum(grad * unit)
    sums[1:2, :] = col_sum(grad)
    grad_start = grad_mid[...] + norm_back(grad, vec[0:1, :], unit, rstd)
    tok_grad[...] = cut_rows(grad_start * (1.0 - replaced))
    sums[6:7, :] = col_sum(grad_start * replaced)
    for group in range(GROUPS):
        cols = slice(group * GROUP_COLS, (group + 1) * GROUP_COLS)
        own = tab[72] == group % 2
        along_x = group // 2
        both = jnp.where(own, bias_own[along_x], bias_sib[along_x])
        sums[9:10, cols] = both[0:1]
        sums[10:11, cols] = both[1:2]
        sums[16 + group : 17 + group, :] = jnp.where(own, units_own[along_x], units_sib[along_x])


def adam_update(weight, gradient, first_moment, second, step_rate, decay_rate):
    moment = BETA_ONE * first_moment + (1.0 - BETA_ONE) * gradient
    square = BETA_TWO * second + (1.0 - BETA_TWO) * gradient * gradient
    first_hat = moment / (1.0 - BETA_ONE**STEP)
    second_hat = square / (1.0 - BETA_TWO**STEP)
    updated = weight - step_rate * (
        first_hat / (jnp.sqrt(second_hat) + EPSILON) + decay_rate * weight
    )
    return (updated, moment, square)


def finish_kernel(
    partial, last, qkv, first_qkv, second_qkv, out, first_out, second_out, *results
):
    grad = partial[...] + last[...].astype(F32)
    for index in range(3):
        cols = slice(index * GROUP_COLS, (index + 1) * GROUP_COLS)
        found = adam_update(
            qkv[index], grad[:, cols], first_qkv[index], second_qkv[index], RATE_MATRIX, DECAY
        )
        for result, values in zip(results[:3], found, strict=True):
            result[index] = values
    found = adam_update(
        out[...], grad[:, 576:768].T, first_out[...], second_out[...], RATE_MATRIX, DECAY
    )
    for result, values in zip(results[3:], found, strict=True):
        result[...] = values


VMEM = pl.BlockSpec(memory_space=pltpu.VMEM)
SMEM = pl.BlockSpec(memory_space=pltpu.SMEM)


def shape(dims, dtype=BF16):
    return jax.ShapeDtypeStruct(dims, dtype)


def call(kernel, args, outs, scratch=(), flops=SHORT, megabytes=10, table=True):
    return pl.pallas_call(
        kernel,
        out_shape=outs,
        in_specs=[SMEM] * table + [VMEM] * (len(args) - table),
        out_specs=[VMEM] * len(outs),
        scratch_shapes=list(scratch),
        cost_estimate=pl.CostEstimate(flops=flops, bytes_accessed=1, transcendentals=0),
        compiler_params=pltpu.CompilerParams(vmem_limit_bytes=megabytes << 20),
    )(*args)


def after(value, *earlier):
    return lax.optimization_barrier((value, earlier))[0]


def fence(*earlier):
    mark = after(jnp.zeros((8, 128), F32), *earlier)
    return call(fence_kernel, (mark,), (shape((8, 128), F32),), flops=LONG, table=False)[0]


def send_across(values, mask):
    return lax.ppermute(values, AXES, [(dev, dev ^ mask) for dev in range(32)])


def add_across(values, mask):
    return values + send_across(values, mask)


class Gather:
    def __init__(self, block, orders):
        self.held = block[None]
        self.orders = orders
        self.level = 0

    def send(self, values, level):
        return lax.ppermute(values, AXES, pairs_of(self.orders, level))

    def start(self, *earlier):
        if earlier:
            self.held = after(self.held, *earlier)
        if self.level < 3:
            self.taken = self.send(self.held, self.level)
            if self.level == 2:
                self.far = self.send(self.held, 3)
        else:
            self.last = self.send(self.held, 3)
        self.level += 1

    def take(self):
        if self.level < 3:
            self.held = jnp.concatenate([self.held, self.taken], axis=0)
            return self.taken
        if self.level == 3:
            self.near = self.held
            self.held = self.taken
            return self.taken, self.far
        return self.last

    def finish(self, *earlier):
        while self.level < 4:
            self.taken = after(self.taken, *earlier)
            self.take()
            self.start()

    def own(self):
        return self.near, self.taken, self.far, self.last

    def sib(self, *earlier):
        own = self.near, self.taken, self.far, after(self.last, *earlier)
        return tuple(lax.ppermute(values, AXES, CORE_PAIRS) for values in own)


class Scatter:
    def __init__(self, orders):
        self.orders = orders
        self.level = 4
        self.terms = []

    def swap(self, sib):
        self.terms.append(lax.ppermute(sib, AXES, CORE_PAIRS))

    def add(self, own):
        self.terms.insert(0, own)

    def total(self, low, high):
        return sum(term[low:high].astype(F32) for term in self.terms)

    def step(self, *earlier):
        self.level -= 1
        size = 1 << self.level
        if earlier:
            self.terms[-1] = after(self.terms[-1], *earlier)
        sent = self.total(size, 2 * size).astype(BF16)
        self.terms.append(lax.ppermute(sent, AXES, pairs_of(self.orders, self.level)))
        return sent

    def spread(self, *earlier):
        if earlier:
            self.hold(*earlier)
        sent = [self.total(place, place + 1).astype(BF16) for place in (1, 2, 3)]
        for place, values in zip((1, 2, 3), sent, strict=True):
            pairs = [(dev, dev ^ offset_of(self.orders[dev & 1], place)) for dev in range(32)]
            self.terms.append(lax.ppermute(values, AXES, pairs))
        return sent

    def hold(self, *earlier):
        self.terms[-1] = after(self.terms[-1], *earlier)

    def result(self):
        return self.total(0, 1)[0]


def gather_plain(block):
    whole = lax.all_gather(block, AXES, axis=0, tiled=False)
    whole = whole.reshape(-1, GROUPS, *block.shape).transpose(1, 0, 2, 3)
    whole = whole.reshape(2, 2, BLOCKS, BLOCK_ROWS, D).transpose(1, 0, 2, 3, 4)
    whole = whole.reshape(2, 4, 4, BLOCK_ROWS, D)
    return tuple(tuple(part[index] for index in range(4)) for part in whole)


def scatter_plain(own, sib, n_dp):
    parts = jnp.stack([own, sib]).reshape(2, BLOCKS, 2, BLOCK_ROWS, D)
    whole = parts.transpose(1, 3, 2, 0, 4).reshape(D, GROUPS, D).astype(F32)
    whole = whole.reshape(n_dp, D // n_dp, GROUPS, D).transpose(0, 2, 1, 3)
    whole = whole.reshape(n_dp * GROUPS, D // n_dp, D)
    return lax.psum_scatter(whole, AXES, scatter_dimension=0, tiled=True)[0]


def on_device(
    n_dp,
    tokens,
    patch_mask,
    cotangent,
    project_qkv,
    first_qkv,
    second_qkv,
    project_out,
    first_out,
    second_out,
    expand_weight,
    first_expand,
    second_expand,
    reduce_weight,
    first_reduce,
    second_reduce,
    vectors,
    first_vectors,
    second_vectors,
    expand_bias,
    first_bias,
    second_bias,
):
    direct = n_dp == BLOCKS
    imgs = patch_mask.shape[0]
    rows = imgs * PAD
    wide = vectors.shape[1]
    units = expand_bias.shape[0]

    def padded(values):
        values = values.reshape(imgs, SEQ, -1)
        return jnp.pad(values, ((0, 0), (0, PAD - SEQ), (0, 0))).reshape(rows, -1)

    positions = lax.broadcasted_iota(jnp.int32, patch_mask.shape, 1)
    replaced = jnp.where((patch_mask == 1) & (positions > 0), 1.0, 0.0).astype(F32)
    rep = padded(replaced)

    def pad_rows(values):
        return call(pad_kernel, (values,), (shape((rows, D)),), flops=LONG, table=False)[0]

    piece_two = expand_weight.astype(BF16)
    piece_three = reduce_weight.astype(BF16).T
    if direct:
        flat = lax.axis_index("dp") * GROUPS + lax.axis_index("tensor")
        chosen = zip(GATHER, (SCATTER[0], SCATTER[2], SCATTER[1]), strict=True)
        every = np.concatenate([build_table(g, s) for g, s in chosen], axis=1)
        table = lax.dynamic_index_in_dim(jnp.asarray(every), flat, 0, keepdims=False)
        tables = [table[0:80], table[80:160], table[160:240]]
        (piece_one,) = call(
            pack_kernel,
            (project_qkv, project_out, vectors, expand_bias),
            (shape((BLOCK_ROWS + EXTRA, D)),),
            table=False,
        )
        streams = [
            Gather(piece, orders)
            for piece, orders in zip((piece_one, piece_two, piece_three), GATHER, strict=True)
        ]
        seen = {}
        for kind, index in zip(STEPS[0::2], STEPS[1::2], strict=True):
            stream = streams[int(index)]
            held = [stream.held for stream in streams]
            if kind == "X":
                seen["mark"] = fence(*held, *seen.values())
            elif kind == "F":
                if index == "0":
                    tok = pad_rows(after(tokens, *held[:2]))
                    seen["tok"] = (tok, rep, *tables)
                else:
                    cot = pad_rows(after(cotangent, held[1]))
                    seen["cot"] = cot
            elif kind == "S":
                stream.start(*seen.values())
            else:
                seen[index] = stream.take()
        marks = [seen[name] for name in seen if name not in "12"]
        w1_own, w1_sib = streams[0].own(), streams[0].sib(*marks)
    else:
        tables = [jnp.asarray(plain_table())] * 3
        tok, cot = pad_rows(tokens), pad_rows(cotangent)
        piece_one = jnp.concatenate(
            [project_qkv[0], project_qkv[1], project_qkv[2], project_out.T], axis=1
        ).astype(BF16)
        w1_parts, (w2_own, w2_sib), (w3_own, w3_sib) = (
            gather_plain(piece) for piece in (piece_one, piece_two, piece_three)
        )
        vector_all = lax.all_gather(vectors.astype(BF16), "dp", axis=1, tiled=True)
        bias_all = lax.all_gather(expand_bias.astype(BF16), "dp", axis=0, tiled=True)
        by_block = vector_all.reshape(11, BLOCKS, BLOCK_ROWS).transpose(1, 0, 2)
        extras = jnp.zeros((BLOCKS, EXTRA, D), BF16)
        extras = extras.at[:, :, 0:BLOCK_ROWS].set(by_block[:, 0:8])
        extras = extras.at[:, 0:3, 128 : 128 + BLOCK_ROWS].set(by_block[:, 8:11])
        extras = extras.at[:, 0, 256:640].set(bias_all.reshape(BLOCKS, FF // BLOCKS))
        w1_own, w1_sib = (
            tuple(
                jnp.concatenate([part, extras[4 * (at % 2) : 4 * (at % 2) + 4]], axis=1)
                for at, part in enumerate(parts)
            )
            for parts in w1_parts
        )

    full = (GROUPS, D, D)
    row_f32 = shape((rows, D), F32)
    row_low = shape((rows, D))
    half = shape((16, BLOCK_ROWS, D))
    two_low = shape((2, rows, D))
    two_f32 = shape((2, rows, D), F32)
    two_bias = shape((2, 1, D), F32)
    group_bias = shape((GROUPS, 1, GROUP_COLS), F32)
    weights = shape((2, D, D))
    heads = (
        shape((2, rows, 3 * GROUP_COLS)),
        shape((2 * HEADS_IN_GROUP * imgs, PAD, PAD), F32),
        shape((2, rows, GROUP_COLS)),
        row_f32,
    )
    vec, bias, start_rows, normed, qb, vb, w1_own, *heads_own, attn = call(
        functools.partial(attend_own_kernel, imgs),
        (tables[0], tok, rep, *w1_own),
        (
            shape((16, D), F32), shape((GROUPS, 1, D), F32), row_f32, row_low,
            group_bias, group_bias, weights, *heads,
        ),
        flops=SHORT,
    )
    w1_sib, *heads_sib, attn, mid, normed_two = call(
        functools.partial(attend_sib_kernel, imgs),
        (tables[0], vec, start_rows, normed, qb, vb, attn, *w1_sib),
        (weights, *heads, row_f32, row_low),
        flops=SHORT,
    )
    if direct:
        streams[1].finish(normed)
        w2_own, w2_sib = streams[1].own(), streams[1].sib(normed_two)
    three, two, one = (Scatter(SCATTER[index]) for index in (2, 1, 0))
    w2_own, act_own, slope_own, grad_branch, reduce_own = call(
        expand_own_kernel,
        (tables[1], normed_two, cot, vec, bias, *w2_own),
        (weights, two_low, two_f32, row_low, half),
        flops=LONG,
    )
    if direct:
        streams[2].finish(grad_branch)
    w2_sib, act_sib, slope_sib, reduce_sib = call(
        expand_sib_kernel,
        (tables[1], normed_two, grad_branch, bias, *w2_sib),
        (weights, two_low, two_f32, half),
        flops=SHORT,
    )
    if direct:
        three.swap(reduce_sib)
        w3_own, w3_sib = streams[2].own(), streams[2].sib(reduce_sib)
    w3_sib, hid_sib, units_sib, expand_sib = call(
        functools.partial(hidden_kernel, 1),
        (tables[2], normed_two, grad_branch, slope_sib, *w3_sib),
        (weights, two_low, two_bias, half),
        flops=LONG,
    )
    if direct:
        two.swap(expand_sib)
        three.add(reduce_own)
        slope_own = after(slope_own, three.step(expand_sib))
    w3_own, hid_own, units_own, expand_own = call(
        functools.partial(hidden_kernel, 0),
        (tables[2], normed_two, grad_branch, slope_own, *w3_own),
        (weights, two_low, two_bias, half),
        flops=LONG,
    )
    if direct:
        two.add(expand_own)
        mid = after(mid, two.step())
    block_out, grad_mid, grad_attn, sums = call(
        middle_kernel,
        (
            act_sib, act_own, hid_sib, hid_own, w2_sib, w2_own, w3_sib, w3_own,
            mid, attn, cot, vec,
        ),
        (shape(tokens.shape), row_f32, row_low, shape((16, D), F32)),
        (pltpu.VMEM((rows, D), F32), pltpu.VMEM((rows, D), F32)),
        flops=SHORT,
        table=False,
    )
    held = pltpu.VMEM((rows, 3 * GROUP_COLS), BF16)
    bias_sums = (2, 2, GROUP_COLS)
    first_sib, grad_one, bias_sib = call(
        functools.partial(back_sib_kernel, imgs),
        (tables[0], w1_sib, normed, *heads_sib, grad_attn),
        (half, row_f32, shape(bias_sums, F32)),
        (held,),
        flops=SHORT,
    )
    if direct:
        one.swap(first_sib)
        grad_one = after(grad_one, three.step(grad_one))
    first_own, grad_one, bias_own = call(
        functools.partial(back_own_kernel, imgs),
        (tables[0], w1_own, normed, *heads_own, grad_attn, grad_one),
        (half, row_f32, shape(bias_sums, F32)),
        (held,),
        flops=LONG,
    )
    if direct:
        first_own, grad_one = after((first_own, grad_one), three.terms[-1])
        one.add(first_own)
        sent = one.step()
        sent_three, sent_two = three.step(sent), two.step(sent)
        grad_one = after(grad_one, sent)
    tok_grad, sums = call(
        start_kernel,
        (
            tables[0], tok, rep, vec, grad_one, bias_sib, bias_own, grad_mid, sums,
            units_sib, units_own,
        ),
        (shape(tokens.shape), shape((24, D), F32)),
    )

    if direct:
        sums = add_across(sums, 1)
        one.hold(fence(sums, sent_three, sent_two))
        part = send_across(sums, 2)
        sent = one.step()
        sums = sums + after(part, sent)
        part = send_across(sums, 16)
        three.step(sent)
        two.step(sent)
        sent = one.spread()
        sums = sums + after(part, sent)
        part = send_across(sums, 8)
        two.step(sent)
        sums = add_across(sums + after(part, sent), 4)
        grad_three = three.result()
        states_three = adam_update(
            reduce_weight, grad_three.T, first_reduce, second_reduce, RATE_MATRIX, DECAY
        )
        two.hold(sent)
        grad_two = two.result()
        partial = sum(term[0].astype(F32) for term in one.terms[:-1])
        finished = call(
            finish_kernel,
            (
                partial, one.terms[-1][0], project_qkv, first_qkv, second_qkv,
                project_out, first_out, second_out,
            ),
            (shape(project_qkv.shape, F32),) * 3 + (shape(project_out.shape, F32),) * 3,
            table=False,
        )
    else:
        grad_three = scatter_plain(reduce_own, reduce_sib, n_dp)
        grad_two = scatter_plain(expand_own, expand_sib, n_dp)
        grad_one = scatter_plain(first_own, first_sib, n_dp)
        sums = lax.psum(sums, AXES)
        grad_qkv = jnp.stack([grad_one[:, i * GROUP_COLS : (i + 1) * GROUP_COLS] for i in range(3)])
        grad_out = grad_one[:, 3 * GROUP_COLS :].T
        states_three = adam_update(
            reduce_weight, grad_three.T, first_reduce, second_reduce, RATE_MATRIX, DECAY
        )
        finished = (
            *adam_update(project_qkv, grad_qkv, first_qkv, second_qkv, RATE_MATRIX, DECAY),
            *adam_update(project_out, grad_out, first_out, second_out, RATE_MATRIX, DECAY),
        )
    spot = lax.axis_index("dp")
    vector_grad = lax.dynamic_slice_in_dim(sums[0:11], spot * wide, wide, 1)
    grad_bias = lax.dynamic_slice_in_dim(sums[16:20].reshape(-1), spot * units, units, 0)
    return (
        block_out,
        tok_grad,
        *finished,
        *adam_update(expand_weight, grad_two, first_expand, second_expand, RATE_MATRIX, DECAY),
        *states_three,
        *adam_update(vectors, vector_grad, first_vectors, second_vectors, RATE_VECTOR, 0.0),
        *adam_update(expand_bias, grad_bias, first_bias, second_bias, RATE_VECTOR, 0.0),
    )


def solution(mesh):
    rows = P(AXES, None)
    states = (
        *(P(None, "dp", "tensor"),) * 3,
        *(P("tensor", "dp"),) * 3,
        *(P("dp", "tensor"),) * 3,
        *(P("tensor", "dp"),) * 3,
        *(P(None, "dp"),) * 3,
        *(P("dp"),) * 3,
    )
    return jax.shard_map(
        functools.partial(on_device, mesh.shape["dp"]),
        mesh=mesh,
        in_specs=(rows, rows, rows, *states),
        out_specs=(rows, rows, *states),
        check_vma=False,
    )
```

```python
import functools

import jax
import jax.numpy as jnp
import numpy as np
from jax import lax
from jax.experimental import pallas as pl
from jax.experimental.pallas import tpu as pltpu
from jax.sharding import PartitionSpec as P

D = 768
HEAD_DIM = 64
FF = 3072
SEQ = 197
STEP = 4
BETA_ONE = 0.5
BETA_TWO = 0.5
EPSILON = 1e-08
DECAY = 0.05
RATE_MATRIX = 0.02
RATE_VECTOR = 0.2
NORM_EPS = 1e-06

AXES = ("dp", "tensor")
PAD = 208
GROUPS = 4
GROUP_COLS = D // GROUPS
HEADS_IN_GROUP = GROUP_COLS // HEAD_DIM
BLOCKS = 8
BLOCK_ROWS = D // BLOCKS
EXTRA = 8
SCALE = HEAD_DIM**-0.5
SHORT = 1
LONG = 10**11
F32 = jnp.float32
BF16 = jnp.bfloat16

BIT = {"c": 1, "x": 2, "y": 4, "1": 8, "2": 16}
GATHER = (("21xy", "12yx"), ("2y1x", "yx21"), ("y21x", "1x2y"))
SCATTER = (("21yx", "12xy"), ("2x1y", "x21y"), ("y2x1", "y21x"))
STEPS = "S0S1S2D1S1D0S0D2S2F0D1S1D0S0D2S2D1S1F1D0"
SPREAD = (True, False, False)


def offset_of(order, place):
    found = 0
    for level in range(4):
        if place >> level & 1:
            found ^= BIT[order[level]]
    return found


def pairs_of(orders, level):
    return [(dev, dev ^ BIT[orders[dev & 1][level]]) for dev in range(32)]


def partners_of(orders, place):
    return [(dev, dev ^ offset_of(orders[dev & 1], place)) for dev in range(32)]


CORE_PAIRS = [(dev, dev ^ 1) for dev in range(32)]


def build_table(gather, scatter):
    table = np.zeros((32, 80), np.int32)
    for dev in range(32):
        core = dev & 1
        for place in range(16):
            table[dev, place] = dev ^ offset_of(gather[core], place)
            table[dev, 16 + place] = dev ^ 1 ^ offset_of(gather[1 - core], place)
            mine = dev ^ offset_of(gather[core], place)
            if mine & 3 == dev & 3:
                table[dev, 32 + (mine >> 2)] = place
            table[dev, 40 + (dev ^ offset_of(scatter[core], place))] = place
            table[dev, 40 + (dev ^ 1 ^ offset_of(scatter[1 - core], place))] = place
        table[dev, 72] = core
    return table


def plain_table():
    table = np.zeros((80,), np.int32)
    for place in range(32):
        part, along_x, block = place // 16, place // 8 % 2, place % 8
        table[place] = block * 4 + along_x * 2 + part
    for block in range(8):
        table[32 + block] = block
        for group in range(4):
            table[40 + block * 4 + group] = block * 2 + group // 2
    return table


def dot(left, right):
    return jnp.dot(left, right, preferred_element_type=F32)


def dot_rt(left, right):
    return lax.dot_general(left, right, (((1,), (1,)), ((), ())), preferred_element_type=F32)


def dot_lt(left, right):
    return lax.dot_general(left, right, (((0,), (0,)), ((), ())), preferred_element_type=F32)


def norm_stats(values):
    mean = jnp.mean(values, axis=-1, keepdims=True)
    centred = values - mean
    var = jnp.mean(centred * centred, axis=-1, keepdims=True)
    rstd = lax.rsqrt(var + NORM_EPS)
    return centred * rstd, rstd


def norm_back(grad, gain, unit, rstd):
    grad_unit = grad * gain
    first = jnp.mean(grad_unit, axis=-1, keepdims=True)
    second = jnp.mean(grad_unit * unit, axis=-1, keepdims=True)
    return rstd * (grad_unit - first - unit * second)


def col_sum(values):
    return jnp.sum(values, axis=0, keepdims=True)


def assemble(tab, first, parts, whole):
    for index, part in enumerate(parts):
        for place in range(4):
            owner = tab[first + index * 4 + place]
            row = pl.multiple_of((owner >> 2) * BLOCK_ROWS, BLOCK_ROWS)
            whole[(owner >> 1) & 1, pl.ds(row, BLOCK_ROWS), :] = part[place, 0:BLOCK_ROWS, :]


def put_blocks(tab, group, grad, out):
    for block in range(BLOCKS):
        place = tab[40 + block * 4 + group]
        rows = slice(block * BLOCK_ROWS, (block + 1) * BLOCK_ROWS)
        out[place] = grad[rows].astype(BF16)


def mask_rows(tok, rep, vec):
    replaced = rep[...]
    return tok[...].astype(F32) * (1.0 - replaced) + vec[6:7, :] * replaced


def pad_kernel(values, out):
    wide = values[...].astype(F32)
    gap = jnp.zeros((PAD - SEQ, D), F32)
    rows = []
    for start in range(0, wide.shape[0], SEQ):
        rows += [wide[start : start + SEQ], gap]
    out[...] = jnp.concatenate(rows, axis=0).astype(BF16)


def cut_rows(wide):
    rows = [wide[start : start + SEQ] for start in range(0, wide.shape[0], PAD)]
    return jnp.concatenate(rows, axis=0).astype(BF16)


def fence_kernel(values, out):
    out[...] = values[...] + 1.0


def pack_kernel(project_qkv, project_out, vectors, expand_bias, out):
    columns = [project_qkv[0], project_qkv[1], project_qkv[2], project_out[...].T]
    block = jnp.concatenate(columns, axis=1)
    fill = jnp.zeros((EXTRA, 128 - BLOCK_ROWS), F32)
    low = jnp.concatenate([vectors[0:8, :], fill], axis=1)
    high = jnp.concatenate([vectors[8:11, :], jnp.zeros((5, BLOCK_ROWS), F32)], axis=0)
    high = jnp.concatenate([high, fill], axis=1)
    last = jnp.concatenate([expand_bias[...].reshape(1, 384), jnp.zeros((EXTRA - 1, 384), F32)], axis=0)
    extra = jnp.concatenate([low, high, last, jnp.zeros((EXTRA, 128), F32)], axis=1)
    out[...] = jnp.concatenate([block, extra], axis=0).astype(BF16)


def attend_groups(imgs, tab, part, normed, qb, vb, w1, qkv, soft, att, attn):
    keep = lax.broadcasted_iota(jnp.int32, (PAD, PAD), 1) < SEQ

    def step(along_x, carry):
        group = along_x * 2 + (tab[72] ^ part)
        result = dot(normed[...], w1[along_x, :, 0:576])
        qkv[along_x, :, 0:192] = (result[:, 0:192] + qb[group, 0:1, :]).astype(BF16)
        qkv[along_x, :, 192:384] = result[:, 192:384].astype(BF16)
        qkv[along_x, :, 384:576] = (result[:, 384:576] + vb[group, 0:1, :]).astype(BF16)
        for head in range(HEADS_IN_GROUP):
            c0 = head * HEAD_DIM
            for img in range(imgs):
                rows = slice(img * PAD, (img + 1) * PAD)
                q = qkv[along_x, rows, c0 : c0 + 64]
                k = qkv[along_x, rows, 192 + c0 : 256 + c0]
                v = qkv[along_x, rows, 384 + c0 : 448 + c0]
                scores = jnp.where(keep, dot_rt(q, k) * SCALE, -1e30)
                top = jnp.max(scores, axis=-1, keepdims=True)
                raised = jnp.exp(scores - top)
                weights = raised / jnp.sum(raised, axis=-1, keepdims=True)
                soft[along_x * (HEADS_IN_GROUP * imgs) + head * imgs + img] = weights
                att[along_x, rows, c0 : c0 + 64] = dot(weights.astype(BF16), v).astype(BF16)
        attn[...] += dot_rt(att[along_x], w1[along_x, :, 576:768])
        return carry

    lax.fori_loop(0, 2, step, 0)


def attend_own_kernel(
    imgs, tab, tok, rep, b0, b1, b2, b3,
    vec, bias, start_rows, normed, qb, vb, w1, qkv, soft, att, attn,
):
    low = jnp.zeros((8, D), F32)
    high = jnp.zeros((8, D), F32)
    fill = jnp.zeros((8, D - 128), F32)
    for block in range(BLOCKS):
        place = tab[32 + block]
        piece = jnp.zeros((EXTRA, D), F32)
        for index, part in enumerate((b0, b1, b2, b3)):
            rows = part[place & 3].astype(F32)[BLOCK_ROWS:]
            piece = jnp.where(place >> 2 == index, rows, piece)
        low += pltpu.roll(jnp.concatenate([piece[:, 0:128], fill], 1), block * BLOCK_ROWS, 1)
        high += pltpu.roll(jnp.concatenate([piece[:, 128:256], fill], 1), block * BLOCK_ROWS, 1)
        half = (block % 2) * 384
        bias[block // 2, 0:1, half : half + 384] = piece[0:1, 256:640]
    vec[0:8, :] = low
    vec[8:16, :] = high
    for group in range(GROUPS):
        cols = slice(group * GROUP_COLS, (group + 1) * GROUP_COLS)
        qb[group, 0:1, :] = vec[9:10, cols]
        vb[group, 0:1, :] = vec[10:11, cols]
    assemble(tab, 0, (b0, b1, b2, b3), w1)
    start = mask_rows(tok, rep, vec)
    start_rows[...] = start
    unit, _ = norm_stats(start)
    normed[...] = (unit * vec[0:1, :] + vec[1:2, :]).astype(BF16)
    attn[...] = jnp.zeros_like(attn)
    attend_groups(imgs, tab, 0, normed, qb, vb, w1, qkv, soft, att, attn)


def attend_sib_kernel(
    imgs, tab, vec, start_rows, normed, qb, vb, attn_in, b0, b1, b2, b3,
    w1, qkv, soft, att, attn, mid, normed_two,
):
    assemble(tab, 16, (b0, b1, b2, b3), w1)
    attn[...] = attn_in[...]
    attend_groups(imgs, tab, 1, normed, qb, vb, w1, qkv, soft, att, attn)
    middle = start_rows[...] + vec[4:5, :] * (attn[...] + vec[7:8, :])
    mid[...] = middle
    unit_two, _ = norm_stats(middle)
    normed_two[...] = (unit_two * vec[2:3, :] + vec[3:4, :]).astype(BF16)


def expand_groups(tab, part, normed_two, grad_branch, bias, w2, active, slope, out):
    def step(along_x, carry):
        group = along_x * 2 + (tab[72] ^ part)
        hidden = dot(normed_two[...], w2[along_x]) + bias[group, 0:1, :]
        cdf = 0.5 * (1.0 + lax.erf(hidden * 0.7071067811865476))
        pdf = 0.3989422804014327 * jnp.exp(-0.5 * hidden * hidden)
        act = (hidden * cdf).astype(BF16)
        active[along_x] = act
        slope[along_x] = cdf + hidden * pdf
        put_blocks(tab, group, dot_lt(grad_branch[...], act), out)
        return carry

    lax.fori_loop(0, 2, step, 0)


def expand_own_kernel(
    tab, normed_two, cot, vec, bias, b0, b1, b2, b3, w2, active, slope, grad_branch, out
):
    assemble(tab, 0, (b0, b1, b2, b3), w2)
    grad_branch[...] = (cot[...].astype(F32) * vec[5:6, :]).astype(BF16)
    expand_groups(tab, 0, normed_two, grad_branch, bias, w2, active, slope, out)


def expand_sib_kernel(
    tab, normed_two, grad_branch, bias, b0, b1, b2, b3, w2, active, slope, out
):
    assemble(tab, 16, (b0, b1, b2, b3), w2)
    expand_groups(tab, 1, normed_two, grad_branch, bias, w2, active, slope, out)


def hidden_groups(tab, part, normed_two, grad_branch, slope, w3, grad_hidden, bias_grad, out):
    def step(along_x, carry):
        group = along_x * 2 + (tab[72] ^ part)
        grad = (dot(grad_branch[...], w3[along_x]) * slope[along_x]).astype(BF16)
        grad_hidden[along_x] = grad
        bias_grad[along_x, 0:1, :] = col_sum(grad.astype(F32))
        put_blocks(tab, group, dot_lt(normed_two[...], grad), out)
        return carry

    lax.fori_loop(0, 2, step, 0)


def hidden_kernel(
    part, tab, normed_two, grad_branch, slope, b0, b1, b2, b3, w3, grad_hidden, bias_grad, out
):
    assemble(tab, 16 * part, (b0, b1, b2, b3), w3)
    hidden_groups(tab, part, normed_two, grad_branch, slope, w3, grad_hidden, bias_grad, out)


def middle_kernel(
    act_sib, act_own, hid_sib, hid_own, w2_sib, w2_own, w3_sib, w3_own, mid, attn, cot, vec,
    block_out, grad_mid, grad_attn, sums, branch, grad_two,
):
    sums[...] = jnp.zeros_like(sums)
    found = jnp.zeros(branch.shape, F32)
    for active, w3 in ((act_sib, w3_sib), (act_own, w3_own)):
        for along_x in range(2):
            found += dot_rt(active[along_x], w3[along_x])
    branch[...] = found
    found = jnp.zeros(branch.shape, F32)
    for grad_hidden, w2 in ((hid_sib, w2_sib), (hid_own, w2_own)):
        for along_x in range(2):
            found += dot_rt(grad_hidden[along_x], w2[along_x])
    grad_two[...] = found
    middle = mid[...]
    total = branch[...] + vec[8:9, :]
    block_out[...] = cut_rows(middle + vec[5:6, :] * total)
    grad_out = cot[...].astype(F32)
    sums[5:6, :] = col_sum(grad_out * total)
    sums[8:9, :] = col_sum(grad_out * vec[5:6, :])
    unit, rstd = norm_stats(middle)
    grad = grad_two[...]
    sums[2:3, :] = col_sum(grad * unit)
    sums[3:4, :] = col_sum(grad)
    grad_middle = grad_out + norm_back(grad, vec[2:3, :], unit, rstd)
    grad_mid[...] = grad_middle
    sums[4:5, :] = col_sum(grad_middle * (attn[...] + vec[7:8, :]))
    scaled = grad_middle * vec[4:5, :]
    sums[7:8, :] = col_sum(scaled)
    grad_attn[...] = scaled.astype(BF16)


def back_groups(
    imgs, tab, part, w1, normed, qkv, soft, att, grad_attn, out, grad_one, gqkv, bias_sums
):
    def step(along_x, carry):
        group = along_x * 2 + (tab[72] ^ part)
        grad_att = dot(grad_attn[...], w1[along_x, :, 576:768]).astype(BF16)
        for head in range(HEADS_IN_GROUP):
            c0 = head * HEAD_DIM
            for img in range(imgs):
                rows = slice(img * PAD, (img + 1) * PAD)
                q = qkv[along_x, rows, c0 : c0 + 64]
                k = qkv[along_x, rows, 192 + c0 : 256 + c0]
                v = qkv[along_x, rows, 384 + c0 : 448 + c0]
                weights = soft[along_x * (HEADS_IN_GROUP * imgs) + head * imgs + img]
                grad = grad_att[rows, c0 : c0 + 64]
                grad_soft = dot_rt(grad, v)
                grad_v = dot_lt(weights.astype(BF16), grad)
                inner = jnp.sum(weights * grad_soft, axis=-1, keepdims=True)
                grad_scores = (weights * (grad_soft - inner)).astype(BF16)
                grad_q = dot(grad_scores, k) * SCALE
                grad_k = dot_lt(grad_scores, q) * SCALE
                gqkv[rows, c0 : c0 + 64] = grad_q.astype(BF16)
                gqkv[rows, 192 + c0 : 256 + c0] = grad_k.astype(BF16)
                gqkv[rows, 384 + c0 : 448 + c0] = grad_v.astype(BF16)
        all_grads = gqkv[...]
        bias_sums[along_x, 0:1, :] = col_sum(all_grads[:, 0:192].astype(F32))
        bias_sums[along_x, 1:2, :] = col_sum(all_grads[:, 384:576].astype(F32))
        grad_one[...] += dot_rt(all_grads, w1[along_x, :, 0:576])
        both = jnp.concatenate(
            [dot_lt(normed[...], all_grads), dot_lt(grad_attn[...], att[along_x])], axis=1
        )
        put_blocks(tab, group, both, out)
        return carry

    lax.fori_loop(0, 2, step, 0)


def back_sib_kernel(
    imgs, tab, w1, normed, qkv, soft, att, grad_attn, out, grad_one, bias_sums, gqkv
):
    grad_one[...] = jnp.zeros_like(grad_one)
    back_groups(
        imgs, tab, 1, w1, normed, qkv, soft, att, grad_attn, out, grad_one, gqkv, bias_sums
    )


def back_own_kernel(
    imgs, tab, w1, normed, qkv, soft, att, grad_attn, grad_one_in, out, grad_one, bias_sums, gqkv
):
    grad_one[...] = grad_one_in[...]
    back_groups(
        imgs, tab, 0, w1, normed, qkv, soft, att, grad_attn, out, grad_one, gqkv, bias_sums
    )


def start_kernel(
    tab, tok, rep, vec, grad_one, bias_sib, bias_own, grad_mid, sums_in, units_sib, units_own,
    tok_grad, sums,
):
    replaced = rep[...]
    unit, rstd = norm_stats(mask_rows(tok, rep, vec))
    grad = grad_one[...]
    sums[0:16, :] = sums_in[...]
    sums[16:24, :] = jnp.zeros((8, D), F32)
    sums[0:1, :] = col_sum(grad * unit)
    sums[1:2, :] = col_sum(grad)
    grad_start = grad_mid[...] + norm_back(grad, vec[0:1, :], unit, rstd)
    tok_grad[...] = cut_rows(grad_start * (1.0 - replaced))
    sums[6:7, :] = col_sum(grad_start * replaced)
    for group in range(GROUPS):
        cols = slice(group * GROUP_COLS, (group + 1) * GROUP_COLS)
        own = tab[72] == group % 2
        along_x = group // 2
        both = jnp.where(own, bias_own[along_x], bias_sib[along_x])
        sums[9:10, cols] = both[0:1]
        sums[10:11, cols] = both[1:2]
        sums[16 + group : 17 + group, :] = jnp.where(own, units_own[along_x], units_sib[along_x])


def adam_update(weight, gradient, first_moment, second, step_rate, decay_rate):
    moment = BETA_ONE * first_moment + (1.0 - BETA_ONE) * gradient
    square = BETA_TWO * second + (1.0 - BETA_TWO) * gradient * gradient
    first_hat = moment / (1.0 - BETA_ONE**STEP)
    second_hat = square / (1.0 - BETA_TWO**STEP)
    updated = weight - step_rate * (
        first_hat / (jnp.sqrt(second_hat) + EPSILON) + decay_rate * weight
    )
    return (updated, moment, square)


def finish_kernel(
    partial, last, qkv, first_qkv, second_qkv, out, first_out, second_out, *results
):
    grad = partial[...] + last[...].astype(F32)
    for index in range(3):
        cols = slice(index * GROUP_COLS, (index + 1) * GROUP_COLS)
        found = adam_update(
            qkv[index], grad[:, cols], first_qkv[index], second_qkv[index], RATE_MATRIX, DECAY
        )
        for result, values in zip(results[:3], found, strict=True):
            result[index] = values
    found = adam_update(
        out[...], grad[:, 576:768].T, first_out[...], second_out[...], RATE_MATRIX, DECAY
    )
    for result, values in zip(results[3:], found, strict=True):
        result[...] = values


VMEM = pl.BlockSpec(memory_space=pltpu.VMEM)
SMEM = pl.BlockSpec(memory_space=pltpu.SMEM)


def shape(dims, dtype=BF16):
    return jax.ShapeDtypeStruct(dims, dtype)


def call(kernel, args, outs, scratch=(), flops=SHORT, megabytes=10, table=True):
    return pl.pallas_call(
        kernel,
        out_shape=outs,
        in_specs=[SMEM] * table + [VMEM] * (len(args) - table),
        out_specs=[VMEM] * len(outs),
        scratch_shapes=list(scratch),
        cost_estimate=pl.CostEstimate(flops=flops, bytes_accessed=1, transcendentals=0),
        compiler_params=pltpu.CompilerParams(vmem_limit_bytes=megabytes << 20),
    )(*args)


def after(value, *earlier):
    return lax.optimization_barrier((value, earlier))[0]


def fence(*earlier):
    mark = after(jnp.zeros((8, 128), F32), *earlier)
    return call(fence_kernel, (mark,), (shape((8, 128), F32),), flops=LONG, table=False)[0]


def send_across(values, mask):
    return lax.ppermute(values, AXES, [(dev, dev ^ mask) for dev in range(32)])


def add_across(values, mask):
    return values + send_across(values, mask)


class Gather:
    def __init__(self, block, orders, spread):
        self.held = block[None]
        self.orders = orders
        self.level = 0
        self.spread = spread

    def send(self, values, level):
        return lax.ppermute(values, AXES, pairs_of(self.orders, level))

    def start(self, *earlier):
        if earlier:
            self.held = after(self.held, *earlier)
        if self.level == 0 and self.spread:
            self.taken = [
                lax.ppermute(self.held, AXES, partners_of(self.orders, place))
                for place in (1, 2, 3)
            ]
            self.level = 1
        elif self.level < 3:
            self.taken = [self.send(self.held, self.level)]
            if self.level == 2:
                self.far = self.send(self.held, 3)
        else:
            self.last = self.send(self.held, 3)
        self.level += 1

    def take(self):
        if self.level < 3:
            self.held = jnp.concatenate([self.held, *self.taken], axis=0)
            return self.taken
        if self.level == 3:
            self.near = self.held
            (self.taken,) = self.taken
            self.held = self.taken
            return self.taken, self.far
        return self.last

    def finish(self, *earlier):
        while self.level < 4:
            self.taken = after(self.taken, *earlier)
            self.take()
            self.start()

    def own(self):
        return self.near, self.taken, self.far, self.last

    def sib(self, *earlier):
        own = self.near, self.taken, self.far, after(self.last, *earlier)
        return tuple(lax.ppermute(values, AXES, CORE_PAIRS) for values in own)


class Scatter:
    def __init__(self, orders):
        self.orders = orders
        self.level = 4
        self.terms = []

    def swap(self, sib):
        self.terms.append(lax.ppermute(sib, AXES, CORE_PAIRS))

    def add(self, own):
        self.terms.insert(0, own)

    def total(self, low, high):
        return sum(term[low:high].astype(F32) for term in self.terms)

    def step(self, *earlier):
        self.level -= 1
        size = 1 << self.level
        if earlier:
            self.terms[-1] = after(self.terms[-1], *earlier)
        sent = self.total(size, 2 * size).astype(BF16)
        self.terms.append(lax.ppermute(sent, AXES, pairs_of(self.orders, self.level)))
        return sent

    def spread(self, *earlier):
        if earlier:
            self.hold(*earlier)
        sent = [self.total(place, place + 1).astype(BF16) for place in (1, 2, 3)]
        for place, values in zip((1, 2, 3), sent, strict=True):
            self.terms.append(lax.ppermute(values, AXES, partners_of(self.orders, place)))
        return sent

    def hold(self, *earlier):
        self.terms[-1] = after(self.terms[-1], *earlier)

    def result(self):
        return self.total(0, 1)[0]


def gather_plain(block):
    whole = lax.all_gather(block, AXES, axis=0, tiled=False)
    whole = whole.reshape(-1, GROUPS, *block.shape).transpose(1, 0, 2, 3)
    whole = whole.reshape(2, 2, BLOCKS, BLOCK_ROWS, D).transpose(1, 0, 2, 3, 4)
    whole = whole.reshape(2, 4, 4, BLOCK_ROWS, D)
    return tuple(tuple(part[index] for index in range(4)) for part in whole)


def scatter_plain(own, sib, n_dp):
    parts = jnp.stack([own, sib]).reshape(2, BLOCKS, 2, BLOCK_ROWS, D)
    whole = parts.transpose(1, 3, 2, 0, 4).reshape(D, GROUPS, D).astype(F32)
    whole = whole.reshape(n_dp, D // n_dp, GROUPS, D).transpose(0, 2, 1, 3)
    whole = whole.reshape(n_dp * GROUPS, D // n_dp, D)
    return lax.psum_scatter(whole, AXES, scatter_dimension=0, tiled=True)[0]


def on_device(
    n_dp,
    tokens,
    patch_mask,
    cotangent,
    project_qkv,
    first_qkv,
    second_qkv,
    project_out,
    first_out,
    second_out,
    expand_weight,
    first_expand,
    second_expand,
    reduce_weight,
    first_reduce,
    second_reduce,
    vectors,
    first_vectors,
    second_vectors,
    expand_bias,
    first_bias,
    second_bias,
):
    direct = n_dp == BLOCKS
    imgs = patch_mask.shape[0]
    rows = imgs * PAD
    wide = vectors.shape[1]
    units = expand_bias.shape[0]

    def padded(values):
        values = values.reshape(imgs, SEQ, -1)
        return jnp.pad(values, ((0, 0), (0, PAD - SEQ), (0, 0))).reshape(rows, -1)

    positions = lax.broadcasted_iota(jnp.int32, patch_mask.shape, 1)
    replaced = jnp.where((patch_mask == 1) & (positions > 0), 1.0, 0.0).astype(F32)
    rep = padded(replaced)

    def pad_rows(values):
        return call(pad_kernel, (values,), (shape((rows, D)),), flops=LONG, table=False)[0]

    piece_two = expand_weight.astype(BF16)
    piece_three = reduce_weight.astype(BF16).T
    if direct:
        flat = lax.axis_index("dp") * GROUPS + lax.axis_index("tensor")
        chosen = zip(GATHER, (SCATTER[0], SCATTER[2], SCATTER[1]), strict=True)
        every = np.concatenate([build_table(g, s) for g, s in chosen], axis=1)
        table = lax.dynamic_index_in_dim(jnp.asarray(every), flat, 0, keepdims=False)
        tables = [table[0:80], table[80:160], table[160:240]]
        (piece_one,) = call(
            pack_kernel,
            (project_qkv, project_out, vectors, expand_bias),
            (shape((BLOCK_ROWS + EXTRA, D)),),
            table=False,
        )
        streams = [
            Gather(piece, orders, spread)
            for piece, orders, spread in zip(
                (piece_one, piece_two, piece_three), GATHER, SPREAD, strict=True
            )
        ]
        seen = {}
        for kind, index in zip(STEPS[0::2], STEPS[1::2], strict=True):
            stream = streams[int(index)]
            held = [stream.held for stream in streams]
            if kind == "X":
                seen["mark"] = fence(*held, *seen.values())
            elif kind == "F":
                if index == "0":
                    tok = pad_rows(after(tokens, *held[:2]))
                    seen["tok"] = (tok, rep, *tables)
                else:
                    cot = pad_rows(after(cotangent, held[1]))
                    seen["cot"] = cot
            elif kind == "S":
                stream.start(*seen.values())
            else:
                seen[index] = stream.take()
        marks = [seen[name] for name in seen if name not in "12"]
        w1_own, w1_sib = streams[0].own(), streams[0].sib(*marks)
    else:
        tables = [jnp.asarray(plain_table())] * 3
        tok, cot = pad_rows(tokens), pad_rows(cotangent)
        piece_one = jnp.concatenate(
            [project_qkv[0], project_qkv[1], project_qkv[2], project_out.T], axis=1
        ).astype(BF16)
        w1_parts, (w2_own, w2_sib), (w3_own, w3_sib) = (
            gather_plain(piece) for piece in (piece_one, piece_two, piece_three)
        )
        vector_all = lax.all_gather(vectors.astype(BF16), "dp", axis=1, tiled=True)
        bias_all = lax.all_gather(expand_bias.astype(BF16), "dp", axis=0, tiled=True)
        by_block = vector_all.reshape(11, BLOCKS, BLOCK_ROWS).transpose(1, 0, 2)
        extras = jnp.zeros((BLOCKS, EXTRA, D), BF16)
        extras = extras.at[:, :, 0:BLOCK_ROWS].set(by_block[:, 0:8])
        extras = extras.at[:, 0:3, 128 : 128 + BLOCK_ROWS].set(by_block[:, 8:11])
        extras = extras.at[:, 0, 256:640].set(bias_all.reshape(BLOCKS, FF // BLOCKS))
        w1_own, w1_sib = (
            tuple(
                jnp.concatenate([part, extras[4 * (at % 2) : 4 * (at % 2) + 4]], axis=1)
                for at, part in enumerate(parts)
            )
            for parts in w1_parts
        )

    full = (GROUPS, D, D)
    row_f32 = shape((rows, D), F32)
    row_low = shape((rows, D))
    half = shape((16, BLOCK_ROWS, D))
    two_low = shape((2, rows, D))
    two_f32 = shape((2, rows, D), F32)
    two_bias = shape((2, 1, D), F32)
    group_bias = shape((GROUPS, 1, GROUP_COLS), F32)
    weights = shape((2, D, D))
    heads = (
        shape((2, rows, 3 * GROUP_COLS)),
        shape((2 * HEADS_IN_GROUP * imgs, PAD, PAD), F32),
        shape((2, rows, GROUP_COLS)),
        row_f32,
    )
    vec, bias, start_rows, normed, qb, vb, w1_own, *heads_own, attn = call(
        functools.partial(attend_own_kernel, imgs),
        (tables[0], tok, rep, *w1_own),
        (
            shape((16, D), F32), shape((GROUPS, 1, D), F32), row_f32, row_low,
            group_bias, group_bias, weights, *heads,
        ),
        flops=SHORT,
    )
    w1_sib, *heads_sib, attn, mid, normed_two = call(
        functools.partial(attend_sib_kernel, imgs),
        (tables[0], vec, start_rows, normed, qb, vb, attn, *w1_sib),
        (weights, *heads, row_f32, row_low),
        flops=SHORT,
    )
    if direct:
        streams[1].finish(normed)
        w2_own, w2_sib = streams[1].own(), streams[1].sib(normed_two)
    three, two, one = (Scatter(SCATTER[index]) for index in (2, 1, 0))
    w2_own, act_own, slope_own, grad_branch, reduce_own = call(
        expand_own_kernel,
        (tables[1], normed_two, cot, vec, bias, *w2_own),
        (weights, two_low, two_f32, row_low, half),
        flops=LONG,
    )
    if direct:
        streams[2].finish(grad_branch)
    w2_sib, act_sib, slope_sib, reduce_sib = call(
        expand_sib_kernel,
        (tables[1], normed_two, grad_branch, bias, *w2_sib),
        (weights, two_low, two_f32, half),
        flops=SHORT,
    )
    if direct:
        three.swap(reduce_sib)
        w3_own, w3_sib = streams[2].own(), streams[2].sib(reduce_sib)
    w3_sib, hid_sib, units_sib, expand_sib = call(
        functools.partial(hidden_kernel, 1),
        (tables[2], normed_two, grad_branch, slope_sib, *w3_sib),
        (weights, two_low, two_bias, half),
        flops=LONG,
    )
    if direct:
        two.swap(expand_sib)
        three.add(reduce_own)
        slope_own = after(slope_own, three.step(expand_sib))
    w3_own, hid_own, units_own, expand_own = call(
        functools.partial(hidden_kernel, 0),
        (tables[2], normed_two, grad_branch, slope_own, *w3_own),
        (weights, two_low, two_bias, half),
        flops=LONG,
    )
    if direct:
        two.add(expand_own)
        mid = after(mid, two.step())
    block_out, grad_mid, grad_attn, sums = call(
        middle_kernel,
        (
            act_sib, act_own, hid_sib, hid_own, w2_sib, w2_own, w3_sib, w3_own,
            mid, attn, cot, vec,
        ),
        (shape(tokens.shape), row_f32, row_low, shape((16, D), F32)),
        (pltpu.VMEM((rows, D), F32), pltpu.VMEM((rows, D), F32)),
        flops=SHORT,
        table=False,
    )
    held = pltpu.VMEM((rows, 3 * GROUP_COLS), BF16)
    bias_sums = (2, 2, GROUP_COLS)
    first_sib, grad_one, bias_sib = call(
        functools.partial(back_sib_kernel, imgs),
        (tables[0], w1_sib, normed, *heads_sib, grad_attn),
        (half, row_f32, shape(bias_sums, F32)),
        (held,),
        flops=SHORT,
    )
    if direct:
        one.swap(first_sib)
        grad_one = after(grad_one, three.step(grad_one))
    first_own, grad_one, bias_own = call(
        functools.partial(back_own_kernel, imgs),
        (tables[0], w1_own, normed, *heads_own, grad_attn, grad_one),
        (half, row_f32, shape(bias_sums, F32)),
        (held,),
        flops=LONG,
    )
    if direct:
        first_own, grad_one = after((first_own, grad_one), three.terms[-1])
        one.add(first_own)
        sent = one.step()
        sent_three, sent_two = three.step(sent), two.step(sent)
        grad_one = after(grad_one, sent)
    tok_grad, sums = call(
        start_kernel,
        (
            tables[0], tok, rep, vec, grad_one, bias_sib, bias_own, grad_mid, sums,
            units_sib, units_own,
        ),
        (shape(tokens.shape), shape((24, D), F32)),
    )

    if direct:
        sums = add_across(sums, 1)
        one.hold(fence(sums, sent_three, sent_two))
        part = send_across(sums, 2)
        sent = one.step()
        sums = sums + after(part, sent)
        part = send_across(sums, 16)
        three.step(sent)
        two.step(sent)
        sent = one.spread()
        sums = sums + after(part, sent)
        part = send_across(sums, 8)
        two.step(sent)
        sums = add_across(sums + after(part, sent), 4)
        grad_three = three.result()
        states_three = adam_update(
            reduce_weight, grad_three.T, first_reduce, second_reduce, RATE_MATRIX, DECAY
        )
        two.hold(sent)
        grad_two = two.result()
        partial = sum(term[0].astype(F32) for term in one.terms[:-1])
        finished = call(
            finish_kernel,
            (
                partial, one.terms[-1][0], project_qkv, first_qkv, second_qkv,
                project_out, first_out, second_out,
            ),
            (shape(project_qkv.shape, F32),) * 3 + (shape(project_out.shape, F32),) * 3,
            table=False,
        )
    else:
        grad_three = scatter_plain(reduce_own, reduce_sib, n_dp)
        grad_two = scatter_plain(expand_own, expand_sib, n_dp)
        grad_one = scatter_plain(first_own, first_sib, n_dp)
        sums = lax.psum(sums, AXES)
        grad_qkv = jnp.stack([grad_one[:, i * GROUP_COLS : (i + 1) * GROUP_COLS] for i in range(3)])
        grad_out = grad_one[:, 3 * GROUP_COLS :].T
        states_three = adam_update(
            reduce_weight, grad_three.T, first_reduce, second_reduce, RATE_MATRIX, DECAY
        )
        finished = (
            *adam_update(project_qkv, grad_qkv, first_qkv, second_qkv, RATE_MATRIX, DECAY),
            *adam_update(project_out, grad_out, first_out, second_out, RATE_MATRIX, DECAY),
        )
    spot = lax.axis_index("dp")
    vector_grad = lax.dynamic_slice_in_dim(sums[0:11], spot * wide, wide, 1)
    grad_bias = lax.dynamic_slice_in_dim(sums[16:20].reshape(-1), spot * units, units, 0)
    return (
        block_out,
        tok_grad,
        *finished,
        *adam_update(expand_weight, grad_two, first_expand, second_expand, RATE_MATRIX, DECAY),
        *states_three,
        *adam_update(vectors, vector_grad, first_vectors, second_vectors, RATE_VECTOR, 0.0),
        *adam_update(expand_bias, grad_bias, first_bias, second_bias, RATE_VECTOR, 0.0),
    )


def solution(mesh):
    rows = P(AXES, None)
    states = (
        *(P(None, "dp", "tensor"),) * 3,
        *(P("tensor", "dp"),) * 3,
        *(P("dp", "tensor"),) * 3,
        *(P("tensor", "dp"),) * 3,
        *(P(None, "dp"),) * 3,
        *(P("dp"),) * 3,
    )
    return jax.shard_map(
        functools.partial(on_device, mesh.shape["dp"]),
        mesh=mesh,
        in_specs=(rows, rows, rows, *states),
        out_specs=(rows, rows, *states),
        check_vma=False,
    )
```

```python
import functools

import jax
import jax.numpy as jnp
import numpy as np
from jax import lax
from jax.experimental import pallas as pl
from jax.experimental.pallas import tpu as pltpu
from jax.sharding import PartitionSpec as P

D = 768
HEAD_DIM = 64
FF = 3072
SEQ = 197
STEP = 4
BETA_ONE = 0.5
BETA_TWO = 0.5
EPSILON = 1e-08
DECAY = 0.05
RATE_MATRIX = 0.02
RATE_VECTOR = 0.2
NORM_EPS = 1e-06

AXES = ("dp", "tensor")
PAD = 208
GROUPS = 4
GROUP_COLS = D // GROUPS
HEADS_IN_GROUP = GROUP_COLS // HEAD_DIM
BLOCKS = 8
BLOCK_ROWS = D // BLOCKS
EXTRA = 8
SCALE = HEAD_DIM**-0.5
SHORT = 1
LONG = 10**11
F32 = jnp.float32
BF16 = jnp.bfloat16

BIT = {"c": 1, "x": 2, "y": 4, "1": 8, "2": 16}
GATHER = (("21xy", "12yx"), ("2y1x", "yx21"), ("y21x", "1x2y"))
SCATTER = (("21yx", "12xy"), ("2x1y", "x21y"), ("y2x1", "y21x"))
STEPS = "S0S1S2D1S1D0S0D2S2F0D1S1D0S0D2S2D1S1F1D0"
SPREAD = (True, False, False)


def offset_of(order, place):
    found = 0
    for level in range(4):
        if place >> level & 1:
            found ^= BIT[order[level]]
    return found


def pairs_of(orders, level):
    return [(dev, dev ^ BIT[orders[dev & 1][level]]) for dev in range(32)]


def partners_of(orders, place):
    return [(dev, dev ^ offset_of(orders[dev & 1], place)) for dev in range(32)]


CORE_PAIRS = [(dev, dev ^ 1) for dev in range(32)]


def build_table(gather, scatter):
    table = np.zeros((32, 80), np.int32)
    for dev in range(32):
        core = dev & 1
        for place in range(16):
            table[dev, place] = dev ^ offset_of(gather[core], place)
            table[dev, 16 + place] = dev ^ 1 ^ offset_of(gather[1 - core], place)
            mine = dev ^ offset_of(gather[core], place)
            if mine & 3 == dev & 3:
                table[dev, 32 + (mine >> 2)] = place
            table[dev, 40 + (dev ^ offset_of(scatter[core], place))] = place
            table[dev, 40 + (dev ^ 1 ^ offset_of(scatter[1 - core], place))] = place
        table[dev, 72] = core
    return table


def plain_table():
    table = np.zeros((80,), np.int32)
    for place in range(32):
        part, along_x, block = place // 16, place // 8 % 2, place % 8
        table[place] = block * 4 + along_x * 2 + part
    for block in range(8):
        table[32 + block] = block
        for group in range(4):
            table[40 + block * 4 + group] = block * 2 + group // 2
    return table


def dot(left, right):
    return jnp.dot(left, right, preferred_element_type=F32)


def dot_rt(left, right):
    return lax.dot_general(left, right, (((1,), (1,)), ((), ())), preferred_element_type=F32)


def dot_lt(left, right):
    return lax.dot_general(left, right, (((0,), (0,)), ((), ())), preferred_element_type=F32)


def norm_stats(values):
    mean = jnp.mean(values, axis=-1, keepdims=True)
    centred = values - mean
    var = jnp.mean(centred * centred, axis=-1, keepdims=True)
    rstd = lax.rsqrt(var + NORM_EPS)
    return centred * rstd, rstd


def norm_back(grad, gain, unit, rstd):
    grad_unit = grad * gain
    first = jnp.mean(grad_unit, axis=-1, keepdims=True)
    second = jnp.mean(grad_unit * unit, axis=-1, keepdims=True)
    return rstd * (grad_unit - first - unit * second)


def col_sum(values):
    return jnp.sum(values, axis=0, keepdims=True)


def assemble(tab, first, parts, whole):
    for index, part in enumerate(parts):
        for place in range(4):
            owner = tab[first + index * 4 + place]
            row = pl.multiple_of((owner >> 2) * BLOCK_ROWS, BLOCK_ROWS)
            whole[(owner >> 1) & 1, pl.ds(row, BLOCK_ROWS), :] = part[place, 0:BLOCK_ROWS, :]


def put_blocks(tab, group, grad, out):
    for block in range(BLOCKS):
        place = tab[40 + block * 4 + group]
        rows = slice(block * BLOCK_ROWS, (block + 1) * BLOCK_ROWS)
        out[place] = grad[rows].astype(BF16)


def mask_rows(tok, rep, vec):
    replaced = rep[...]
    return tok[...].astype(F32) * (1.0 - replaced) + vec[6:7, :] * replaced


def pad_kernel(values, out):
    wide = values[...].astype(F32)
    gap = jnp.zeros((PAD - SEQ, D), F32)
    rows = []
    for start in range(0, wide.shape[0], SEQ):
        rows += [wide[start : start + SEQ], gap]
    out[...] = jnp.concatenate(rows, axis=0).astype(BF16)


def cut_rows(wide):
    rows = [wide[start : start + SEQ] for start in range(0, wide.shape[0], PAD)]
    return jnp.concatenate(rows, axis=0).astype(BF16)


def fence_kernel(values, out):
    out[...] = values[...] + 1.0


def pack_kernel(project_qkv, project_out, vectors, expand_bias, out):
    columns = [project_qkv[0], project_qkv[1], project_qkv[2], project_out[...].T]
    block = jnp.concatenate(columns, axis=1)
    fill = jnp.zeros((EXTRA, 128 - BLOCK_ROWS), F32)
    low = jnp.concatenate([vectors[0:8, :], fill], axis=1)
    high = jnp.concatenate([vectors[8:11, :], jnp.zeros((5, BLOCK_ROWS), F32)], axis=0)
    high = jnp.concatenate([high, fill], axis=1)
    last = jnp.concatenate([expand_bias[...].reshape(1, 384), jnp.zeros((EXTRA - 1, 384), F32)], axis=0)
    extra = jnp.concatenate([low, high, last, jnp.zeros((EXTRA, 128), F32)], axis=1)
    out[...] = jnp.concatenate([block, extra], axis=0).astype(BF16)


def attend_groups(imgs, tab, part, normed, qb, vb, w1, qkv, soft, att, attn):
    keep = lax.broadcasted_iota(jnp.int32, (PAD, PAD), 1) < SEQ

    def step(along_x, carry):
        group = along_x * 2 + (tab[72] ^ part)
        result = dot(normed[...], w1[along_x, :, 0:576])
        qkv[along_x, :, 0:192] = (result[:, 0:192] + qb[group, 0:1, :]).astype(BF16)
        qkv[along_x, :, 192:384] = result[:, 192:384].astype(BF16)
        qkv[along_x, :, 384:576] = (result[:, 384:576] + vb[group, 0:1, :]).astype(BF16)
        for head in range(HEADS_IN_GROUP):
            c0 = head * HEAD_DIM
            for img in range(imgs):
                rows = slice(img * PAD, (img + 1) * PAD)
                q = qkv[along_x, rows, c0 : c0 + 64]
                k = qkv[along_x, rows, 192 + c0 : 256 + c0]
                v = qkv[along_x, rows, 384 + c0 : 448 + c0]
                scores = jnp.where(keep, dot_rt(q, k) * SCALE, -1e30)
                top = jnp.max(scores, axis=-1, keepdims=True)
                raised = jnp.exp(scores - top)
                weights = raised / jnp.sum(raised, axis=-1, keepdims=True)
                soft[along_x * (HEADS_IN_GROUP * imgs) + head * imgs + img] = weights
                att[along_x, rows, c0 : c0 + 64] = dot(weights.astype(BF16), v).astype(BF16)
        attn[...] += dot_rt(att[along_x], w1[along_x, :, 576:768])
        return carry

    lax.fori_loop(0, 2, step, 0)


def attend_own_kernel(
    imgs, tab, tok, rep, b0, b1, b2, b3,
    vec, bias, start_rows, normed, qb, vb, w1, qkv, soft, att, attn,
):
    low = jnp.zeros((8, D), F32)
    high = jnp.zeros((8, D), F32)
    fill = jnp.zeros((8, D - 128), F32)
    for block in range(BLOCKS):
        place = tab[32 + block]
        piece = jnp.zeros((EXTRA, D), F32)
        for index, part in enumerate((b0, b1, b2, b3)):
            rows = part[place & 3].astype(F32)[BLOCK_ROWS:]
            piece = jnp.where(place >> 2 == index, rows, piece)
        low += pltpu.roll(jnp.concatenate([piece[:, 0:128], fill], 1), block * BLOCK_ROWS, 1)
        high += pltpu.roll(jnp.concatenate([piece[:, 128:256], fill], 1), block * BLOCK_ROWS, 1)
        half = (block % 2) * 384
        bias[block // 2, 0:1, half : half + 384] = piece[0:1, 256:640]
    vec[0:8, :] = low
    vec[8:16, :] = high
    for group in range(GROUPS):
        cols = slice(group * GROUP_COLS, (group + 1) * GROUP_COLS)
        qb[group, 0:1, :] = vec[9:10, cols]
        vb[group, 0:1, :] = vec[10:11, cols]
    assemble(tab, 0, (b0, b1, b2, b3), w1)
    start = mask_rows(tok, rep, vec)
    start_rows[...] = start
    unit, _ = norm_stats(start)
    normed[...] = (unit * vec[0:1, :] + vec[1:2, :]).astype(BF16)
    attn[...] = jnp.zeros_like(attn)
    attend_groups(imgs, tab, 0, normed, qb, vb, w1, qkv, soft, att, attn)


def attend_sib_kernel(
    imgs, tab, vec, start_rows, normed, qb, vb, attn_in, b0, b1, b2, b3,
    w1, qkv, soft, att, attn, mid, normed_two,
):
    assemble(tab, 16, (b0, b1, b2, b3), w1)
    attn[...] = attn_in[...]
    attend_groups(imgs, tab, 1, normed, qb, vb, w1, qkv, soft, att, attn)
    middle = start_rows[...] + vec[4:5, :] * (attn[...] + vec[7:8, :])
    mid[...] = middle
    unit_two, _ = norm_stats(middle)
    normed_two[...] = (unit_two * vec[2:3, :] + vec[3:4, :]).astype(BF16)


def expand_groups(tab, part, normed_two, grad_branch, bias, w2, active, slope, out):
    def step(along_x, carry):
        group = along_x * 2 + (tab[72] ^ part)
        hidden = dot(normed_two[...], w2[along_x]) + bias[group, 0:1, :]
        cdf = 0.5 * (1.0 + lax.erf(hidden * 0.7071067811865476))
        pdf = 0.3989422804014327 * jnp.exp(-0.5 * hidden * hidden)
        act = (hidden * cdf).astype(BF16)
        active[along_x] = act
        slope[along_x] = cdf + hidden * pdf
        put_blocks(tab, group, dot_lt(grad_branch[...], act), out)
        return carry

    lax.fori_loop(0, 2, step, 0)


def expand_own_kernel(
    tab, normed_two, cot, vec, bias, b0, b1, b2, b3, w2, active, slope, grad_branch, out
):
    assemble(tab, 0, (b0, b1, b2, b3), w2)
    grad_branch[...] = (cot[...].astype(F32) * vec[5:6, :]).astype(BF16)
    expand_groups(tab, 0, normed_two, grad_branch, bias, w2, active, slope, out)


def expand_sib_kernel(
    tab, normed_two, grad_branch, bias, b0, b1, b2, b3, w2, active, slope, out
):
    assemble(tab, 16, (b0, b1, b2, b3), w2)
    expand_groups(tab, 1, normed_two, grad_branch, bias, w2, active, slope, out)


def hidden_groups(tab, part, normed_two, grad_branch, slope, w3, grad_hidden, bias_grad, out):
    def step(along_x, carry):
        group = along_x * 2 + (tab[72] ^ part)
        grad = (dot(grad_branch[...], w3[along_x]) * slope[along_x]).astype(BF16)
        grad_hidden[along_x] = grad
        bias_grad[along_x, 0:1, :] = col_sum(grad.astype(F32))
        put_blocks(tab, group, dot_lt(normed_two[...], grad), out)
        return carry

    lax.fori_loop(0, 2, step, 0)


def hidden_kernel(
    part, tab, normed_two, grad_branch, slope, b0, b1, b2, b3, w3, grad_hidden, bias_grad, out
):
    assemble(tab, 16 * part, (b0, b1, b2, b3), w3)
    hidden_groups(tab, part, normed_two, grad_branch, slope, w3, grad_hidden, bias_grad, out)


def middle_kernel(
    act_sib, act_own, hid_sib, hid_own, w2_sib, w2_own, w3_sib, w3_own, mid, attn, cot, vec,
    block_out, grad_mid, grad_attn, sums, branch, grad_two,
):
    sums[...] = jnp.zeros_like(sums)
    found = jnp.zeros(branch.shape, F32)
    for active, w3 in ((act_sib, w3_sib), (act_own, w3_own)):
        for along_x in range(2):
            found += dot_rt(active[along_x], w3[along_x])
    branch[...] = found
    found = jnp.zeros(branch.shape, F32)
    for grad_hidden, w2 in ((hid_sib, w2_sib), (hid_own, w2_own)):
        for along_x in range(2):
            found += dot_rt(grad_hidden[along_x], w2[along_x])
    grad_two[...] = found
    middle = mid[...]
    total = branch[...] + vec[8:9, :]
    block_out[...] = cut_rows(middle + vec[5:6, :] * total)
    grad_out = cot[...].astype(F32)
    sums[5:6, :] = col_sum(grad_out * total)
    sums[8:9, :] = col_sum(grad_out * vec[5:6, :])
    unit, rstd = norm_stats(middle)
    grad = grad_two[...]
    sums[2:3, :] = col_sum(grad * unit)
    sums[3:4, :] = col_sum(grad)
    grad_middle = grad_out + norm_back(grad, vec[2:3, :], unit, rstd)
    grad_mid[...] = grad_middle
    sums[4:5, :] = col_sum(grad_middle * (attn[...] + vec[7:8, :]))
    scaled = grad_middle * vec[4:5, :]
    sums[7:8, :] = col_sum(scaled)
    grad_attn[...] = scaled.astype(BF16)


def back_groups(
    imgs, tab, part, w1, normed, qkv, soft, att, grad_attn, out, grad_one, gqkv, bias_sums
):
    def step(along_x, carry):
        group = along_x * 2 + (tab[72] ^ part)
        grad_att = dot(grad_attn[...], w1[along_x, :, 576:768]).astype(BF16)
        for head in range(HEADS_IN_GROUP):
            c0 = head * HEAD_DIM
            for img in range(imgs):
                rows = slice(img * PAD, (img + 1) * PAD)
                q = qkv[along_x, rows, c0 : c0 + 64]
                k = qkv[along_x, rows, 192 + c0 : 256 + c0]
                v = qkv[along_x, rows, 384 + c0 : 448 + c0]
                weights = soft[along_x * (HEADS_IN_GROUP * imgs) + head * imgs + img]
                grad = grad_att[rows, c0 : c0 + 64]
                grad_soft = dot_rt(grad, v)
                grad_v = dot_lt(weights.astype(BF16), grad)
                inner = jnp.sum(weights * grad_soft, axis=-1, keepdims=True)
                grad_scores = (weights * (grad_soft - inner)).astype(BF16)
                grad_q = dot(grad_scores, k) * SCALE
                grad_k = dot_lt(grad_scores, q) * SCALE
                gqkv[rows, c0 : c0 + 64] = grad_q.astype(BF16)
                gqkv[rows, 192 + c0 : 256 + c0] = grad_k.astype(BF16)
                gqkv[rows, 384 + c0 : 448 + c0] = grad_v.astype(BF16)
        all_grads = gqkv[...]
        bias_sums[along_x, 0:1, :] = col_sum(all_grads[:, 0:192].astype(F32))
        bias_sums[along_x, 1:2, :] = col_sum(all_grads[:, 384:576].astype(F32))
        grad_one[...] += dot_rt(all_grads, w1[along_x, :, 0:576])
        both = jnp.concatenate(
            [dot_lt(normed[...], all_grads), dot_lt(grad_attn[...], att[along_x])], axis=1
        )
        put_blocks(tab, group, both, out)
        return carry

    lax.fori_loop(0, 2, step, 0)


def back_sib_kernel(
    imgs, tab, w1, normed, qkv, soft, att, grad_attn, out, grad_one, bias_sums, gqkv
):
    grad_one[...] = jnp.zeros_like(grad_one)
    back_groups(
        imgs, tab, 1, w1, normed, qkv, soft, att, grad_attn, out, grad_one, gqkv, bias_sums
    )


def back_own_kernel(
    imgs, tab, w1, normed, qkv, soft, att, grad_attn, grad_one_in, out, grad_one, bias_sums, gqkv
):
    grad_one[...] = grad_one_in[...]
    back_groups(
        imgs, tab, 0, w1, normed, qkv, soft, att, grad_attn, out, grad_one, gqkv, bias_sums
    )


def start_kernel(
    tab, tok, rep, vec, grad_one, bias_sib, bias_own, grad_mid, sums_in, units_sib, units_own,
    tok_grad, sums,
):
    replaced = rep[...]
    unit, rstd = norm_stats(mask_rows(tok, rep, vec))
    grad = grad_one[...]
    sums[0:16, :] = sums_in[...]
    sums[16:24, :] = jnp.zeros((8, D), F32)
    sums[0:1, :] = col_sum(grad * unit)
    sums[1:2, :] = col_sum(grad)
    grad_start = grad_mid[...] + norm_back(grad, vec[0:1, :], unit, rstd)
    tok_grad[...] = cut_rows(grad_start * (1.0 - replaced))
    sums[6:7, :] = col_sum(grad_start * replaced)
    for group in range(GROUPS):
        cols = slice(group * GROUP_COLS, (group + 1) * GROUP_COLS)
        own = tab[72] == group % 2
        along_x = group // 2
        both = jnp.where(own, bias_own[along_x], bias_sib[along_x])
        sums[9:10, cols] = both[0:1]
        sums[10:11, cols] = both[1:2]
        sums[16 + group : 17 + group, :] = jnp.where(own, units_own[along_x], units_sib[along_x])


def adam_update(weight, gradient, first_moment, second, step_rate, decay_rate):
    moment = BETA_ONE * first_moment + (1.0 - BETA_ONE) * gradient
    square = BETA_TWO * second + (1.0 - BETA_TWO) * gradient * gradient
    first_hat = moment / (1.0 - BETA_ONE**STEP)
    second_hat = square / (1.0 - BETA_TWO**STEP)
    updated = weight - step_rate * (
        first_hat / (jnp.sqrt(second_hat) + EPSILON) + decay_rate * weight
    )
    return (updated, moment, square)


def finish_kernel(
    partial, last, qkv, first_qkv, second_qkv, out, first_out, second_out, *results
):
    grad = partial[...] + last[...].astype(F32)
    for index in range(3):
        cols = slice(index * GROUP_COLS, (index + 1) * GROUP_COLS)
        found = adam_update(
            qkv[index], grad[:, cols], first_qkv[index], second_qkv[index], RATE_MATRIX, DECAY
        )
        for result, values in zip(results[:3], found, strict=True):
            result[index] = values
    found = adam_update(
        out[...], grad[:, 576:768].T, first_out[...], second_out[...], RATE_MATRIX, DECAY
    )
    for result, values in zip(results[3:], found, strict=True):
        result[...] = values


VMEM = pl.BlockSpec(memory_space=pltpu.VMEM)
SMEM = pl.BlockSpec(memory_space=pltpu.SMEM)


def shape(dims, dtype=BF16):
    return jax.ShapeDtypeStruct(dims, dtype)


def call(kernel, args, outs, scratch=(), flops=SHORT, megabytes=10, table=True):
    return pl.pallas_call(
        kernel,
        out_shape=outs,
        in_specs=[SMEM] * table + [VMEM] * (len(args) - table),
        out_specs=[VMEM] * len(outs),
        scratch_shapes=list(scratch),
        cost_estimate=pl.CostEstimate(flops=flops, bytes_accessed=1, transcendentals=0),
        compiler_params=pltpu.CompilerParams(vmem_limit_bytes=megabytes << 20),
    )(*args)


def after(value, *earlier):
    return lax.optimization_barrier((value, earlier))[0]


def fence(*earlier):
    mark = after(jnp.zeros((8, 128), F32), *earlier)
    return call(fence_kernel, (mark,), (shape((8, 128), F32),), flops=LONG, table=False)[0]


def send_across(values, mask):
    return lax.ppermute(values, AXES, [(dev, dev ^ mask) for dev in range(32)])


def add_across(values, mask):
    return values + send_across(values, mask)


class Gather:
    def __init__(self, block, orders, spread):
        self.held = block[None]
        self.orders = orders
        self.level = 0
        self.spread = spread

    def send(self, values, level):
        return lax.ppermute(values, AXES, pairs_of(self.orders, level))

    def start(self, *earlier):
        if earlier:
            self.held = after(self.held, *earlier)
        if self.level == 0 and self.spread:
            self.taken = [
                lax.ppermute(self.held, AXES, partners_of(self.orders, place))
                for place in (1, 2, 3)
            ]
            self.level = 1
        elif self.level < 3:
            self.taken = [self.send(self.held, self.level)]
            if self.level == 2:
                self.far = self.send(self.held, 3)
        else:
            self.last = self.send(self.held, 3)
        self.level += 1

    def take(self):
        if self.level < 3:
            self.held = jnp.concatenate([self.held, *self.taken], axis=0)
            return self.taken
        if self.level == 3:
            self.near = self.held
            (self.taken,) = self.taken
            self.held = self.taken
            return self.taken, self.far
        return self.last

    def finish(self, *earlier):
        while self.level < 4:
            self.taken = after(self.taken, *earlier)
            self.take()
            self.start()

    def own(self):
        return self.near, self.taken, self.far, self.last

    def sib(self, *earlier):
        own = self.near, self.taken, self.far, after(self.last, *earlier)
        return tuple(lax.ppermute(values, AXES, CORE_PAIRS) for values in own)


class Scatter:
    def __init__(self, orders):
        self.orders = orders
        self.level = 4
        self.terms = []

    def swap(self, sib):
        self.terms.append(lax.ppermute(sib, AXES, CORE_PAIRS))

    def add(self, own):
        self.terms.insert(0, own)

    def total(self, low, high):
        return sum(term[low:high].astype(F32) for term in self.terms)

    def step(self, *earlier):
        self.level -= 1
        size = 1 << self.level
        if earlier:
            self.terms[-1] = after(self.terms[-1], *earlier)
        sent = self.total(size, 2 * size).astype(BF16)
        self.terms.append(lax.ppermute(sent, AXES, pairs_of(self.orders, self.level)))
        return sent

    def spread(self, *earlier):
        if earlier:
            self.hold(*earlier)
        sent = [self.total(place, place + 1).astype(BF16) for place in (1, 2, 3)]
        for place, values in zip((1, 2, 3), sent, strict=True):
            self.terms.append(lax.ppermute(values, AXES, partners_of(self.orders, place)))
        return sent

    def hold(self, *earlier):
        self.terms[-1] = after(self.terms[-1], *earlier)

    def result(self):
        return self.total(0, 1)[0]


def gather_plain(block):
    whole = lax.all_gather(block, AXES, axis=0, tiled=False)
    whole = whole.reshape(-1, GROUPS, *block.shape).transpose(1, 0, 2, 3)
    whole = whole.reshape(2, 2, BLOCKS, BLOCK_ROWS, D).transpose(1, 0, 2, 3, 4)
    whole = whole.reshape(2, 4, 4, BLOCK_ROWS, D)
    return tuple(tuple(part[index] for index in range(4)) for part in whole)


def scatter_plain(own, sib, n_dp):
    parts = jnp.stack([own, sib]).reshape(2, BLOCKS, 2, BLOCK_ROWS, D)
    whole = parts.transpose(1, 3, 2, 0, 4).reshape(D, GROUPS, D).astype(F32)
    whole = whole.reshape(n_dp, D // n_dp, GROUPS, D).transpose(0, 2, 1, 3)
    whole = whole.reshape(n_dp * GROUPS, D // n_dp, D)
    return lax.psum_scatter(whole, AXES, scatter_dimension=0, tiled=True)[0]


def on_device(
    n_dp,
    tokens,
    patch_mask,
    cotangent,
    project_qkv,
    first_qkv,
    second_qkv,
    project_out,
    first_out,
    second_out,
    expand_weight,
    first_expand,
    second_expand,
    reduce_weight,
    first_reduce,
    second_reduce,
    vectors,
    first_vectors,
    second_vectors,
    expand_bias,
    first_bias,
    second_bias,
):
    direct = n_dp == BLOCKS
    imgs = patch_mask.shape[0]
    rows = imgs * PAD
    wide = vectors.shape[1]
    units = expand_bias.shape[0]

    def padded(values):
        values = values.reshape(imgs, SEQ, -1)
        return jnp.pad(values, ((0, 0), (0, PAD - SEQ), (0, 0))).reshape(rows, -1)

    positions = lax.broadcasted_iota(jnp.int32, patch_mask.shape, 1)
    replaced = jnp.where((patch_mask == 1) & (positions > 0), 1.0, 0.0).astype(F32)
    rep = padded(replaced)

    def pad_rows(values):
        return call(pad_kernel, (values,), (shape((rows, D)),), flops=LONG, table=False)[0]

    piece_two = expand_weight.astype(BF16)
    piece_three = reduce_weight.astype(BF16).T
    if direct:
        flat = lax.axis_index("dp") * GROUPS + lax.axis_index("tensor")
        chosen = zip(GATHER, (SCATTER[0], SCATTER[2], SCATTER[1]), strict=True)
        every = np.concatenate([build_table(g, s) for g, s in chosen], axis=1)
        table = lax.dynamic_index_in_dim(jnp.asarray(every), flat, 0, keepdims=False)
        tables = [table[0:80], table[80:160], table[160:240]]
        (piece_one,) = call(
            pack_kernel,
            (project_qkv, project_out, vectors, expand_bias),
            (shape((BLOCK_ROWS + EXTRA, D)),),
            table=False,
        )
        streams = [
            Gather(piece, orders, spread)
            for piece, orders, spread in zip(
                (piece_one, piece_two, piece_three), GATHER, SPREAD, strict=True
            )
        ]
        seen = {}
        for kind, index in zip(STEPS[0::2], STEPS[1::2], strict=True):
            stream = streams[int(index)]
            held = [stream.held for stream in streams]
            if kind == "X":
                seen["mark"] = fence(*held, *seen.values())
            elif kind == "F":
                if index == "0":
                    tok = pad_rows(after(tokens, *held[:2]))
                    seen["tok"] = (tok, rep, *tables)
                else:
                    cot = pad_rows(after(cotangent, held[1]))
                    seen["cot"] = cot
            elif kind == "S":
                stream.start(*seen.values())
            else:
                seen[index] = stream.take()
        marks = [seen[name] for name in seen if name not in "12"]
        w1_own, w1_sib = streams[0].own(), streams[0].sib(*marks)
    else:
        tables = [jnp.asarray(plain_table())] * 3
        tok, cot = pad_rows(tokens), pad_rows(cotangent)
        piece_one = jnp.concatenate(
            [project_qkv[0], project_qkv[1], project_qkv[2], project_out.T], axis=1
        ).astype(BF16)
        w1_parts, (w2_own, w2_sib), (w3_own, w3_sib) = (
            gather_plain(piece) for piece in (piece_one, piece_two, piece_three)
        )
        vector_all = lax.all_gather(vectors.astype(BF16), "dp", axis=1, tiled=True)
        bias_all = lax.all_gather(expand_bias.astype(BF16), "dp", axis=0, tiled=True)
        by_block = vector_all.reshape(11, BLOCKS, BLOCK_ROWS).transpose(1, 0, 2)
        extras = jnp.zeros((BLOCKS, EXTRA, D), BF16)
        extras = extras.at[:, :, 0:BLOCK_ROWS].set(by_block[:, 0:8])
        extras = extras.at[:, 0:3, 128 : 128 + BLOCK_ROWS].set(by_block[:, 8:11])
        extras = extras.at[:, 0, 256:640].set(bias_all.reshape(BLOCKS, FF // BLOCKS))
        w1_own, w1_sib = (
            tuple(
                jnp.concatenate([part, extras[4 * (at % 2) : 4 * (at % 2) + 4]], axis=1)
                for at, part in enumerate(parts)
            )
            for parts in w1_parts
        )

    full = (GROUPS, D, D)
    row_f32 = shape((rows, D), F32)
    row_low = shape((rows, D))
    half = shape((16, BLOCK_ROWS, D))
    two_low = shape((2, rows, D))
    two_f32 = shape((2, rows, D), F32)
    two_bias = shape((2, 1, D), F32)
    group_bias = shape((GROUPS, 1, GROUP_COLS), F32)
    weights = shape((2, D, D))
    heads = (
        shape((2, rows, 3 * GROUP_COLS)),
        shape((2 * HEADS_IN_GROUP * imgs, PAD, PAD), F32),
        shape((2, rows, GROUP_COLS)),
        row_f32,
    )
    vec, bias, start_rows, normed, qb, vb, w1_own, *heads_own, attn = call(
        functools.partial(attend_own_kernel, imgs),
        (tables[0], tok, rep, *w1_own),
        (
            shape((16, D), F32), shape((GROUPS, 1, D), F32), row_f32, row_low,
            group_bias, group_bias, weights, *heads,
        ),
        flops=LONG,
    )
    w1_sib, *heads_sib, attn, mid, normed_two = call(
        functools.partial(attend_sib_kernel, imgs),
        (tables[0], vec, start_rows, normed, qb, vb, attn, *w1_sib),
        (weights, *heads, row_f32, row_low),
        flops=SHORT,
    )
    if direct:
        streams[1].finish(normed)
        w2_own, w2_sib = streams[1].own(), streams[1].sib(normed_two)
    three, two, one = (Scatter(SCATTER[index]) for index in (2, 1, 0))
    w2_own, act_own, slope_own, grad_branch, reduce_own = call(
        expand_own_kernel,
        (tables[1], normed_two, cot, vec, bias, *w2_own),
        (weights, two_low, two_f32, row_low, half),
        flops=LONG,
    )
    if direct:
        streams[2].finish(grad_branch)
    w2_sib, act_sib, slope_sib, reduce_sib = call(
        expand_sib_kernel,
        (tables[1], normed_two, grad_branch, bias, *w2_sib),
        (weights, two_low, two_f32, half),
        flops=SHORT,
    )
    if direct:
        three.swap(reduce_sib)
        w3_own, w3_sib = streams[2].own(), streams[2].sib(reduce_sib)
    w3_sib, hid_sib, units_sib, expand_sib = call(
        functools.partial(hidden_kernel, 1),
        (tables[2], normed_two, grad_branch, slope_sib, *w3_sib),
        (weights, two_low, two_bias, half),
        flops=LONG,
    )
    if direct:
        two.swap(expand_sib)
        three.add(reduce_own)
        slope_own = after(slope_own, three.step(expand_sib))
    w3_own, hid_own, units_own, expand_own = call(
        functools.partial(hidden_kernel, 0),
        (tables[2], normed_two, grad_branch, slope_own, *w3_own),
        (weights, two_low, two_bias, half),
        flops=LONG,
    )
    if direct:
        two.add(expand_own)
        mid = after(mid, two.step())
    block_out, grad_mid, grad_attn, sums = call(
        middle_kernel,
        (
            act_sib, act_own, hid_sib, hid_own, w2_sib, w2_own, w3_sib, w3_own,
            mid, attn, cot, vec,
        ),
        (shape(tokens.shape), row_f32, row_low, shape((16, D), F32)),
        (pltpu.VMEM((rows, D), F32), pltpu.VMEM((rows, D), F32)),
        flops=SHORT,
        table=False,
    )
    held = pltpu.VMEM((rows, 3 * GROUP_COLS), BF16)
    bias_sums = (2, 2, GROUP_COLS)
    first_sib, grad_one, bias_sib = call(
        functools.partial(back_sib_kernel, imgs),
        (tables[0], w1_sib, normed, *heads_sib, grad_attn),
        (half, row_f32, shape(bias_sums, F32)),
        (held,),
        flops=SHORT,
    )
    if direct:
        one.swap(first_sib)
        grad_one = after(grad_one, three.step(grad_one))
    first_own, grad_one, bias_own = call(
        functools.partial(back_own_kernel, imgs),
        (tables[0], w1_own, normed, *heads_own, grad_attn, grad_one),
        (half, row_f32, shape(bias_sums, F32)),
        (held,),
        flops=LONG,
    )
    if direct:
        first_own, grad_one = after((first_own, grad_one), three.terms[-1])
        one.add(first_own)
        sent = one.step()
        sent_three, sent_two = three.step(sent), two.step(sent)
        grad_one = after(grad_one, sent)
    tok_grad, sums = call(
        start_kernel,
        (
            tables[0], tok, rep, vec, grad_one, bias_sib, bias_own, grad_mid, sums,
            units_sib, units_own,
        ),
        (shape(tokens.shape), shape((24, D), F32)),
    )

    if direct:
        sums = add_across(sums, 1)
        one.hold(fence(sums, sent_three, sent_two))
        part = send_across(sums, 2)
        sent = one.step()
        sums = sums + after(part, sent)
        part = send_across(sums, 16)
        three.step(sent)
        two.step(sent)
        sent = one.spread()
        sums = sums + after(part, sent)
        part = send_across(sums, 8)
        two.step(sent)
        sums = add_across(sums + after(part, sent), 4)
        grad_three = three.result()
        states_three = adam_update(
            reduce_weight, grad_three.T, first_reduce, second_reduce, RATE_MATRIX, DECAY
        )
        two.hold(sent)
        grad_two = two.result()
        partial = sum(term[0].astype(F32) for term in one.terms[:-1])
        finished = call(
            finish_kernel,
            (
                partial, one.terms[-1][0], project_qkv, first_qkv, second_qkv,
                project_out, first_out, second_out,
            ),
            (shape(project_qkv.shape, F32),) * 3 + (shape(project_out.shape, F32),) * 3,
            table=False,
        )
    else:
        grad_three = scatter_plain(reduce_own, reduce_sib, n_dp)
        grad_two = scatter_plain(expand_own, expand_sib, n_dp)
        grad_one = scatter_plain(first_own, first_sib, n_dp)
        sums = lax.psum(sums, AXES)
        grad_qkv = jnp.stack([grad_one[:, i * GROUP_COLS : (i + 1) * GROUP_COLS] for i in range(3)])
        grad_out = grad_one[:, 3 * GROUP_COLS :].T
        states_three = adam_update(
            reduce_weight, grad_three.T, first_reduce, second_reduce, RATE_MATRIX, DECAY
        )
        finished = (
            *adam_update(project_qkv, grad_qkv, first_qkv, second_qkv, RATE_MATRIX, DECAY),
            *adam_update(project_out, grad_out, first_out, second_out, RATE_MATRIX, DECAY),
        )
    spot = lax.axis_index("dp")
    vector_grad = lax.dynamic_slice_in_dim(sums[0:11], spot * wide, wide, 1)
    grad_bias = lax.dynamic_slice_in_dim(sums[16:20].reshape(-1), spot * units, units, 0)
    return (
        block_out,
        tok_grad,
        *finished,
        *adam_update(expand_weight, grad_two, first_expand, second_expand, RATE_MATRIX, DECAY),
        *states_three,
        *adam_update(vectors, vector_grad, first_vectors, second_vectors, RATE_VECTOR, 0.0),
        *adam_update(expand_bias, grad_bias, first_bias, second_bias, RATE_VECTOR, 0.0),
    )


def solution(mesh):
    rows = P(AXES, None)
    states = (
        *(P(None, "dp", "tensor"),) * 3,
        *(P("tensor", "dp"),) * 3,
        *(P("dp", "tensor"),) * 3,
        *(P("tensor", "dp"),) * 3,
        *(P(None, "dp"),) * 3,
        *(P("dp"),) * 3,
    )
    return jax.shard_map(
        functools.partial(on_device, mesh.shape["dp"]),
        mesh=mesh,
        in_specs=(rows, rows, rows, *states),
        out_specs=(rows, rows, *states),
        check_vma=False,
    )
```
